32 devices in a mesh: face: 4 (over y, core), blk: 8 (over z, x).
Axes of the slice: x: 2, y: 2, z: 4, core: 2. Of those that a mesh axis runs over, the one named last changes fastest.
Arguments:
- isotope_ratios: float32 [3, 32, 64, 1024], P(None, None, 'face', 'blk'), may hold values from 2 to 4
- advecting_velocity: float32 [2, 32, 64, 1024], P(None, None, 'face', 'blk'), may hold values from -1 to 1
- metric_scaling: float32 [64, 1024], P('face', 'blk'), may hold values from 0.5 to 2
- thermal_state: float32 [4, 32, 9216], P('face', None, 'blk'), may hold values from 255 to 300
- outgoing_site_order: int32 [4, 9216], P('face', 'blk'), may hold values from 0 to 1151, as said below
- daytime_indicator: int32 [4, 9216], P('face', 'blk'), may hold values from 0 to 1, as said below
Outputs:
- new_tracers: float32 [3, 32, 64, 1024], P(None, None, 'face', 'blk')
- phys_tracers: float32 [4, 3, 32, 9216], P('face', None, None, 'blk')
The draws below stay inside these ranges and needn't reach their ends.
Inputs may be any that keep to these rules, and one draw needn't show every extreme that they name: `outgoing_site_order`: the 1152 entries that belong to one device are a permutation of 0 .. 1151; the device's entries k of its block name the local column it sends in position k, to blk peer k // 144. `daytime_indicator`: each device sends the same number of day columns to every peer along blk, and every physics batch (the 1152 columns one device receives) holds exactly 576 day columns.
All inputs are finite; a program needn't handle non-finite values.
Results may differ from the reference program's by a relative error of at most 0.0003.
Values sent between devices are 32-bit elements; how exact they have to be, the bound alone decides.
No kernel may reach another device: no remote copies, remote signals or barrier semaphores. Data moves between devices by JAX's collectives and lax.ppermute only.
A program may use at most 64 MiB of HBM per device.

```python
import math
import jax
import jax.numpy as jnp
import numpy as np
from jax import lax

EX = 4
EY = 32
HEIGHT_LAYERS = 32
PARTS_ON_SQUARE = 4
PARTS_ALONG_SPAN = 8
NXN = 64
NYN = 1024
PROCESSOR_SITES = 1152
PEERCOLS = 144
SITES_PER_STRIP = 9216


def permute_columns(item_key):
    return jax.random.permutation(item_key, PROCESSOR_SITES).astype(jnp.int32)


def permute_block(item_key):
    return jax.random.permutation(item_key, PEERCOLS).astype(jnp.int32)


def column_plan(key):
    base = jax.random.fold_in(key, 7001)
    perm_keys = jax.random.split(jax.random.fold_in(base, 1), PARTS_ON_SQUARE * PARTS_ALONG_SPAN)
    send_perm = jax.vmap(permute_columns)(perm_keys).reshape(PARTS_ON_SQUARE, PARTS_ALONG_SPAN, PROCESSOR_SITES)
    half_count = jax.random.randint(jax.random.fold_in(base, 2), (PARTS_ON_SQUARE, PARTS_ALONG_SPAN // 2), 0, PEERCOLS + 1).astype(jnp.int32)
    day_count = jnp.concatenate([half_count, PEERCOLS - half_count], axis=1)
    rank_keys = jax.random.split(jax.random.fold_in(base, 3), PARTS_ON_SQUARE * PARTS_ALONG_SPAN * PARTS_ALONG_SPAN)
    ranks = jax.vmap(permute_block)(rank_keys).reshape(PARTS_ON_SQUARE, PARTS_ALONG_SPAN, PROCESSOR_SITES)
    send_day = (ranks < day_count[:, :, None]).astype(jnp.int32)
    inverse = jnp.argsort(send_perm, axis=-1).astype(jnp.int32)
    illuminated = jnp.take_along_axis(send_day, inverse, axis=-1)
    return (send_perm.reshape(PARTS_ON_SQUARE, PARTS_ALONG_SPAN * PROCESSOR_SITES), illuminated.reshape(PARTS_ON_SQUARE, PARTS_ALONG_SPAN * PROCESSOR_SITES))


def draw_outgoing_site_order(key, part):
    return column_plan(key)[0]


def draw_daytime_indicator(key, part):
    return column_plan(key)[1]


def steps_of(rng, extent, pieces, least, high):
    def one(dim, shards_of):
        steps = jax.random.uniform(jax.random.fold_in(jax.random.fold_in(rng, 6), dim), (shards_of,), jnp.float32, least / len(pieces), high / len(pieces))
        return jnp.repeat(jnp.exp(steps), extent[dim] // shards_of).reshape((-1,) + (1,) * (len(extent) - dim - 1))

    factor_of = one(*pieces[0])
    for cut in pieces[1:]:
        factor_of = factor_of * one(*cut)
    return factor_of


def setup_inputs(seed: int = 0) -> dict:
    seeds = jax.random.split(jax.random.key(seed), 7)
    return {
        "isotope_ratios": jnp.clip(2.0 + 2.0 * jax.random.uniform(seeds[0], (3, HEIGHT_LAYERS, NXN, NYN), jnp.float32) ** steps_of(seeds[0], (3, HEIGHT_LAYERS, NXN, NYN), ((2, 4), (3, 8)), -0.2, 0.2), 2.0, 4.0),
        "advecting_velocity": jnp.clip(jax.random.uniform(seeds[1], (2, HEIGHT_LAYERS, NXN, NYN), jnp.float32, -1.0, 1.0) * steps_of(seeds[1], (2, HEIGHT_LAYERS, NXN, NYN), ((2, 4), (3, 8)), -0.4, 0.0), -1.0, 1.0),
        "metric_scaling": jnp.clip(jnp.exp(math.log(2.0) - 1.3862944 * jax.random.uniform(seeds[2], (NXN, NYN), jnp.float32) ** steps_of(seeds[2], (NXN, NYN), ((0, 4), (1, 8)), -0.2, 0.2)), 0.5, 2.0),
        "thermal_state": jnp.clip(255.0 + 45.0 * jax.random.uniform(seeds[3], (PARTS_ON_SQUARE, HEIGHT_LAYERS, SITES_PER_STRIP), jnp.float32) ** steps_of(seeds[3], (PARTS_ON_SQUARE, HEIGHT_LAYERS, SITES_PER_STRIP), ((0, 4), (2, 8)), -0.2, 0.2), 255.0, 300.0),
        "outgoing_site_order": draw_outgoing_site_order(jax.random.fold_in(seeds[6], 71), 0),
        "daytime_indicator": draw_daytime_indicator(jax.random.fold_in(seeds[6], 71), 0),
    }


time_step = 0.006
absorb_coef = 0.02
heat_gain = 100.0
sat_base = 3.0
clausius = 0.07
ref_temp = 280.0

def gll_tables():
    inv_root = 1.0 / math.sqrt(5.0)
    gll_nodes = np.array([-1.0, -inv_root, inv_root, 1.0])
    legendre = (5.0 * gll_nodes ** 3 - 3.0 * gll_nodes) / 2.0
    deriv_matrix = np.zeros((4, 4))
    for row_index in range(4):
        for col_index in range(4):
            if row_index != col_index:
                deriv_matrix[row_index, col_index] = legendre[row_index] / (legendre[col_index] * (gll_nodes[row_index] - gll_nodes[col_index]))
    deriv_matrix[0, 0] = -3.0
    deriv_matrix[3, 3] = 3.0
    weights = np.array([1.0, 5.0, 5.0, 1.0]) / 6.0
    return (deriv_matrix, weights)

def derive_first(field, deriv):
    shaped = field.reshape(field.shape[0], field.shape[1] // 4, 4, field.shape[2])
    result = jnp.einsum('ij,lejy->leiy', deriv, shaped, precision=lax.Precision.HIGHEST)
    return result.reshape(field.shape)

def derive_second(field, deriv):
    shaped = field.reshape(field.shape[0], field.shape[1], field.shape[2] // 4, 4)
    result = jnp.einsum('ij,lxej->lxei', deriv, shaped, precision=lax.Precision.HIGHEST)
    return result.reshape(field.shape)

def add_partners(values, axis_dim):
    span_len = values.shape[axis_dim]
    bcast_shape = [1] * values.ndim
    bcast_shape[axis_dim] = span_len
    position = (jnp.arange(span_len) % 4).reshape(bcast_shape)
    following = jnp.roll(values, -1, axis_dim)
    before = jnp.roll(values, 1, axis_dim)
    return values + jnp.where(position == 3, following, 0.0) + jnp.where(position == 0, before, 0.0)

def radiative_warming(vapour):
    depth = jnp.cumsum(absorb_coef * vapour, axis=0)
    return heat_gain * absorb_coef * vapour * jnp.exp(-depth)

def condense(vapour, heavy, deuter, warmed_profiles):
    saturation = sat_base * jnp.exp(clausius * (warmed_profiles - ref_temp))
    remain = jnp.minimum(vapour, saturation)
    log_ratio = jnp.log(remain / vapour)
    inverse = 1.0 / warmed_profiles
    alpha_heavy = jnp.exp(1137.0 * inverse * inverse - 0.4156 * inverse - 0.0020667)
    alpha_deut = jnp.exp(24844.0 * inverse * inverse - 76.248 * inverse + 0.052612)
    return jnp.stack([remain, heavy * jnp.exp(alpha_heavy * log_ratio), deuter * jnp.exp(alpha_deut * log_ratio)])

def reference(isotope_ratios, advecting_velocity, metric_scaling, thermal_state, outgoing_site_order, daytime_indicator):
    deriv_np, weight_np = gll_tables()
    deriv = jnp.asarray(deriv_np, jnp.float32)
    size_x, size_y = metric_scaling.shape
    outer_weight = np.outer(np.tile(weight_np, size_x // 4), np.tile(weight_np, size_y // 4))
    node_mass = jnp.asarray(outer_weight, jnp.float32) * metric_scaling

    def tendency_of(tracer):
        flux_x = metric_scaling * advecting_velocity[0] * tracer
        flux_y = metric_scaling * advecting_velocity[1] * tracer
        return -(derive_first(flux_x, deriv) + derive_second(flux_y, deriv)) / metric_scaling
    tendency = lax.map(tendency_of, isotope_ratios)
    numer = add_partners(add_partners(node_mass * tendency, 2), 3)
    denom = add_partners(add_partners(node_mass, 0), 1)
    new_tracers = isotope_ratios + time_step * (numer / denom)
    shaped = new_tracers.reshape(3, HEIGHT_LAYERS, PARTS_ON_SQUARE, EX, 4, PARTS_ALONG_SPAN, EY, 4)[:, :, :, :, :3, :, :, :3]
    profile_list = shaped.transpose(0, 1, 2, 5, 3, 4, 6, 7).reshape(3, HEIGHT_LAYERS, PARTS_ON_SQUARE, PARTS_ALONG_SPAN, PROCESSOR_SITES)
    profile_warmth = thermal_state.reshape(PARTS_ON_SQUARE, HEIGHT_LAYERS, PARTS_ALONG_SPAN, PROCESSOR_SITES).transpose(1, 0, 2, 3)
    illuminated = daytime_indicator.reshape(PARTS_ON_SQUARE, PARTS_ALONG_SPAN, PROCESSOR_SITES)
    warmed_profiles = profile_warmth + jnp.where(illuminated[None] == 1, radiative_warming(profile_list[0]), 0.0)
    physics = condense(profile_list[0], profile_list[1], profile_list[2], warmed_profiles)
    send_perm = outgoing_site_order.reshape(PARTS_ON_SQUARE, PARTS_ALONG_SPAN, PROCESSOR_SITES)
    sent = jnp.take_along_axis(physics, jnp.broadcast_to(send_perm[None, None], physics.shape), axis=-1)
    sent = sent.reshape(3, HEIGHT_LAYERS, PARTS_ON_SQUARE, PARTS_ALONG_SPAN, PARTS_ALONG_SPAN, PEERCOLS).transpose(0, 1, 2, 4, 3, 5)
    sent = sent.reshape(3, HEIGHT_LAYERS, PARTS_ON_SQUARE, PARTS_ALONG_SPAN * PROCESSOR_SITES)
    return (new_tracers, sent.transpose(2, 0, 1, 3))
```

```python
import math

import jax
import jax.numpy as jnp
import numpy as np
from jax import lax
from jax.experimental import pallas as pl
from jax.experimental.pallas import tpu as pltpu
from jax.sharding import PartitionSpec as P

time_step = 0.006
absorb_coef = 0.02
heat_gain = 100.0
sat_base = 3.0
clausius = 0.07
ref_temp = 280.0
LANES = 128


def gll_tables():
    inv_root = 1.0 / math.sqrt(5.0)
    gll_nodes = np.array([-1.0, -inv_root, inv_root, 1.0])
    legendre = (5.0 * gll_nodes**3 - 3.0 * gll_nodes) / 2.0
    deriv_matrix = np.zeros((4, 4))
    for row_index in range(4):
        for col_index in range(4):
            if row_index != col_index:
                deriv_matrix[row_index, col_index] = legendre[row_index] / (
                    legendre[col_index] * (gll_nodes[row_index] - gll_nodes[col_index])
                )
    deriv_matrix[0, 0] = -3.0
    deriv_matrix[3, 3] = 3.0
    weights = np.array([1.0, 5.0, 5.0, 1.0]) / 6.0
    return (deriv_matrix, weights)


def row_maps(size_x):
    shared, count = [], -1
    for n in range(size_x):
        if n == 0 or n % 4 != 0:
            count += 1
        shared.append(count)
    return shared, [n for n in range(size_x) if n % 4 != 3]


def second_dim_matrix(size_y):
    deriv, weight = gll_tables()
    w = np.diag(np.tile(weight, size_y // 4))
    d = np.kron(np.eye(size_y // 4), deriv)
    e = np.eye(size_y)
    for m in range(3, size_y - 1, 4):
        e[m, m + 1] = e[m + 1, m] = 1.0
    both = np.concatenate([-(e @ w @ d).T, -(e @ w).T], axis=0)
    hi = both.astype(jnp.bfloat16)
    lo = (both - hi.astype(np.float64)).astype(jnp.bfloat16)
    return np.concatenate([hi, lo], axis=1)


def split(x):
    hi = x.astype(jnp.bfloat16)
    return hi, (x - hi.astype(jnp.float32)).astype(jnp.bfloat16)


def dot(a, b):
    return jnp.dot(a, b, preferred_element_type=jnp.float32)


def lanes_of(rows):
    return lax.broadcasted_iota(jnp.int32, (rows, LANES), 1)


def transport_kernel(iso_ref, wind_ref, metric_ref, mat_ref, sums_ref, den_ref, row_ref, col_ref, hi_ref, lo_ref):
    size_x, size_y = metric_ref.shape
    levels = wind_ref.shape[0] // (2 * size_x)
    chans = 3 * levels
    deriv, weight = gll_tables()
    shared, _ = row_maps(size_x)
    n_rows = shared[-1] + 1

    def put(row, a, b):
        at = pl.ds(row * chans, chans)
        ahi, alo = split(a)
        bhi, blo = split(b)
        hi_ref[at, 0:size_y] = ahi
        hi_ref[at, size_y : 2 * size_y] = bhi
        lo_ref[at, 0:size_y] = alo
        lo_ref[at, size_y : 2 * size_y] = blo

    held = None
    for e in range(size_x // 4):
        fx, fy = [], []
        for j in range(4):
            n = 4 * e + j
            jac = metric_ref[n : n + 1, :]
            q = iso_ref[pl.ds(n, chans, stride=size_x), :]
            ju = jac * wind_ref[pl.ds(n, levels, stride=size_x), :]
            jv = (jac * float(weight[j])) * wind_ref[pl.ds(levels * size_x + n, levels, stride=size_x), :]
            fx.append(jnp.concatenate([ju, ju, ju], axis=0) * q)
            fy.append(jnp.concatenate([jv, jv, jv], axis=0) * q)
        for i in range(4):
            b = None
            for j in range(4):
                coef = float(weight[i] * deriv[i, j])
                if coef != 0.0:
                    b = coef * fx[j] if b is None else b + coef * fx[j]
            a = fy[i]
            n = 4 * e + i
            if i == 0 and held is not None:
                a, b = a + held[0], b + held[1]
            if i == 3 and n != size_x - 1:
                held = (a, b)
            else:
                put(shared[n], a, b)
    hi = hi_ref[...]
    first = dot(hi, mat_ref[...])
    total = first[:, 0:size_y] + (first[:, size_y:] + dot(lo_ref[...], mat_ref[:, 0:size_y]))
    sums_ref[...] = total

    lane = lanes_of(size_x)
    sub = lax.broadcasted_iota(jnp.int32, (size_x, LANES), 0)
    wl = jnp.where((lane % 4 == 0) | (lane % 4 == 3), float(weight[0]), float(weight[1]))
    ws = jnp.where((sub % 4 == 0) | (sub % 4 == 3), float(weight[0]), float(weight[1]))
    mass = (wl * ws) * metric_ref[...]
    after, before = pltpu.roll(mass, size_x - 1, 0), pltpu.roll(mass, 1, 0)
    mass = mass + jnp.where((sub % 4 == 3) & (sub != size_x - 1), after, 0.0) + jnp.where((sub % 4 == 0) & (sub != 0), before, 0.0)
    after, before = pltpu.roll(mass, size_y - 1, 1), pltpu.roll(mass, 1, 1)
    mass = mass + jnp.where((lane % 4 == 3) & (lane != size_y - 1), after, 0.0) + jnp.where((lane % 4 == 0) & (lane != 0), before, 0.0)
    den_ref[...] = mass

    row_ref[0:chans, :] = sums_ref[pl.ds((n_rows - 1) * chans, chans), :]
    row_ref[chans : chans + 8, :] = jnp.broadcast_to(mass[size_x - 1 : size_x, :], (8, LANES))
    wide = lanes_of(chans)
    col = jnp.zeros((chans, LANES), jnp.float32)
    for r in range(n_rows):
        moved = pltpu.roll(sums_ref[pl.ds(r * chans, chans), :], r + 1, 1)
        col = jnp.where(wide == r, moved, col)
    col_ref[0:chans, :] = col
    dcol = jnp.zeros((1, LANES), jnp.float32)
    for n in range(size_x):
        r = shared[n]
        dcol = jnp.where(lanes_of(1) == r, pltpu.roll(mass, r + 1, 1)[n : n + 1, :], dcol)
    col_ref[chans : chans + 8, :] = jnp.broadcast_to(dcol, (8, LANES))


def cumulative(x):
    rows = x.shape[0]
    sub = lax.broadcasted_iota(jnp.int32, x.shape, 0)
    step = 1
    while step < rows:
        x = x + jnp.where(sub >= step, pltpu.roll(x, step, 0), 0.0)
        step *= 2
    return x


def physics(tracers, temps, day):
    levels = temps.shape[0]
    vapour = tracers[0:levels]
    scaled = absorb_coef * vapour
    heating = heat_gain * scaled * jnp.exp(-cumulative(scaled))
    heated = temps + jnp.where(day == 1.0, heating, 0.0)
    saturation = sat_base * jnp.exp(clausius * (heated - ref_temp))
    remain = jnp.minimum(vapour, saturation)
    log_ratio = jnp.log(remain / vapour)
    inverse = 1.0 / heated
    alpha_heavy = jnp.exp(1137.0 * inverse * inverse - 0.4156 * inverse - 0.0020667)
    alpha_deut = jnp.exp(24844.0 * inverse * inverse - 76.248 * inverse + 0.052612)
    return jnp.concatenate(
        [
            remain,
            tracers[levels : 2 * levels] * jnp.exp(alpha_heavy * log_ratio),
            tracers[2 * levels :] * jnp.exp(alpha_deut * log_ratio),
        ],
        axis=0,
    )


def third(x):
    return lax.shift_right_logical(x * 43691, 17)


def spread_lanes(x):
    rows = x.shape[0]
    lane = lanes_of(rows)
    source = 3 * lax.shift_right_logical(lane, 2) + jnp.minimum(lane & 3, 2)
    padded = jnp.concatenate([x, jnp.zeros((rows, LANES - x.shape[1]), x.dtype)], axis=1)
    return jnp.take_along_axis(padded, source, axis=1)


def before_kernel(n_peers, iso_ref, sums_ref, den_ref, temps_ref, day_ref, order_ref, acc_ref, pick_ref, htemps_ref, hiso_ref, hsum_ref, lhs_ref, hot_ref):
    size_x, size_y = den_ref.shape
    levels, sites = temps_ref.shape
    chans = 3 * levels
    shared, node_rows = row_maps(size_x)
    per_row = sites // len(node_rows)
    per_peer = sites // n_peers
    full, rest = per_peer // LANES, per_peer % LANES
    k_total = (len(node_rows) - 1) * LANES

    order = order_ref[...]
    pieces = [order[:, p * per_peer + LANES * j : p * per_peer + LANES * (j + 1)] for p in range(n_peers) for j in range(full)]
    if rest:
        pieces += [order[:, p * per_peer + LANES * full : (p + 1) * per_peer] for p in range(n_peers)]
    order = jnp.concatenate(pieces, axis=1)
    row = third(lax.shift_right_logical(order, 5))
    within = order - per_row * row
    group = third(within)
    node = 4 * group + (within - 3 * group)
    main = jnp.where((row == 0) | (node == 0), -1, (row - 1) * LANES + node)
    first = jnp.where(row == 0, node, -1)
    side = jnp.where((row != 0) & (node == 0), row, -1)
    sub = lax.broadcasted_iota(jnp.int32, (LANES, LANES), 0)

    def one_hot(index):
        return jnp.where(sub == index, 1.0, 0.0).astype(jnp.bfloat16)

    for t in range(sites // LANES):
        at = slice(t * LANES, (t + 1) * LANES)
        here = main[:, at]
        for k in range(len(node_rows) - 1):
            hot_ref[k * LANES : (k + 1) * LANES, at] = one_hot(here - k * LANES)
        pick_ref[0:LANES, at] = one_hot(first[:, at])
        pick_ref[LANES : 2 * LANES, at] = one_hot(side[:, at])

    temps = temps_ref[...]
    day = day_ref[...].astype(jnp.float32)
    lane1 = lanes_of(1)
    unused = (lane1 & 3) == 3
    own = unused | (lane1 == 0)
    wide, wide_l = lanes_of(chans), lanes_of(levels)
    hiso = jnp.full((chans, LANES), 3.0, jnp.float32)
    hsum = jnp.zeros((chans, LANES), jnp.float32)
    htemp = jnp.full((levels, LANES), ref_temp, jnp.float32)
    hday = jnp.zeros((1, LANES), jnp.float32)
    inv = 1.0 / den_ref[...]
    for k, n in enumerate(node_rows):
        iso = iso_ref[pl.ds(n, chans, stride=size_x), :]
        here = sums_ref[pl.ds(k * chans, chans), :]
        t_here = temps[:, k * per_row : (k + 1) * per_row]
        t_here = jnp.where(unused, ref_temp, spread_lanes(t_here))
        d_here = spread_lanes(jnp.broadcast_to(day[:, k * per_row : (k + 1) * per_row], (8, per_row)))[0:1, :]
        if k == 0:
            htemps_ref[0:levels, :] = t_here
            htemps_ref[2 * levels : 2 * levels + 8, :] = jnp.broadcast_to(d_here, (8, LANES))
            continue
        shift = k
        hiso = jnp.where(wide == k, pltpu.roll(iso, shift, 1), hiso)
        hsum = jnp.where(wide == k, pltpu.roll(here, shift, 1), hsum)
        htemp = jnp.where(wide_l == k, pltpu.roll(t_here, shift, 1), htemp)
        hday = jnp.where(lane1 == k, pltpu.roll(jnp.broadcast_to(d_here, (8, LANES)), shift, 1)[0:1, :], hday)
        gain = jnp.where(own, 0.0, time_step * inv[n : n + 1, :])
        hi, lo = split(physics(iso + gain * here, t_here, d_here))
        lhs_ref[0:chans, (k - 1) * LANES : k * LANES] = hi
        lhs_ref[chans : 2 * chans, (k - 1) * LANES : k * LANES] = lo
    last = len(node_rows)
    hsum = jnp.where(wide == last, pltpu.roll(sums_ref[pl.ds(last * chans, chans), :], last, 1), hsum)
    htemps_ref[levels : 2 * levels, :] = htemp
    htemps_ref[2 * levels + 8 : 2 * levels + 16, :] = jnp.broadcast_to(hday, (8, LANES))
    hiso_ref[...] = hiso
    hsum_ref[0:chans, :] = hsum
    dcol = jnp.ones((1, LANES), jnp.float32)
    for n in range(size_x):
        r = shared[n]
        dcol = jnp.where(lane1 == r, pltpu.roll(den_ref[...], r, 1)[n : n + 1, :] if r else den_ref[n : n + 1, :], dcol)
    hsum_ref[chans : chans + 8, :] = jnp.broadcast_to(dcol, (8, LANES))
    both = dot(lhs_ref[...], hot_ref[...])
    acc_ref[...] = both[0:chans] + both[chans:]


def after_kernel(n_peers, iso_ref, sums_ref, den_ref, acc_ref, pick_ref, htemps_ref, hiso_ref, hsum_ref, row_ref, col_ref, corner_ref, send_ref, rows_ref, cols_ref):
    size_x = den_ref.shape[0]
    chans, sites = acc_ref.shape
    levels = chans // 3
    shared, node_rows = row_maps(size_x)
    n_rows = shared[-1] + 1
    per_peer = sites // n_peers
    full, rest = per_peer // LANES, per_peer % LANES
    wide, lane1 = lanes_of(chans), lanes_of(1)

    corner = pltpu.roll(corner_ref[...], LANES - (n_rows - 1), 1)
    extra = col_ref[...] + corner
    total = sums_ref[0:chans, :] + row_ref[0:chans, :] + jnp.where(wide == 0, extra[0:chans], 0.0)
    den = den_ref[0:1, :] + row_ref[chans : chans + 1, :] + jnp.where(lane1 == 0, extra[chans : chans + 1], 0.0)
    ratio = total / den
    rows_ref[...] = ratio
    iso = iso_ref[pl.ds(0, chans, stride=size_x), :]
    unused = (lane1 & 3) == 3
    new_row = iso + jnp.where(unused, 0.0, time_step * ratio)
    phys_row = physics(new_row, htemps_ref[0:levels, :], htemps_ref[2 * levels : 2 * levels + 1, :])

    live = lane1 < n_rows
    dcol = hsum_ref[chans : chans + 1, :] + jnp.where(live, col_ref[chans : chans + 1, :], 0.0)
    ratio_c = (hsum_ref[0:chans, :] + jnp.where(live, col_ref[0:chans, :], 0.0)) / dcol
    cols_ref[...] = jnp.where(wide == 0, ratio, ratio_c)
    in_use = (lane1 > 0) & (lane1 < len(node_rows))
    new_col = hiso_ref[...] + jnp.where(in_use, time_step * ratio_c, 0.0)
    phys_col = physics(new_col, htemps_ref[levels : 2 * levels, :], htemps_ref[2 * levels + 8 : 2 * levels + 9, :])

    rhi, rlo = split(phys_row)
    chi, clo = split(phys_col)
    lhs = jnp.concatenate([jnp.concatenate([rhi, chi], axis=1), jnp.concatenate([rlo, clo], axis=1)], axis=0)
    both = dot(lhs, pick_ref[...])
    out = acc_ref[...] + (both[0:chans] + both[chans:])
    for p in range(n_peers):
        for j in range(full):
            t = p * full + j
            send_ref[p, j * chans : (j + 1) * chans, :] = out[:, t * LANES : (t + 1) * LANES]
    if rest:
        begin = n_peers * full * LANES
        for t in range(n_peers * rest // LANES):
            block = out[:, begin + t * LANES : begin + (t + 1) * LANES]
            block = jnp.concatenate([block, jnp.zeros((LANES - chans, LANES), jnp.float32)], axis=0).T
            at = t * LANES
            while at < (t + 1) * LANES:
                p, i = at // rest, at % rest
                count = min(rest - i, (t + 1) * LANES - at)
                send_ref[p, full * chans + i : full * chans + i + count, :] = block[at - t * LANES : at - t * LANES + count, :]
                at += count


def advance_kernel(iso_ref, sums_ref, den_ref, rows_ref, cols_ref, back_row_ref, back_col_ref, new_ref):
    size_x = den_ref.shape[0]
    chans = rows_ref.shape[0]
    shared, _ = row_maps(size_x)
    wide = lanes_of(chans)
    inv = 1.0 / den_ref[...]
    for n in range(size_x):
        r = shared[n]
        if n == 0:
            ratio = rows_ref[...]
        elif n == size_x - 1:
            ratio = back_row_ref[...]
        else:
            ratio = sums_ref[pl.ds(r * chans, chans), :] * inv[n : n + 1, :]
            ratio = jnp.where(wide == 0, cols_ref[:, r : r + 1], ratio)
        if n != size_x - 1:
            ratio = jnp.where(wide == LANES - 1, back_col_ref[:, r : r + 1], ratio)
        new_ref[pl.ds(n, chans, stride=size_x), :] = iso_ref[pl.ds(n, chans, stride=size_x), :] + time_step * ratio


def gather_kernel(got_ref, out_ref):
    n_peers, rows, _ = got_ref.shape
    chans, sites = out_ref.shape
    per_peer = sites // n_peers
    full, rest = per_peer // LANES, per_peer % LANES
    lane = lanes_of(chans)
    blocks = [None] * (sites // LANES)

    def place(block, value, low, high):
        old = blocks[block]
        blocks[block] = value if old is None else jnp.where((lane >= low) & (lane < high), value, old)

    for p in range(n_peers):
        for j in range(full):
            begin = p * per_peer + j * LANES
            shift = begin % LANES
            value = got_ref[p, j * chans : (j + 1) * chans, :]
            if shift:
                value = pltpu.roll(value, shift, 1)
            place(begin // LANES, value, shift, LANES)
            if shift:
                place(begin // LANES + 1, value, 0, shift)
    if rest:
        tails = [got_ref[p, full * chans : full * chans + rest, :] for p in range(n_peers)]
        tails = jnp.concatenate(tails, axis=0)
        for t in range(n_peers * rest // LANES):
            block = tails[t * LANES : (t + 1) * LANES, :].T[0:chans, :]
            at = t * LANES
            while at < (t + 1) * LANES:
                p, i = at // rest, at % rest
                count = min(rest - i, (t + 1) * LANES - at)
                column = p * per_peer + full * LANES + i
                place(column // LANES, block, column % LANES, column % LANES + count)
                at += count
    for t, block in enumerate(blocks):
        out_ref[:, t * LANES : (t + 1) * LANES] = block


def call(kernel, outs, scratch, name, *args):
    return pl.pallas_call(
        kernel,
        out_shape=outs,
        scratch_shapes=scratch,
        name=name,
        compiler_params=pltpu.CompilerParams(vmem_limit_bytes=40 * 1024 * 1024),
    )(*args)


def on_device(
    isotope_ratios,
    advecting_velocity,
    metric_scaling,
    thermal_state,
    outgoing_site_order,
    daytime_indicator,
):
    size_x, size_y = metric_scaling.shape
    levels = isotope_ratios.shape[1]
    chans = 3 * levels
    sites = outgoing_site_order.shape[1]
    n_face, n_blk = lax.axis_size("face"), lax.axis_size("blk")
    shared, node_rows = row_maps(size_x)
    n_rows = shared[-1] + 1
    per_peer = sites // n_blk
    send_rows = chans * (per_peer // LANES) + per_peer % LANES

    def f32(*shape):
        return jax.ShapeDtypeStruct(shape, jnp.float32)

    iso = isotope_ratios.reshape(chans * size_x, size_y)
    wind = advecting_velocity.reshape(2 * levels * size_x, size_y)
    matrix = jnp.asarray(second_dim_matrix(size_y))
    sums, den, row, col = call(
        transport_kernel,
        (f32(n_rows * chans, size_y), f32(size_x, size_y), f32(chans + 8, LANES), f32(chans + 8, LANES)),
        [pltpu.VMEM((n_rows * chans, 2 * size_y), jnp.bfloat16)] * 2,
        "transport",
        iso,
        wind,
        metric_scaling,
        matrix,
    )
    face_up = [(i, (i + 1) % n_face) for i in range(n_face)]
    blk_up = [(i, (i + 1) % n_blk) for i in range(n_blk)]
    diagonal = [(i * n_blk + j, (i + 1) % n_face * n_blk + (j + 1) % n_blk) for i in range(n_face) for j in range(n_blk)]
    got_row = lax.ppermute(row, "face", face_up)
    got_col = lax.ppermute(col, "blk", blk_up)
    got_corner = lax.ppermute(col, ("face", "blk"), diagonal)

    bf16 = jnp.bfloat16
    acc, pick, htemps, hiso, hsum = call(
        lambda *refs: before_kernel(n_blk, *refs),
        (
            f32(chans, sites),
            jax.ShapeDtypeStruct((2 * LANES, sites), bf16),
            f32(2 * levels + 16, LANES),
            f32(chans, LANES),
            f32(chans + 8, LANES),
        ),
        [pltpu.VMEM((2 * chans, (len(node_rows) - 1) * LANES), bf16), pltpu.VMEM(((len(node_rows) - 1) * LANES, sites), bf16)],
        "inner_columns",
        iso,
        sums,
        den,
        thermal_state[0],
        daytime_indicator,
        outgoing_site_order,
    )
    send, rows, cols = call(
        lambda *refs: after_kernel(n_blk, *refs),
        (f32(n_blk, send_rows, LANES), f32(chans, LANES), f32(chans, LANES)),
        [],
        "edge_columns",
        iso,
        sums,
        den,
        acc,
        pick,
        htemps,
        hiso,
        hsum,
        got_row,
        got_col,
        got_corner,
    )
    got = lax.all_to_all(send, "blk", split_axis=0, concat_axis=0, tiled=True)
    back_col = lax.ppermute(cols, "blk", [(j, i) for i, j in blk_up])
    ends = jnp.where(jnp.arange(LANES)[None, :] == LANES - 1, back_col[:, 0:1], rows)
    back_row = lax.ppermute(ends, "face", [(j, i) for i, j in face_up])
    new = call(advance_kernel, f32(chans * size_x, size_y), [], "advance", iso, sums, den, rows, cols, back_row, back_col)
    phys = call(gather_kernel, f32(chans, sites), [], "assemble", got)
    return (new.reshape(isotope_ratios.shape), phys.reshape(1, 3, levels, sites))


def solution(mesh):
    placed = (
        P(None, None, "face", "blk"),
        P(None, None, "face", "blk"),
        P("face", "blk"),
        P("face", None, "blk"),
        P("face", "blk"),
        P("face", "blk"),
    )
    return jax.shard_map(
        on_device,
        mesh=mesh,
        in_specs=placed,
        out_specs=(P(None, None, "face", "blk"), P("face", None, None, "blk")),
        check_vma=False,
    )
```

```python
import math

import jax
import jax.numpy as jnp
import numpy as np
from jax import lax
from jax.experimental import pallas as pl
from jax.experimental.pallas import tpu as pltpu
from jax.sharding import PartitionSpec as P

time_step = 0.006
absorb_coef = 0.02
heat_gain = 100.0
sat_base = 3.0
clausius = 0.07
ref_temp = 280.0
LANES = 128


def gll_tables():
    inv_root = 1.0 / math.sqrt(5.0)
    gll_nodes = np.array([-1.0, -inv_root, inv_root, 1.0])
    legendre = (5.0 * gll_nodes**3 - 3.0 * gll_nodes) / 2.0
    deriv_matrix = np.zeros((4, 4))
    for row_index in range(4):
        for col_index in range(4):
            if row_index != col_index:
                deriv_matrix[row_index, col_index] = legendre[row_index] / (
                    legendre[col_index] * (gll_nodes[row_index] - gll_nodes[col_index])
                )
    deriv_matrix[0, 0] = -3.0
    deriv_matrix[3, 3] = 3.0
    weights = np.array([1.0, 5.0, 5.0, 1.0]) / 6.0
    return (deriv_matrix, weights)


def row_maps(size_x):
    shared, count = [], -1
    for n in range(size_x):
        if n == 0 or n % 4 != 0:
            count += 1
        shared.append(count)
    return shared, [n for n in range(size_x) if n % 4 != 3]


def second_dim_matrix(size_y):
    deriv, weight = gll_tables()
    w = np.diag(np.tile(weight, size_y // 4))
    d = np.kron(np.eye(size_y // 4), deriv)
    e = np.eye(size_y)
    for m in range(3, size_y - 1, 4):
        e[m, m + 1] = e[m + 1, m] = 1.0
    both = np.concatenate([-(e @ w @ d).T, -(e @ w).T], axis=0)
    hi = both.astype(jnp.bfloat16)
    lo = (both - hi.astype(np.float64)).astype(jnp.bfloat16)
    return np.concatenate([hi, lo], axis=1)


def split(x):
    hi = x.astype(jnp.bfloat16)
    return hi, (x - hi.astype(jnp.float32)).astype(jnp.bfloat16)


def dot(a, b):
    return jnp.dot(a, b, preferred_element_type=jnp.float32)


def lanes_of(rows):
    return lax.broadcasted_iota(jnp.int32, (rows, LANES), 1)


def put_split(hi_ref, lo_ref, at, a, b):
    size_y = a.shape[1]
    ahi, alo = split(a)
    bhi, blo = split(b)
    hi_ref[at, 0:size_y] = ahi
    hi_ref[at, size_y : 2 * size_y] = bhi
    lo_ref[at, 0:size_y] = alo
    lo_ref[at, size_y : 2 * size_y] = blo


def second_dim(hi, lo, mat):
    size_y = hi.shape[1] // 2
    first = dot(hi, mat)
    return first[:, 0:size_y] + (first[:, size_y:] + dot(lo, mat[:, 0:size_y]))


def fluxes(iso_ref, wind_ref, metric_ref, s, n, weight):
    size_x = metric_ref.shape[0]
    part = wind_ref.shape[0] // 2
    levels = part // size_x
    jac = metric_ref[n : n + 1, :]
    q = iso_ref[pl.ds(s * part + n, levels, stride=size_x), :]
    fx = (jac * wind_ref[pl.ds(n, levels, stride=size_x), :]) * q
    if weight is None:
        return fx
    return fx, ((jac * weight) * wind_ref[pl.ds(part + n, levels, stride=size_x), :]) * q


def weighted_derivative(coefs, fx):
    total = None
    for coef, f in zip(coefs, fx):
        if coef != 0.0:
            total = float(coef) * f if total is None else total + float(coef) * f
    return total


def edge_rows_kernel(
    iso_hbm,
    wind_hbm,
    metric_hbm,
    mat_hbm,
    temps_hbm,
    day_hbm,
    order_hbm,
    iso_ref,
    wind_ref,
    metric_ref,
    mat_ref,
    temps_ref,
    day_ref,
    order_ref,
    den_ref,
    low_ref,
    high_ref,
    hi_ref,
    lo_ref,
    sems,
):
    size_x, size_y = metric_ref.shape
    part = wind_ref.shape[0] // 2
    levels = part // size_x
    chans = 3 * levels
    deriv, weight = gll_tables()
    copies = [pltpu.make_async_copy(metric_hbm, metric_ref, sems.at[0])]
    for k in range(2):
        copies.append(pltpu.make_async_copy(wind_hbm.at[pl.ds(k * part, part)], wind_ref.at[pl.ds(k * part, part)], sems.at[1 + k]))
    for s in range(3):
        copies.append(pltpu.make_async_copy(iso_hbm.at[pl.ds(s * part, part)], iso_ref.at[pl.ds(s * part, part)], sems.at[3 + s]))
    copies.append(pltpu.make_async_copy(mat_hbm, mat_ref, sems.at[6]))
    for k, (src, dst) in enumerate(((temps_hbm, temps_ref), (day_hbm, day_ref), (order_hbm, order_ref))):
        copies.append(pltpu.make_async_copy(src, dst, sems.at[7 + k]))
    for c in copies:
        c.start()

    copies[0].wait()
    lane = lanes_of(size_x)
    sub = lax.broadcasted_iota(jnp.int32, (size_x, LANES), 0)
    wl = jnp.where((lane % 4 == 0) | (lane % 4 == 3), float(weight[0]), float(weight[1]))
    ws = jnp.where((sub % 4 == 0) | (sub % 4 == 3), float(weight[0]), float(weight[1]))
    mass = (wl * ws) * metric_ref[...]
    after, before = pltpu.roll(mass, size_x - 1, 0), pltpu.roll(mass, 1, 0)
    mass = mass + jnp.where((sub % 4 == 3) & (sub != size_x - 1), after, 0.0) + jnp.where((sub % 4 == 0) & (sub != 0), before, 0.0)
    after, before = pltpu.roll(mass, size_y - 1, 1), pltpu.roll(mass, 1, 1)
    mass = mass + jnp.where((lane % 4 == 3) & (lane != size_y - 1), after, 0.0) + jnp.where((lane % 4 == 0) & (lane != 0), before, 0.0)
    den_ref[...] = mass

    for c in copies[1:3]:
        c.wait()
    for s in range(3):
        copies[3 + s].wait()
        for k, (first, i) in enumerate(((0, 0), (size_x - 4, 3))):
            fx = []
            for j in range(4):
                if j == i:
                    f, fy = fluxes(iso_ref, wind_ref, metric_ref, s, first + j, float(weight[i]))
                else:
                    f = fluxes(iso_ref, wind_ref, metric_ref, s, first + j, None)
                fx.append(f)
            put_split(hi_ref, lo_ref, pl.ds(k * chans + s * levels, levels), fy, weighted_derivative(weight[i] * deriv[i], fx))
    copies[6].wait()
    total = second_dim(hi_ref[...], lo_ref[...], mat_ref[...])
    for ref, k, n in ((low_ref, 0, 0), (high_ref, 1, size_x - 1)):
        ref[0:chans, :] = total[k * chans : (k + 1) * chans, :]
        ref[chans : chans + 8, :] = jnp.broadcast_to(mass[n : n + 1, :], (8, LANES))
    for c in copies[7:]:
        c.wait()


def transport_kernel(iso_ref, wind_ref, metric_ref, mat_ref, den_ref, low_ref, high_ref, sums_ref, left_ref, right_ref, hi_ref, lo_ref):
    size_x, size_y = metric_ref.shape
    levels = wind_ref.shape[0] // (2 * size_x)
    chans = 3 * levels
    deriv, weight = gll_tables()
    shared, _ = row_maps(size_x)
    n_rows = shared[-1] + 1
    for s in range(3):
        held = None
        for e in range(size_x // 4):
            fx, fy = [], []
            for j in range(4):
                f, g = fluxes(iso_ref, wind_ref, metric_ref, s, 4 * e + j, float(weight[j]))
                fx.append(f)
                fy.append(g)
            for i in range(4):
                n = 4 * e + i
                if n == 0 or n == size_x - 1:
                    continue
                a, b = fy[i], weighted_derivative(weight[i] * deriv[i], fx)
                if i == 0:
                    a, b = a + held[0], b + held[1]
                if i == 3:
                    held = (a, b)
                else:
                    put_split(hi_ref, lo_ref, pl.ds((shared[n] - 1) * chans + s * levels, levels), a, b)
    last = (n_rows - 1) * chans
    sums_ref[0:chans, :] = low_ref[0:chans, :]
    sums_ref[chans:last, :] = second_dim(hi_ref[...], lo_ref[...], mat_ref[...])
    sums_ref[last : last + chans, :] = high_ref[0:chans, :]

    mass = den_ref[...]
    wide, lane1 = lanes_of(chans), lanes_of(1)
    first_col = jnp.zeros((chans, LANES), jnp.float32)
    last_col = first_col
    first_den = jnp.zeros((1, LANES), jnp.float32)
    last_den = first_den
    for r in range(n_rows):
        here = sums_ref[pl.ds(r * chans, chans), :]
        n = shared.index(r)
        if r:
            first_col = jnp.where(wide == r, pltpu.roll(here, r, 1), first_col)
            first_den = jnp.where(lane1 == r, pltpu.roll(mass, r, 1)[n : n + 1, :], first_den)
        else:
            first_col = jnp.where(wide == 0, here, first_col)
            first_den = jnp.where(lane1 == 0, mass[0:1, :], first_den)
        last_col = jnp.where(wide == r, pltpu.roll(here, r + 1, 1), last_col)
        last_den = jnp.where(lane1 == r, pltpu.roll(mass, r + 1, 1)[n : n + 1, :], last_den)
    left_ref[0:chans, :] = first_col
    left_ref[chans : chans + 8, :] = jnp.broadcast_to(first_den, (8, LANES))
    right_ref[0:chans, :] = last_col
    right_ref[chans : chans + 8, :] = jnp.broadcast_to(last_den, (8, LANES))


def corners_kernel(n_rows, filler_ref, left_ref, right_ref, from_low_ref, from_high_ref, new_left_ref, new_right_ref):
    del filler_ref
    low, high = from_low_ref[...], from_high_ref[...]
    lane = lanes_of(low.shape[0])
    last = n_rows - 1
    new_left_ref[...] = left_ref[...] + jnp.where(lane == 0, low, 0.0) + jnp.where(lane == last, pltpu.roll(high, last, 1), 0.0)
    new_right_ref[...] = (
        right_ref[...] + jnp.where(lane == 0, pltpu.roll(low, 1, 1), 0.0) + jnp.where(lane == last, pltpu.roll(high, last + 1, 1), 0.0)
    )


def cumulative(x):
    rows = x.shape[0]
    sub = lax.broadcasted_iota(jnp.int32, x.shape, 0)
    step = 1
    while step < rows:
        x = x + jnp.where(sub >= step, pltpu.roll(x, step, 0), 0.0)
        step *= 2
    return x


def physics(tracers, temps, day):
    levels = temps.shape[0]
    vapour = tracers[0:levels]
    scaled = absorb_coef * vapour
    heating = heat_gain * scaled * jnp.exp(-cumulative(scaled))
    heated = temps + jnp.where(day == 1.0, heating, 0.0)
    saturation = sat_base * jnp.exp(clausius * (heated - ref_temp))
    remain = jnp.minimum(vapour, saturation)
    log_ratio = jnp.log(remain / vapour)
    inverse = 1.0 / heated
    alpha_heavy = jnp.exp(1137.0 * inverse * inverse - 0.4156 * inverse - 0.0020667)
    alpha_deut = jnp.exp(24844.0 * inverse * inverse - 76.248 * inverse + 0.052612)
    return jnp.concatenate(
        [
            remain,
            tracers[levels : 2 * levels] * jnp.exp(alpha_heavy * log_ratio),
            tracers[2 * levels :] * jnp.exp(alpha_deut * log_ratio),
        ],
        axis=0,
    )


def peer_of(slot, paired):
    return lax.axis_index("blk") ^ slot if paired else slot


def third(x):
    return lax.shift_right_logical(x * 43691, 17)


def spread_lanes(x):
    rows = x.shape[0]
    lane = lanes_of(rows)
    source = 3 * lax.shift_right_logical(lane, 2) + jnp.minimum(lane & 3, 2)
    padded = jnp.concatenate([x, jnp.zeros((rows, LANES - x.shape[1]), x.dtype)], axis=1)
    return jnp.take_along_axis(padded, source, axis=1)


def send_order_kernel(n_peers, paired, temps_ref, day_ref, order_ref, hot_ref, pick_ref, ntemps_ref, nday_ref, slots_ref):
    levels, sites = temps_ref.shape
    count = ntemps_ref.shape[0] // levels - 1
    per_row = sites // count
    per_peer = sites // n_peers
    full, rest = per_peer // LANES, per_peer % LANES

    order = order_ref[...]
    for p in range(n_peers):
        mine = order[:, p * per_peer : (p + 1) * per_peer]
        pad = slots_ref.shape[1] - per_peer
        slots_ref[p : p + 1, :] = jnp.concatenate([mine, jnp.zeros((1, pad), jnp.int32)], axis=1) if pad else mine
    peers = [slots_ref[pl.ds(peer_of(k, paired), 1), :] for k in range(n_peers)]
    pieces = [mine[:, LANES * j : LANES * (j + 1)] for mine in peers for j in range(full)]
    if rest:
        pieces += [mine[:, LANES * full : per_peer] for mine in peers]
    order = jnp.concatenate(pieces, axis=1)
    row = third(lax.shift_right_logical(order, 5))
    within = order - per_row * row
    group = third(within)
    node = 4 * group + (within - 3 * group)
    main = jnp.where((row == 0) | (node == 0), -1, (row - 1) * LANES + node)
    first = jnp.where(row == 0, node, -1)
    side = jnp.where((row != 0) & (node == 0), row, -1)
    sub = lax.broadcasted_iota(jnp.int32, (LANES, LANES), 0)

    def one_hot(index):
        return jnp.where(sub == index, 1.0, 0.0).astype(jnp.bfloat16)

    for t in range(sites // LANES):
        at = slice(t * LANES, (t + 1) * LANES)
        here = main[:, at]
        for k in range(count - 1):
            hot_ref[k * LANES : (k + 1) * LANES, at] = one_hot(here - k * LANES)
        pick_ref[0:LANES, at] = one_hot(first[:, at])
        pick_ref[LANES : 2 * LANES, at] = one_hot(side[:, at])

    temps = temps_ref[...]
    day = jnp.broadcast_to(day_ref[...].astype(jnp.float32), (8, sites))
    lane1, wide_l = lanes_of(1), lanes_of(levels)
    unused = (lane1 & 3) == 3
    side_temps = jnp.full((levels, LANES), ref_temp, jnp.float32)
    side_day = jnp.zeros((8, LANES), jnp.float32)
    for k in range(count):
        t_here = jnp.where(unused, ref_temp, spread_lanes(temps[:, k * per_row : (k + 1) * per_row]))
        d_here = spread_lanes(day[:, k * per_row : (k + 1) * per_row])
        ntemps_ref[k * levels : (k + 1) * levels, :] = t_here
        nday_ref[8 * k : 8 * k + 8, :] = d_here
        if k:
            side_temps = jnp.where(wide_l == k, pltpu.roll(t_here, k, 1), side_temps)
            side_day = jnp.where(lanes_of(8) == k, pltpu.roll(d_here, k, 1), side_day)
    ntemps_ref[count * levels :, :] = side_temps
    nday_ref[8 * count :, :] = side_day


def inner_columns_kernel(after_ref, iso_ref, sums_ref, den_ref, ntemps_ref, nday_ref, hot_ref, acc_ref, hiso_ref, lhs_ref):
    del after_ref
    size_x, size_y = den_ref.shape
    chans = acc_ref.shape[0]
    levels = chans // 3
    _, node_rows = row_maps(size_x)
    lane1 = lanes_of(1)
    own = ((lane1 & 3) == 3) | (lane1 == 0)
    wide = lanes_of(chans)
    hiso = jnp.full((chans, LANES), 3.0, jnp.float32)
    inv = 1.0 / den_ref[...]
    for k, n in enumerate(node_rows):
        if k == 0:
            continue
        iso = iso_ref[pl.ds(n, chans, stride=size_x), :]
        hiso = jnp.where(wide == k, pltpu.roll(iso, k, 1), hiso)
        gain = jnp.where(own, 0.0, time_step * inv[n : n + 1, :])
        tracers = iso + gain * sums_ref[pl.ds(k * chans, chans), :]
        hi, lo = split(physics(tracers, ntemps_ref[k * levels : (k + 1) * levels, :], nday_ref[8 * k : 8 * k + 1, :]))
        lhs_ref[0:chans, (k - 1) * LANES : k * LANES] = hi
        lhs_ref[chans : 2 * chans, (k - 1) * LANES : k * LANES] = lo
    hiso_ref[...] = hiso
    both = dot(lhs_ref[...], hot_ref[...])
    acc_ref[...] = both[0:chans] + both[chans:]


def edge_columns_kernel(
    n_peers, iso_ref, sums_ref, den_ref, left_ref, acc_ref, pick_ref, ntemps_ref, nday_ref, hiso_ref, low_ref, before_ref, after_ref, *send_refs
):
    del after_ref
    chans, sites = acc_ref.shape
    levels = chans // 3
    size_x = den_ref.shape[0]
    _, node_rows = row_maps(size_x)
    count = len(node_rows)
    per_peer = sites // n_peers
    full, rest = per_peer // LANES, per_peer % LANES
    wide, lane1 = lanes_of(chans), lanes_of(1)
    unused = (lane1 & 3) == 3

    total = sums_ref[0:chans, :] + low_ref[0:chans, :] + jnp.where(wide == 0, before_ref[0:chans, :], 0.0)
    den = den_ref[0:1, :] + low_ref[chans : chans + 1, :] + jnp.where(lane1 == 0, before_ref[chans : chans + 1, :], 0.0)
    iso = iso_ref[pl.ds(0, chans, stride=size_x), :]
    new_row = iso + jnp.where(unused, 0.0, time_step / den) * total
    phys_row = physics(new_row, ntemps_ref[0:levels, :], nday_ref[0:1, :])

    in_use = (lane1 > 0) & (lane1 < count)
    dcol = jnp.where(in_use, left_ref[chans : chans + 1, :] + before_ref[chans : chans + 1, :], 1.0)
    tcol = jnp.where(in_use, left_ref[0:chans, :] + before_ref[0:chans, :], 0.0)
    new_col = hiso_ref[...] + (time_step / dcol) * tcol
    phys_col = physics(new_col, ntemps_ref[count * levels :, :], nday_ref[8 * count : 8 * count + 1, :])

    rhi, rlo = split(phys_row)
    chi, clo = split(phys_col)
    lhs = jnp.concatenate([jnp.concatenate([rhi, chi], axis=1), jnp.concatenate([rlo, clo], axis=1)], axis=0)
    both = dot(lhs, pick_ref[...])
    out = acc_ref[...] + (both[0:chans] + both[chans:])
    for p in range(n_peers):
        for j in range(full):
            t = p * full + j
            send_refs[p][0, j * chans : (j + 1) * chans, :] = out[:, t * LANES : (t + 1) * LANES]
    if rest:
        begin = n_peers * full * LANES
        for t in range(n_peers * rest // LANES):
            block = out[:, begin + t * LANES : begin + (t + 1) * LANES]
            block = jnp.concatenate([block, jnp.zeros((LANES - chans, LANES), jnp.float32)], axis=0).T
            at = t * LANES
            while at < (t + 1) * LANES:
                p, i = at // rest, at % rest
                count = min(rest - i, (t + 1) * LANES - at)
                send_refs[p][0, full * chans + i : full * chans + i + count, :] = block[at - t * LANES : at - t * LANES + count, :]
                at += count


def advance_kernel(iso_ref, sums_ref, den_ref, low_ref, high_ref, before_ref, after_ref, new_ref):
    size_x = den_ref.shape[0]
    chans = low_ref.shape[0] - 8
    shared, _ = row_maps(size_x)
    wide, lane1 = lanes_of(chans), lanes_of(1)
    for n in range(size_x):
        r = shared[n]
        total = sums_ref[pl.ds(r * chans, chans), :]
        den = den_ref[n : n + 1, :]
        for ref, at in ((low_ref, 0), (high_ref, size_x - 1)):
            if n == at:
                total = total + ref[0:chans, :]
                den = den + ref[chans : chans + 1, :]
        for ref, at in ((before_ref, 0), (after_ref, LANES - 1)):
            total = jnp.where(wide == at, total + ref[0:chans, r : r + 1], total)
            den = jnp.where(lane1 == at, den + ref[chans : chans + 1, r : r + 1], den)
        new_ref[pl.ds(n, chans, stride=size_x), :] = iso_ref[pl.ds(n, chans, stride=size_x), :] + (time_step / den) * total


def assemble_kernel(n_peers, paired, *refs):
    if paired:
        *slot_refs, out_hbm, got_ref, out_ref, sems = refs
        for k, ref in enumerate(slot_refs):
            got_ref[pl.ds(peer_of(k, paired), 1), :, :] = ref[...]
    else:
        got_ref, out_hbm, out_ref, sems = refs
    chans, sites = out_ref.shape
    per_peer = sites // n_peers
    full, rest = per_peer // LANES, per_peer % LANES
    lane = lanes_of(chans)
    blocks = [None] * (sites // LANES)

    def place(block, value, low, high):
        old = blocks[block]
        blocks[block] = value if old is None else jnp.where((lane >= low) & (lane < high), value, old)

    for p in range(n_peers):
        for j in range(full):
            begin = p * per_peer + j * LANES
            shift = begin % LANES
            value = got_ref[p, j * chans : (j + 1) * chans, :]
            if shift:
                value = pltpu.roll(value, shift, 1)
            place(begin // LANES, value, shift, LANES)
            if shift:
                place(begin // LANES + 1, value, 0, shift)
    if rest:
        tails = [got_ref[p, full * chans : full * chans + rest, :] for p in range(n_peers)]
        tails = jnp.concatenate(tails, axis=0)
        for t in range(n_peers * rest // LANES):
            block = tails[t * LANES : (t + 1) * LANES, :].T[0:chans, :]
            at = t * LANES
            while at < (t + 1) * LANES:
                p, i = at // rest, at % rest
                count = min(rest - i, (t + 1) * LANES - at)
                column = p * per_peer + full * LANES + i
                place(column // LANES, block, column % LANES, column % LANES + count)
                at += count
    copies = []
    for t, block in enumerate(blocks):
        at = pl.ds(t * LANES, LANES)
        out_ref[:, at] = block
        copies.append(pltpu.make_async_copy(out_ref.at[:, at], out_hbm.at[:, at], sems.at[t]))
        copies[-1].start()
    for c in copies:
        c.wait()


def exchange(slots, paired):
    if not paired:
        return [lax.all_to_all(jnp.concatenate(slots, axis=0), "blk", split_axis=0, concat_axis=0, tiled=True)]
    got = {}
    sent = (4, 5, 6, 7, 2, 3, 1)
    for n, k in enumerate(sent):
        block = slots[k]
        if n >= 5:
            block, got[sent[n - 5]] = lax.optimization_barrier((block, got[sent[n - 5]]))
        got[k] = lax.ppermute(block, "blk", [(j, j ^ k) for j in range(len(slots))])
    return [slots[0]] + [got[k] for k in range(1, len(slots))]


def call(kernel, outs, scratch, name, *args, **more):
    return pl.pallas_call(
        kernel,
        out_shape=outs,
        **more,
        scratch_shapes=scratch,
        name=name,
        compiler_params=pltpu.CompilerParams(vmem_limit_bytes=40 * 1024 * 1024),
    )(*args)


def on_device(
    isotope_ratios,
    advecting_velocity,
    metric_scaling,
    thermal_state,
    outgoing_site_order,
    daytime_indicator,
):
    size_x, size_y = metric_scaling.shape
    levels = isotope_ratios.shape[1]
    chans = 3 * levels
    sites = outgoing_site_order.shape[1]
    n_face, n_blk = lax.axis_size("face"), lax.axis_size("blk")
    shared, node_rows = row_maps(size_x)
    n_rows = shared[-1] + 1
    per_peer = sites // n_blk
    paired = n_blk == 8
    send_rows = chans * (per_peer // LANES) + per_peer % LANES

    def f32(*shape):
        return jax.ShapeDtypeStruct(shape, jnp.float32)

    iso = isotope_ratios.reshape(chans * size_x, size_y)
    wind = advecting_velocity.reshape(2 * levels * size_x, size_y)
    matrix = jnp.asarray(second_dim_matrix(size_y))
    edge = f32(chans + 8, LANES)
    integers = jax.ShapeDtypeStruct((1, sites), jnp.int32)
    bf16 = jnp.bfloat16
    args = (iso, wind, metric_scaling, matrix, thermal_state[0], daytime_indicator, outgoing_site_order)
    iso, wind, metric, matrix, temps, day, order, den, low, high = call(
        edge_rows_kernel,
        (*[jax.ShapeDtypeStruct(x.shape, x.dtype) for x in args], f32(size_x, size_y), edge, edge),
        [pltpu.VMEM((2 * chans, 2 * size_y), bf16)] * 2 + [pltpu.SemaphoreType.DMA((10,))],
        "edge_rows",
        *(pltpu.with_memory_space_constraint(x, pltpu.HBM) for x in args),
        in_specs=[pl.BlockSpec(memory_space=pltpu.HBM)] * len(args),
    )
    face_up = [(i, (i + 1) % n_face) for i in range(n_face)]
    blk_up = [(i, (i + 1) % n_blk) for i in range(n_blk)]
    from_low = lax.ppermute(high, "face", face_up)
    from_high = lax.ppermute(low, "face", [(j, i) for i, j in face_up])
    sums, left, right = call(
        transport_kernel,
        (f32(n_rows * chans, size_y), edge, edge),
        [pltpu.VMEM(((n_rows - 2) * chans, 2 * size_y), bf16)] * 2,
        "transport",
        iso,
        wind,
        metric,
        matrix,
        den,
        low,
        high,
    )
    count = len(node_rows)
    hot, pick, ntemps, nday = call(
        lambda *refs: send_order_kernel(n_blk, paired, *refs),
        (
            jax.ShapeDtypeStruct(((count - 1) * LANES, sites), bf16),
            jax.ShapeDtypeStruct((2 * LANES, sites), bf16),
            f32((count + 1) * levels, LANES),
            f32((count + 1) * 8, LANES),
        ),
        [pltpu.VMEM((n_blk, -(-per_peer // LANES) * LANES), jnp.int32)],
        "send_order",
        temps,
        day,
        order,
    )
    left, right = call(
        lambda *refs: corners_kernel(n_rows, *refs), (f32(chans + 8, LANES),) * 2, [], "corners", nday, left, right, from_low, from_high
    )
    before = lax.ppermute(right, "blk", blk_up)
    after = lax.ppermute(left, "blk", [(j, i) for i, j in blk_up])
    acc, hiso = call(
        inner_columns_kernel,
        (f32(chans, sites), f32(chans, LANES)),
        [pltpu.VMEM((2 * chans, (count - 1) * LANES), bf16)],
        "inner_columns",
        left,
        iso,
        sums,
        den,
        ntemps,
        nday,
        hot,
    )
    slots = call(
        lambda *refs: edge_columns_kernel(n_blk, *refs),
        (f32(1, send_rows, LANES),) * n_blk,
        [],
        "edge_columns",
        iso,
        sums,
        den,
        left,
        acc,
        pick,
        ntemps,
        nday,
        hiso,
        from_low,
        before,
        after,
    )
    got = exchange(slots, paired)
    new = call(advance_kernel, f32(chans * size_x, size_y), [], "advance", iso, sums, den, from_low, from_high, before, after)
    phys = call(
        lambda *refs: assemble_kernel(n_blk, paired, *refs),
        f32(chans, sites),
        ([pltpu.VMEM((n_blk, send_rows, LANES), jnp.float32)] if paired else [])
        + [pltpu.VMEM((chans, sites), jnp.float32), pltpu.SemaphoreType.DMA((sites // LANES,))],
        "assemble",
        *got,
        out_specs=pl.BlockSpec(memory_space=pltpu.HBM),
    )
    return (new.reshape(isotope_ratios.shape), phys.reshape(1, 3, levels, sites))


def solution(mesh):
    placed = (
        P(None, None, "face", "blk"),
        P(None, None, "face", "blk"),
        P("face", "blk"),
        P("face", None, "blk"),
        P("face", "blk"),
        P("face", "blk"),
    )
    return jax.shard_map(
        on_device,
        mesh=mesh,
        in_specs=placed,
        out_specs=(P(None, None, "face", "blk"), P("face", None, None, "blk")),
        check_vma=False,
    )
```

```python
import math

import jax
import jax.numpy as jnp
import numpy as np
from jax import lax
from jax.experimental import pallas as pl
from jax.experimental.pallas import tpu as pltpu
from jax.sharding import PartitionSpec as P

time_step = 0.006
absorb_coef = 0.02
heat_gain = 100.0
sat_base = 3.0
clausius = 0.07
ref_temp = 280.0
LANES = 128
SENT = (4, 7, 5, 3, 1, 6, 2)


def gll_tables():
    inv_root = 1.0 / math.sqrt(5.0)
    gll_nodes = np.array([-1.0, -inv_root, inv_root, 1.0])
    legendre = (5.0 * gll_nodes**3 - 3.0 * gll_nodes) / 2.0
    deriv_matrix = np.zeros((4, 4))
    for row_index in range(4):
        for col_index in range(4):
            if row_index != col_index:
                deriv_matrix[row_index, col_index] = legendre[row_index] / (
                    legendre[col_index] * (gll_nodes[row_index] - gll_nodes[col_index])
                )
    deriv_matrix[0, 0] = -3.0
    deriv_matrix[3, 3] = 3.0
    weights = np.array([1.0, 5.0, 5.0, 1.0]) / 6.0
    return (deriv_matrix, weights)


def row_maps(size_x):
    shared, count = [], -1
    for n in range(size_x):
        if n == 0 or n % 4 != 0:
            count += 1
        shared.append(count)
    return shared, [n for n in range(size_x) if n % 4 != 3]


def second_dim_matrix(size_y):
    deriv, weight = gll_tables()
    w = np.diag(np.tile(weight, size_y // 4))
    d = np.kron(np.eye(size_y // 4), deriv)
    e = np.eye(size_y)
    for m in range(3, size_y - 1, 4):
        e[m, m + 1] = e[m + 1, m] = 1.0
    both = np.concatenate([-(e @ w @ d).T, -(e @ w).T], axis=0)
    hi = both.astype(jnp.bfloat16)
    lo = (both - hi.astype(np.float64)).astype(jnp.bfloat16)
    return np.concatenate([hi, lo], axis=1)


def split(x):
    hi = x.astype(jnp.bfloat16)
    return hi, (x - hi.astype(jnp.float32)).astype(jnp.bfloat16)


def dot(a, b):
    return jnp.dot(a, b, preferred_element_type=jnp.float32)


def lanes_of(rows):
    return lax.broadcasted_iota(jnp.int32, (rows, LANES), 1)


def put_split(hi_ref, lo_ref, at, a, b):
    size_y = a.shape[1]
    ahi, alo = split(a)
    bhi, blo = split(b)
    hi_ref[at, 0:size_y] = ahi
    hi_ref[at, size_y : 2 * size_y] = bhi
    lo_ref[at, 0:size_y] = alo
    lo_ref[at, size_y : 2 * size_y] = blo


def second_dim(hi, lo, mat):
    size_y = hi.shape[1] // 2
    first = dot(hi, mat)
    return first[:, 0:size_y] + (first[:, size_y:] + dot(lo, mat[:, 0:size_y]))


def fluxes(iso_ref, wind_ref, metric_ref, s, n, weight):
    size_x = metric_ref.shape[0]
    part = wind_ref.shape[0] // 2
    levels = part // size_x
    jac = metric_ref[n : n + 1, :]
    q = iso_ref[pl.ds(s * part + n, levels, stride=size_x), :]
    fx = (jac * wind_ref[pl.ds(n, levels, stride=size_x), :]) * q
    if weight is None:
        return fx
    return fx, ((jac * weight) * wind_ref[pl.ds(part + n, levels, stride=size_x), :]) * q


def weighted_derivative(coefs, fx):
    total = None
    for coef, f in zip(coefs, fx):
        if coef != 0.0:
            total = float(coef) * f if total is None else total + float(coef) * f
    return total


def edge_rows_kernel(
    iso_hbm,
    wind_hbm,
    metric_hbm,
    mat_hbm,
    temps_hbm,
    day_hbm,
    order_hbm,
    iso_ref,
    wind_ref,
    metric_ref,
    mat_ref,
    temps_ref,
    day_ref,
    order_ref,
    den_ref,
    low_ref,
    high_ref,
    hi_ref,
    lo_ref,
    sems,
):
    size_x, size_y = metric_ref.shape
    part = wind_ref.shape[0] // 2
    levels = part // size_x
    chans = 3 * levels
    deriv, weight = gll_tables()
    copies = [pltpu.make_async_copy(metric_hbm, metric_ref, sems.at[0])]
    for k in range(2):
        copies.append(pltpu.make_async_copy(wind_hbm.at[pl.ds(k * part, part)], wind_ref.at[pl.ds(k * part, part)], sems.at[1 + k]))
    for s in range(3):
        copies.append(pltpu.make_async_copy(iso_hbm.at[pl.ds(s * part, part)], iso_ref.at[pl.ds(s * part, part)], sems.at[3 + s]))
    copies.append(pltpu.make_async_copy(mat_hbm, mat_ref, sems.at[6]))
    for k, (src, dst) in enumerate(((temps_hbm, temps_ref), (day_hbm, day_ref), (order_hbm, order_ref))):
        copies.append(pltpu.make_async_copy(src, dst, sems.at[7 + k]))
    for c in copies:
        c.start()

    copies[0].wait()
    lane = lanes_of(size_x)
    sub = lax.broadcasted_iota(jnp.int32, (size_x, LANES), 0)
    wl = jnp.where((lane % 4 == 0) | (lane % 4 == 3), float(weight[0]), float(weight[1]))
    ws = jnp.where((sub % 4 == 0) | (sub % 4 == 3), float(weight[0]), float(weight[1]))
    mass = (wl * ws) * metric_ref[...]
    after, before = pltpu.roll(mass, size_x - 1, 0), pltpu.roll(mass, 1, 0)
    mass = mass + jnp.where((sub % 4 == 3) & (sub != size_x - 1), after, 0.0) + jnp.where((sub % 4 == 0) & (sub != 0), before, 0.0)
    after, before = pltpu.roll(mass, size_y - 1, 1), pltpu.roll(mass, 1, 1)
    mass = mass + jnp.where((lane % 4 == 3) & (lane != size_y - 1), after, 0.0) + jnp.where((lane % 4 == 0) & (lane != 0), before, 0.0)
    den_ref[...] = mass

    for c in copies[1:3]:
        c.wait()
    for s in range(3):
        copies[3 + s].wait()
        for k, (first, i) in enumerate(((0, 0), (size_x - 4, 3))):
            fx = []
            for j in range(4):
                if j == i:
                    f, fy = fluxes(iso_ref, wind_ref, metric_ref, s, first + j, float(weight[i]))
                else:
                    f = fluxes(iso_ref, wind_ref, metric_ref, s, first + j, None)
                fx.append(f)
            put_split(hi_ref, lo_ref, pl.ds(k * chans + s * levels, levels), fy, weighted_derivative(weight[i] * deriv[i], fx))
    copies[6].wait()
    total = second_dim(hi_ref[...], lo_ref[...], mat_ref[...])
    for ref, k, n in ((low_ref, 0, 0), (high_ref, 1, size_x - 1)):
        ref[0:chans, :] = total[k * chans : (k + 1) * chans, :]
        ref[chans : chans + 8, :] = jnp.broadcast_to(mass[n : n + 1, :], (8, LANES))
    for c in copies[7:]:
        c.wait()


def transport_kernel(iso_ref, wind_ref, metric_ref, mat_ref, den_ref, low_ref, high_ref, sums_ref, left_ref, right_ref, hi_ref, lo_ref):
    size_x, size_y = metric_ref.shape
    levels = wind_ref.shape[0] // (2 * size_x)
    chans = 3 * levels
    deriv, weight = gll_tables()
    shared, _ = row_maps(size_x)
    n_rows = shared[-1] + 1
    for s in range(3):
        held = None
        for e in range(size_x // 4):
            fx, fy = [], []
            for j in range(4):
                f, g = fluxes(iso_ref, wind_ref, metric_ref, s, 4 * e + j, float(weight[j]))
                fx.append(f)
                fy.append(g)
            for i in range(4):
                n = 4 * e + i
                if n == 0 or n == size_x - 1:
                    continue
                a, b = fy[i], weighted_derivative(weight[i] * deriv[i], fx)
                if i == 0:
                    a, b = a + held[0], b + held[1]
                if i == 3:
                    held = (a, b)
                else:
                    put_split(hi_ref, lo_ref, pl.ds((shared[n] - 1) * chans + s * levels, levels), a, b)
    last = (n_rows - 1) * chans
    sums_ref[0:chans, :] = low_ref[0:chans, :]
    sums_ref[chans:last, :] = second_dim(hi_ref[...], lo_ref[...], mat_ref[...])
    sums_ref[last : last + chans, :] = high_ref[0:chans, :]

    mass = den_ref[...]
    wide, lane1 = lanes_of(chans), lanes_of(1)
    first_col = jnp.zeros((chans, LANES), jnp.float32)
    last_col = first_col
    first_den = jnp.zeros((1, LANES), jnp.float32)
    last_den = first_den
    for r in range(n_rows):
        here = sums_ref[pl.ds(r * chans, chans), :]
        n = shared.index(r)
        if r:
            first_col = jnp.where(wide == r, pltpu.roll(here, r, 1), first_col)
            first_den = jnp.where(lane1 == r, pltpu.roll(mass, r, 1)[n : n + 1, :], first_den)
        else:
            first_col = jnp.where(wide == 0, here, first_col)
            first_den = jnp.where(lane1 == 0, mass[0:1, :], first_den)
        last_col = jnp.where(wide == r, pltpu.roll(here, r + 1, 1), last_col)
        last_den = jnp.where(lane1 == r, pltpu.roll(mass, r + 1, 1)[n : n + 1, :], last_den)
    left_ref[0:chans, :] = first_col
    left_ref[chans : chans + 8, :] = jnp.broadcast_to(first_den, (8, LANES))
    right_ref[0:chans, :] = last_col
    right_ref[chans : chans + 8, :] = jnp.broadcast_to(last_den, (8, LANES))


def corners_kernel(n_rows, filler_ref, left_ref, right_ref, from_low_ref, from_high_ref, new_left_ref, new_right_ref):
    del filler_ref
    low, high = from_low_ref[...], from_high_ref[...]
    lane = lanes_of(low.shape[0])
    last = n_rows - 1
    new_left_ref[...] = left_ref[...] + jnp.where(lane == 0, low, 0.0) + jnp.where(lane == last, pltpu.roll(high, last, 1), 0.0)
    new_right_ref[...] = (
        right_ref[...] + jnp.where(lane == 0, pltpu.roll(low, 1, 1), 0.0) + jnp.where(lane == last, pltpu.roll(high, last + 1, 1), 0.0)
    )


def cumulative(x):
    rows = x.shape[0]
    sub = lax.broadcasted_iota(jnp.int32, x.shape, 0)
    step = 1
    while step < rows:
        x = x + jnp.where(sub >= step, pltpu.roll(x, step, 0), 0.0)
        step *= 2
    return x


def physics(tracers, temps, day):
    levels = temps.shape[0]
    vapour = tracers[0:levels]
    scaled = absorb_coef * vapour
    heating = heat_gain * scaled * jnp.exp(-cumulative(scaled))
    heated = temps + jnp.where(day == 1.0, heating, 0.0)
    saturation = sat_base * jnp.exp(clausius * (heated - ref_temp))
    remain = jnp.minimum(vapour, saturation)
    log_ratio = jnp.log(remain / vapour)
    inverse = 1.0 / heated
    alpha_heavy = jnp.exp(1137.0 * inverse * inverse - 0.4156 * inverse - 0.0020667)
    alpha_deut = jnp.exp(24844.0 * inverse * inverse - 76.248 * inverse + 0.052612)
    return jnp.concatenate(
        [
            remain,
            tracers[levels : 2 * levels] * jnp.exp(alpha_heavy * log_ratio),
            tracers[2 * levels :] * jnp.exp(alpha_deut * log_ratio),
        ],
        axis=0,
    )


def peer_of(slot, paired):
    return lax.axis_index("blk") ^ slot if paired else slot


def carriers(n_peers):
    return sorted({j ^ ((j - 1) % n_peers) for j in range(n_peers)})


def third(x):
    return lax.shift_right_logical(x * 43691, 17)


def spread_lanes(x):
    rows = x.shape[0]
    lane = lanes_of(rows)
    source = 3 * lax.shift_right_logical(lane, 2) + jnp.minimum(lane & 3, 2)
    padded = jnp.concatenate([x, jnp.zeros((rows, LANES - x.shape[1]), x.dtype)], axis=1)
    return jnp.take_along_axis(padded, source, axis=1)


def send_order_kernel(n_peers, paired, temps_ref, day_ref, order_ref, hot_ref, pick_ref, ntemps_ref, nday_ref, slots_ref):
    levels, sites = temps_ref.shape
    count = ntemps_ref.shape[0] // levels - 1
    per_row = sites // count
    per_peer = sites // n_peers
    full, rest = per_peer // LANES, per_peer % LANES

    order = order_ref[...]
    for p in range(n_peers):
        mine = order[:, p * per_peer : (p + 1) * per_peer]
        pad = slots_ref.shape[1] - per_peer
        slots_ref[p : p + 1, :] = jnp.concatenate([mine, jnp.zeros((1, pad), jnp.int32)], axis=1) if pad else mine
    peers = [slots_ref[pl.ds(peer_of(k, paired), 1), :] for k in range(n_peers)]
    pieces = [mine[:, LANES * j : LANES * (j + 1)] for mine in peers for j in range(full)]
    if rest:
        pieces += [mine[:, LANES * full : per_peer] for mine in peers]
    order = jnp.concatenate(pieces, axis=1)
    row = third(lax.shift_right_logical(order, 5))
    within = order - per_row * row
    group = third(within)
    node = 4 * group + (within - 3 * group)
    main = jnp.where((row == 0) | (node == 0), -1, (row - 1) * LANES + node)
    first = jnp.where(row == 0, node, -1)
    side = jnp.where((row != 0) & (node == 0), row, -1)
    sub = lax.broadcasted_iota(jnp.int32, (LANES, LANES), 0)

    def one_hot(index):
        return jnp.where(sub == index, 1.0, 0.0).astype(jnp.bfloat16)

    for t in range(sites // LANES):
        at = slice(t * LANES, (t + 1) * LANES)
        here = main[:, at]
        for k in range(count - 1):
            hot_ref[k * LANES : (k + 1) * LANES, at] = one_hot(here - k * LANES)
        pick_ref[0:LANES, at] = one_hot(first[:, at])
        pick_ref[LANES : 2 * LANES, at] = one_hot(side[:, at])

    temps = temps_ref[...]
    day = jnp.broadcast_to(day_ref[...].astype(jnp.float32), (8, sites))
    lane1, wide_l = lanes_of(1), lanes_of(levels)
    unused = (lane1 & 3) == 3
    side_temps = jnp.full((levels, LANES), ref_temp, jnp.float32)
    side_day = jnp.zeros((8, LANES), jnp.float32)
    for k in range(count):
        t_here = jnp.where(unused, ref_temp, spread_lanes(temps[:, k * per_row : (k + 1) * per_row]))
        d_here = spread_lanes(day[:, k * per_row : (k + 1) * per_row])
        ntemps_ref[k * levels : (k + 1) * levels, :] = t_here
        nday_ref[8 * k : 8 * k + 8, :] = d_here
        if k:
            side_temps = jnp.where(wide_l == k, pltpu.roll(t_here, k, 1), side_temps)
            side_day = jnp.where(lanes_of(8) == k, pltpu.roll(d_here, k, 1), side_day)
    ntemps_ref[count * levels :, :] = side_temps
    nday_ref[8 * count :, :] = side_day


def inner_columns_kernel(after_ref, iso_ref, sums_ref, den_ref, ntemps_ref, nday_ref, hot_ref, acc_ref, hiso_ref, lhs_ref):
    del after_ref
    size_x, size_y = den_ref.shape
    chans = acc_ref.shape[0]
    levels = chans // 3
    _, node_rows = row_maps(size_x)
    lane1 = lanes_of(1)
    own = ((lane1 & 3) == 3) | (lane1 == 0)
    wide = lanes_of(chans)
    hiso = jnp.full((chans, LANES), 3.0, jnp.float32)
    inv = 1.0 / den_ref[...]
    for k, n in enumerate(node_rows):
        if k == 0:
            continue
        iso = iso_ref[pl.ds(n, chans, stride=size_x), :]
        hiso = jnp.where(wide == k, pltpu.roll(iso, k, 1), hiso)
        gain = jnp.where(own, 0.0, time_step * inv[n : n + 1, :])
        tracers = iso + gain * sums_ref[pl.ds(k * chans, chans), :]
        hi, lo = split(physics(tracers, ntemps_ref[k * levels : (k + 1) * levels, :], nday_ref[8 * k : 8 * k + 1, :]))
        lhs_ref[0:chans, (k - 1) * LANES : k * LANES] = hi
        lhs_ref[chans : 2 * chans, (k - 1) * LANES : k * LANES] = lo
    hiso_ref[...] = hiso
    both = dot(lhs_ref[...], hot_ref[...])
    acc_ref[...] = both[0:chans] + both[chans:]


def edge_columns_kernel(
    n_peers, paired, iso_ref, sums_ref, den_ref, left_ref, acc_ref, pick_ref, ntemps_ref, nday_ref, hiso_ref, low_ref, before_ref, *send_refs
):
    chans, sites = acc_ref.shape
    levels = chans // 3
    size_x = den_ref.shape[0]
    _, node_rows = row_maps(size_x)
    count = len(node_rows)
    per_peer = sites // n_peers
    full, rest = per_peer // LANES, per_peer % LANES
    wide, lane1 = lanes_of(chans), lanes_of(1)
    unused = (lane1 & 3) == 3

    total = sums_ref[0:chans, :] + low_ref[0:chans, :] + jnp.where(wide == 0, before_ref[0:chans, :], 0.0)
    den = den_ref[0:1, :] + low_ref[chans : chans + 1, :] + jnp.where(lane1 == 0, before_ref[chans : chans + 1, :], 0.0)
    iso = iso_ref[pl.ds(0, chans, stride=size_x), :]
    new_row = iso + jnp.where(unused, 0.0, time_step / den) * total
    phys_row = physics(new_row, ntemps_ref[0:levels, :], nday_ref[0:1, :])

    in_use = (lane1 > 0) & (lane1 < count)
    dcol = jnp.where(in_use, left_ref[chans : chans + 1, :] + before_ref[chans : chans + 1, :], 1.0)
    tcol = jnp.where(in_use, left_ref[0:chans, :] + before_ref[0:chans, :], 0.0)
    new_col = hiso_ref[...] + (time_step / dcol) * tcol
    phys_col = physics(new_col, ntemps_ref[count * levels :, :], nday_ref[8 * count : 8 * count + 1, :])

    rhi, rlo = split(phys_row)
    chi, clo = split(phys_col)
    lhs = jnp.concatenate([jnp.concatenate([rhi, chi], axis=1), jnp.concatenate([rlo, clo], axis=1)], axis=0)
    both = dot(lhs, pick_ref[...])
    out = acc_ref[...] + (both[0:chans] + both[chans:])
    for p in range(n_peers):
        for j in range(full):
            t = p * full + j
            send_refs[p][0, j * chans : (j + 1) * chans, :] = out[:, t * LANES : (t + 1) * LANES]
    if rest:
        begin = n_peers * full * LANES
        for t in range(n_peers * rest // LANES):
            block = out[:, begin + t * LANES : begin + (t + 1) * LANES]
            block = jnp.concatenate([block, jnp.zeros((LANES - chans, LANES), jnp.float32)], axis=0).T
            at = t * LANES
            while at < (t + 1) * LANES:
                p, i = at // rest, at % rest
                count = min(rest - i, (t + 1) * LANES - at)
                send_refs[p][0, full * chans + i : full * chans + i + count, :] = block[at - t * LANES : at - t * LANES + count, :]
                at += count


    if paired:
        pad = jnp.zeros((LANES - left_ref.shape[0], LANES), jnp.float32)
        turned = jnp.concatenate([left_ref[...], pad], axis=0).T
        for k in carriers(n_peers):
            rows = send_refs[k].shape[1] - send_refs[0].shape[1]
            send_refs[k][0, send_refs[0].shape[1] :, :] = turned[0:rows, :]


def advance_kernel(n_peers, paired, carried, iso_ref, sums_ref, den_ref, low_ref, high_ref, before_ref, *rest):
    *after_refs, new_hbm, after_ref, new_ref, sems = rest
    size_x = den_ref.shape[0]
    chans = low_ref.shape[0] - 8
    shared, _ = row_maps(size_x)
    lane1 = lanes_of(1)
    if paired:
        me = lax.axis_index("blk")
        mine = me ^ lax.rem(me + 1, n_peers)
        turned = jnp.zeros((carried, LANES), jnp.float32)
        for k, ref in zip(carriers(n_peers), after_refs):
            turned = jnp.where(mine == k, ref[0, ref.shape[1] - carried :, :], turned)
        pad = jnp.zeros((LANES - carried, LANES), jnp.float32)
        after_ref[...] = jnp.concatenate([turned, pad], axis=0).T[0 : chans + 8, :]
    else:
        after_ref[...] = after_refs[0][...]
    gains = []
    for n in range(size_x):
        den = den_ref[n : n + 1, :]
        for ref, at in ((low_ref, 0), (high_ref, size_x - 1)):
            if n == at:
                den = den + ref[chans : chans + 1, :]
        for ref, at in ((before_ref, 0), (after_ref, LANES - 1)):
            den = jnp.where(lane1 == at, den + ref[chans : chans + 1, shared[n] : shared[n] + 1], den)
        gains.append(time_step / den)
    levels = chans // 3
    part = levels * size_x
    wide = lanes_of(levels)
    copies = []
    for s in range(3):
        for n in range(size_x):
            r = shared[n]
            total = sums_ref[pl.ds(r * chans + s * levels, levels), :]
            at_s = pl.ds(s * levels, levels)
            for ref, at in ((low_ref, 0), (high_ref, size_x - 1)):
                if n == at:
                    total = total + ref[at_s, :]
            for ref, at in ((before_ref, 0), (after_ref, LANES - 1)):
                total = jnp.where(wide == at, total + ref[at_s, r : r + 1], total)
            here = pl.ds(s * part + n, levels, stride=size_x)
            new_ref[here, :] = iso_ref[here, :] + gains[n] * total
        done = pl.ds(s * part, part)
        copies.append(pltpu.make_async_copy(new_ref.at[done], new_hbm.at[done], sems.at[s]))
        copies[-1].start()
    for c in copies:
        c.wait()


def assemble_kernel(n_peers, paired, *refs):
    if paired:
        *slot_refs, out_hbm, got_ref, out_ref, sems = refs
        for k, ref in enumerate(slot_refs):
            got_ref[pl.ds(peer_of(k, paired), 1), :, :] = ref[:, 0 : got_ref.shape[1], :]
    else:
        got_ref, out_hbm, out_ref, sems = refs
    chans, sites = out_ref.shape
    per_peer = sites // n_peers
    full, rest = per_peer // LANES, per_peer % LANES
    lane = lanes_of(chans)
    blocks = [None] * (sites // LANES)

    def place(block, value, low, high):
        old = blocks[block]
        blocks[block] = value if old is None else jnp.where((lane >= low) & (lane < high), value, old)

    for p in range(n_peers):
        for j in range(full):
            begin = p * per_peer + j * LANES
            shift = begin % LANES
            value = got_ref[p, j * chans : (j + 1) * chans, :]
            if shift:
                value = pltpu.roll(value, shift, 1)
            place(begin // LANES, value, shift, LANES)
            if shift:
                place(begin // LANES + 1, value, 0, shift)
    if rest:
        tails = [got_ref[p, full * chans : full * chans + rest, :] for p in range(n_peers)]
        tails = jnp.concatenate(tails, axis=0)
        for t in range(n_peers * rest // LANES):
            block = tails[t * LANES : (t + 1) * LANES, :].T[0:chans, :]
            at = t * LANES
            while at < (t + 1) * LANES:
                p, i = at // rest, at % rest
                count = min(rest - i, (t + 1) * LANES - at)
                column = p * per_peer + full * LANES + i
                place(column // LANES, block, column % LANES, column % LANES + count)
                at += count
    copies = []
    for t, block in enumerate(blocks):
        at = pl.ds(t * LANES, LANES)
        out_ref[:, at] = block
        copies.append(pltpu.make_async_copy(out_ref.at[:, at], out_hbm.at[:, at], sems.at[t]))
        copies[-1].start()
    for c in copies:
        c.wait()


def exchange(slots, left, paired):
    n_peers = lax.axis_size("blk")
    if not paired:
        got = lax.all_to_all(jnp.concatenate(slots, axis=0), "blk", split_axis=0, concat_axis=0, tiled=True)
        return [got], [lax.ppermute(left, "blk", [((j + 1) % n_peers, j) for j in range(n_peers)])]
    got = []
    sent = SENT
    for n, k in enumerate(sent):
        block = slots[k]
        if n >= 5:
            block, got[n - 5] = lax.optimization_barrier((block, got[n - 5]))
        got.append(lax.ppermute(block, "blk", [(j, j ^ k) for j in range(n_peers)]))
    got = [slots[0]] + [got[sent.index(k)] for k in range(1, n_peers)]
    return got, [got[k] for k in carriers(n_peers)]


def call(kernel, outs, scratch, name, *args, **more):
    return pl.pallas_call(
        kernel,
        out_shape=outs,
        **more,
        scratch_shapes=scratch,
        name=name,
        compiler_params=pltpu.CompilerParams(vmem_limit_bytes=40 * 1024 * 1024),
    )(*args)


def on_device(
    isotope_ratios,
    advecting_velocity,
    metric_scaling,
    thermal_state,
    outgoing_site_order,
    daytime_indicator,
):
    size_x, size_y = metric_scaling.shape
    levels = isotope_ratios.shape[1]
    chans = 3 * levels
    sites = outgoing_site_order.shape[1]
    n_face, n_blk = lax.axis_size("face"), lax.axis_size("blk")
    shared, node_rows = row_maps(size_x)
    n_rows = shared[-1] + 1
    per_peer = sites // n_blk
    paired = n_blk == 8
    carried = -(-n_rows // 8) * 8
    send_rows = chans * (per_peer // LANES) + per_peer % LANES

    def f32(*shape):
        return jax.ShapeDtypeStruct(shape, jnp.float32)

    iso = isotope_ratios.reshape(chans * size_x, size_y)
    wind = advecting_velocity.reshape(2 * levels * size_x, size_y)
    matrix = jnp.asarray(second_dim_matrix(size_y))
    edge = f32(chans + 8, LANES)
    integers = jax.ShapeDtypeStruct((1, sites), jnp.int32)
    bf16 = jnp.bfloat16
    args = (iso, wind, metric_scaling, matrix, thermal_state[0], daytime_indicator, outgoing_site_order)
    iso, wind, metric, matrix, temps, day, order, den, low, high = call(
        edge_rows_kernel,
        (*[jax.ShapeDtypeStruct(x.shape, x.dtype) for x in args], f32(size_x, size_y), edge, edge),
        [pltpu.VMEM((2 * chans, 2 * size_y), bf16)] * 2 + [pltpu.SemaphoreType.DMA((10,))],
        "edge_rows",
        *(pltpu.with_memory_space_constraint(x, pltpu.HBM) for x in args),
        in_specs=[pl.BlockSpec(memory_space=pltpu.HBM)] * len(args),
    )
    face_up = [(i, (i + 1) % n_face) for i in range(n_face)]
    blk_up = [(i, (i + 1) % n_blk) for i in range(n_blk)]
    from_low = lax.ppermute(high, "face", face_up)
    from_high = lax.ppermute(low, "face", [(j, i) for i, j in face_up])
    sums, left, right = call(
        transport_kernel,
        (f32(n_rows * chans, size_y), edge, edge),
        [pltpu.VMEM(((n_rows - 2) * chans, 2 * size_y), bf16)] * 2,
        "transport",
        iso,
        wind,
        metric,
        matrix,
        den,
        low,
        high,
    )
    count = len(node_rows)
    hot, pick, ntemps, nday = call(
        lambda *refs: send_order_kernel(n_blk, paired, *refs),
        (
            jax.ShapeDtypeStruct(((count - 1) * LANES, sites), bf16),
            jax.ShapeDtypeStruct((2 * LANES, sites), bf16),
            f32((count + 1) * levels, LANES),
            f32((count + 1) * 8, LANES),
        ),
        [pltpu.VMEM((n_blk, -(-per_peer // LANES) * LANES), jnp.int32)],
        "send_order",
        temps,
        day,
        order,
    )
    left, right = call(
        lambda *refs: corners_kernel(n_rows, *refs), (f32(chans + 8, LANES),) * 2, [], "corners", nday, left, right, from_low, from_high
    )
    before = lax.ppermute(right, "blk", blk_up)
    acc, hiso = call(
        inner_columns_kernel,
        (f32(chans, sites), f32(chans, LANES)),
        [pltpu.VMEM((2 * chans, (count - 1) * LANES), bf16)],
        "inner_columns",
        left,
        iso,
        sums,
        den,
        ntemps,
        nday,
        hot,
    )
    slots = call(
        lambda *refs: edge_columns_kernel(n_blk, paired, *refs),
        [f32(1, send_rows + (carried if paired and k in carriers(n_blk) else 0), LANES) for k in range(n_blk)],
        [],
        "edge_columns",
        iso,
        sums,
        den,
        left,
        acc,
        pick,
        ntemps,
        nday,
        hiso,
        from_low,
        before,
    )
    got, after = exchange(slots, left, paired)
    new = call(
        lambda *refs: advance_kernel(n_blk, paired, carried, *refs),
        f32(chans * size_x, size_y),
        [pltpu.VMEM((chans + 8, LANES), jnp.float32), pltpu.VMEM((chans * size_x, size_y), jnp.float32), pltpu.SemaphoreType.DMA((3,))],
        "advance",
        iso,
        sums,
        den,
        from_low,
        from_high,
        before,
        *after,
        out_specs=pl.BlockSpec(memory_space=pltpu.HBM),
    )
    phys = call(
        lambda *refs: assemble_kernel(n_blk, paired, *refs),
        f32(chans, sites),
        ([pltpu.VMEM((n_blk, send_rows, LANES), jnp.float32)] if paired else [])
        + [pltpu.VMEM((chans, sites), jnp.float32), pltpu.SemaphoreType.DMA((sites // LANES,))],
        "assemble",
        *got,
        out_specs=pl.BlockSpec(memory_space=pltpu.HBM),
    )
    return (new.reshape(isotope_ratios.shape), phys.reshape(1, 3, levels, sites))


def solution(mesh):
    placed = (
        P(None, None, "face", "blk"),
        P(None, None, "face", "blk"),
        P("face", "blk"),
        P("face", None, "blk"),
        P("face", "blk"),
        P("face", "blk"),
    )
    return jax.shard_map(
        on_device,
        mesh=mesh,
        in_specs=placed,
        out_specs=(P(None, None, "face", "blk"), P("face", None, None, "blk")),
        check_vma=False,
    )
```

```python
import math

import jax
import jax.numpy as jnp
import numpy as np
from jax import lax
from jax.experimental import pallas as pl
from jax.experimental.pallas import tpu as pltpu
from jax.sharding import PartitionSpec as P

time_step = 0.006
absorb_coef = 0.02
heat_gain = 100.0
sat_base = 3.0
clausius = 0.07
ref_temp = 280.0
LANES = 128
SENT = (7, 4, 5, 1, 3, 6, 2)
AFTER = {6: (1,), 2: (7,)}


def gll_tables():
    inv_root = 1.0 / math.sqrt(5.0)
    gll_nodes = np.array([-1.0, -inv_root, inv_root, 1.0])
    legendre = (5.0 * gll_nodes**3 - 3.0 * gll_nodes) / 2.0
    deriv_matrix = np.zeros((4, 4))
    for row_index in range(4):
        for col_index in range(4):
            if row_index != col_index:
                deriv_matrix[row_index, col_index] = legendre[row_index] / (
                    legendre[col_index] * (gll_nodes[row_index] - gll_nodes[col_index])
                )
    deriv_matrix[0, 0] = -3.0
    deriv_matrix[3, 3] = 3.0
    weights = np.array([1.0, 5.0, 5.0, 1.0]) / 6.0
    return (deriv_matrix, weights)


def row_maps(size_x):
    shared, count = [], -1
    for n in range(size_x):
        if n == 0 or n % 4 != 0:
            count += 1
        shared.append(count)
    return shared, [n for n in range(size_x) if n % 4 != 3]


def second_dim_matrix(size_y):
    deriv, weight = gll_tables()
    w = np.diag(np.tile(weight, size_y // 4))
    d = np.kron(np.eye(size_y // 4), deriv)
    e = np.eye(size_y)
    for m in range(3, size_y - 1, 4):
        e[m, m + 1] = e[m + 1, m] = 1.0
    both = np.concatenate([-(e @ w @ d).T, -(e @ w).T], axis=0)
    hi = both.astype(jnp.bfloat16)
    lo = (both - hi.astype(np.float64)).astype(jnp.bfloat16)
    return np.concatenate([hi, lo], axis=1)


def split(x):
    hi = x.astype(jnp.bfloat16)
    return hi, (x - hi.astype(jnp.float32)).astype(jnp.bfloat16)


def dot(a, b):
    return jnp.dot(a, b, preferred_element_type=jnp.float32)


def lanes_of(rows):
    return lax.broadcasted_iota(jnp.int32, (rows, LANES), 1)


def put_split(hi_ref, lo_ref, at, a, b):
    size_y = a.shape[1]
    ahi, alo = split(a)
    bhi, blo = split(b)
    hi_ref[at, 0:size_y] = ahi
    hi_ref[at, size_y : 2 * size_y] = bhi
    lo_ref[at, 0:size_y] = alo
    lo_ref[at, size_y : 2 * size_y] = blo


def second_dim(hi, lo, mat):
    size_y = hi.shape[1] // 2
    first = dot(hi, mat)
    return first[:, 0:size_y] + (first[:, size_y:] + dot(lo, mat[:, 0:size_y]))


def fluxes(iso_ref, wind_ref, metric_ref, s, n, weight):
    size_x = metric_ref.shape[0]
    part = wind_ref.shape[0] // 2
    levels = part // size_x
    jac = metric_ref[n : n + 1, :]
    q = iso_ref[pl.ds(s * part + n, levels, stride=size_x), :]
    fx = (jac * wind_ref[pl.ds(n, levels, stride=size_x), :]) * q
    if weight is None:
        return fx
    return fx, ((jac * weight) * wind_ref[pl.ds(part + n, levels, stride=size_x), :]) * q


def weighted_derivative(coefs, fx):
    total = None
    for coef, f in zip(coefs, fx):
        if coef != 0.0:
            total = float(coef) * f if total is None else total + float(coef) * f
    return total


def transport_kernel(
    iso_hbm,
    wind_hbm,
    metric_hbm,
    mat_hbm,
    temps_hbm,
    day_hbm,
    order_hbm,
    iso_ref,
    temps_ref,
    day_ref,
    order_ref,
    sums_ref,
    den_ref,
    low_ref,
    high_ref,
    right_ref,
    wind_ref,
    metric_ref,
    mat_ref,
    hi_ref,
    lo_ref,
    sems,
):
    size_x, size_y = metric_ref.shape
    part = wind_ref.shape[0] // 2
    levels = part // size_x
    chans = 3 * levels
    deriv, weight = gll_tables()
    shared, _ = row_maps(size_x)
    n_rows = shared[-1] + 1
    copies = [pltpu.make_async_copy(metric_hbm, metric_ref, sems.at[0])]
    for k in range(2):
        copies.append(pltpu.make_async_copy(wind_hbm.at[pl.ds(k * part, part)], wind_ref.at[pl.ds(k * part, part)], sems.at[1 + k]))
    for s in range(3):
        copies.append(pltpu.make_async_copy(iso_hbm.at[pl.ds(s * part, part)], iso_ref.at[pl.ds(s * part, part)], sems.at[3 + s]))
    copies.append(pltpu.make_async_copy(mat_hbm, mat_ref, sems.at[6]))
    for k, (src, dst) in enumerate(((temps_hbm, temps_ref), (day_hbm, day_ref), (order_hbm, order_ref))):
        copies.append(pltpu.make_async_copy(src, dst, sems.at[7 + k]))
    for c in copies:
        c.start()

    copies[0].wait()
    lane = lanes_of(size_x)
    sub = lax.broadcasted_iota(jnp.int32, (size_x, LANES), 0)
    wl = jnp.where((lane % 4 == 0) | (lane % 4 == 3), float(weight[0]), float(weight[1]))
    ws = jnp.where((sub % 4 == 0) | (sub % 4 == 3), float(weight[0]), float(weight[1]))
    mass = (wl * ws) * metric_ref[...]
    after, before = pltpu.roll(mass, size_x - 1, 0), pltpu.roll(mass, 1, 0)
    mass = mass + jnp.where((sub % 4 == 3) & (sub != size_x - 1), after, 0.0) + jnp.where((sub % 4 == 0) & (sub != 0), before, 0.0)
    after, before = pltpu.roll(mass, size_y - 1, 1), pltpu.roll(mass, 1, 1)
    mass = mass + jnp.where((lane % 4 == 3) & (lane != size_y - 1), after, 0.0) + jnp.where((lane % 4 == 0) & (lane != 0), before, 0.0)
    den_ref[...] = mass

    for c in copies[1:3]:
        c.wait()
    for s in range(3):
        copies[3 + s].wait()
        held = None
        for e in range(size_x // 4):
            fx, fy = [], []
            for j in range(4):
                f, g = fluxes(iso_ref, wind_ref, metric_ref, s, 4 * e + j, float(weight[j]))
                fx.append(f)
                fy.append(g)
            for i in range(4):
                n = 4 * e + i
                a, b = fy[i], weighted_derivative(weight[i] * deriv[i], fx)
                if i == 0 and held is not None:
                    a, b = a + held[0], b + held[1]
                if i == 3 and n != size_x - 1:
                    held = (a, b)
                else:
                    put_split(hi_ref, lo_ref, pl.ds(shared[n] * chans + s * levels, levels), a, b)
    copies[6].wait()
    sums_ref[...] = second_dim(hi_ref[...], lo_ref[...], mat_ref[...])
    for ref, r, n in ((low_ref, 0, 0), (high_ref, n_rows - 1, size_x - 1)):
        ref[0:chans, :] = sums_ref[pl.ds(r * chans, chans), :]
        ref[chans : chans + 8, :] = jnp.broadcast_to(mass[n : n + 1, :], (8, LANES))
    gather_column(size_y - 1, sums_ref, mass, right_ref)
    for c in copies[7:]:
        c.wait()


def gather_column(lane, sums_ref, mass, out_ref):
    chans = out_ref.shape[0] - 8
    shared, _ = row_maps(mass.shape[0])
    wide, lane1 = lanes_of(chans), lanes_of(1)
    col = jnp.zeros((chans, LANES), jnp.float32)
    den = jnp.zeros((1, LANES), jnp.float32)
    for r in range(shared[-1] + 1):
        shift = (r - lane) % LANES
        here, n = sums_ref[pl.ds(r * chans, chans), :], shared.index(r)
        col = jnp.where(wide == r, pltpu.roll(here, shift, 1) if shift else here, col)
        den = jnp.where(lane1 == r, (pltpu.roll(mass, shift, 1) if shift else mass)[n : n + 1, :], den)
    out_ref[0:chans, :] = col
    out_ref[chans : chans + 8, :] = jnp.broadcast_to(den, (8, LANES))


def cumulative(x):
    rows = x.shape[0]
    sub = lax.broadcasted_iota(jnp.int32, x.shape, 0)
    step = 1
    while step < rows:
        x = x + jnp.where(sub >= step, pltpu.roll(x, step, 0), 0.0)
        step *= 2
    return x


def physics(tracers, temps, day):
    levels = temps.shape[0]
    vapour = tracers[0:levels]
    scaled = absorb_coef * vapour
    heating = heat_gain * scaled * jnp.exp(-cumulative(scaled))
    heated = temps + jnp.where(day == 1.0, heating, 0.0)
    saturation = sat_base * jnp.exp(clausius * (heated - ref_temp))
    remain = jnp.minimum(vapour, saturation)
    log_ratio = jnp.log(remain / vapour)
    inverse = 1.0 / heated
    alpha_heavy = jnp.exp(1137.0 * inverse * inverse - 0.4156 * inverse - 0.0020667)
    alpha_deut = jnp.exp(24844.0 * inverse * inverse - 76.248 * inverse + 0.052612)
    return jnp.concatenate(
        [
            remain,
            tracers[levels : 2 * levels] * jnp.exp(alpha_heavy * log_ratio),
            tracers[2 * levels :] * jnp.exp(alpha_deut * log_ratio),
        ],
        axis=0,
    )


def peer_of(slot, paired):
    return lax.axis_index("blk") ^ slot if paired else slot


def carriers(n_peers):
    return sorted({j ^ ((j - 1) % n_peers) for j in range(n_peers)})


def third(x):
    return lax.shift_right_logical(x * 43691, 17)


def spread_lanes(x):
    rows = x.shape[0]
    lane = lanes_of(rows)
    source = 3 * lax.shift_right_logical(lane, 2) + jnp.minimum(lane & 3, 2)
    padded = jnp.concatenate([x, jnp.zeros((rows, LANES - x.shape[1]), x.dtype)], axis=1)
    return jnp.take_along_axis(padded, source, axis=1)


def send_order_kernel(n_peers, paired, after_ref, temps_ref, day_ref, order_ref, hot_ref, pick_ref, ntemps_ref, nday_ref, slots_ref):
    del after_ref
    levels, sites = temps_ref.shape
    count = ntemps_ref.shape[0] // levels - 1
    per_row = sites // count
    per_peer = sites // n_peers
    full, rest = per_peer // LANES, per_peer % LANES

    order = order_ref[...]
    for p in range(n_peers):
        mine = order[:, p * per_peer : (p + 1) * per_peer]
        pad = slots_ref.shape[1] - per_peer
        slots_ref[p : p + 1, :] = jnp.concatenate([mine, jnp.zeros((1, pad), jnp.int32)], axis=1) if pad else mine
    peers = [slots_ref[pl.ds(peer_of(k, paired), 1), :] for k in range(n_peers)]
    pieces = [mine[:, LANES * j : LANES * (j + 1)] for mine in peers for j in range(full)]
    if rest:
        pieces += [mine[:, LANES * full : per_peer] for mine in peers]
    order = jnp.concatenate(pieces, axis=1)
    row = third(lax.shift_right_logical(order, 5))
    within = order - per_row * row
    group = third(within)
    node = 4 * group + (within - 3 * group)
    main = jnp.where((row == 0) | (node == 0), -1, (row - 1) * LANES + node)
    first = jnp.where(row == 0, node, -1)
    side = jnp.where((row != 0) & (node == 0), row, -1)
    bf16 = jnp.bfloat16
    sub = lax.broadcasted_iota(jnp.int32, (LANES, LANES), 0).astype(bf16)

    def one_hot(index):
        index = jnp.broadcast_to(jnp.clip(index, -1, LANES).astype(jnp.float32), (16, LANES)).astype(bf16)
        index = jnp.concatenate([index] * (LANES // 16), axis=0)
        return jnp.where(sub == index, jnp.ones((), bf16), jnp.zeros((), bf16))

    for t in range(sites // LANES):
        at = slice(t * LANES, (t + 1) * LANES)
        here = main[:, at]
        for k in range(count - 1):
            hot_ref[k * LANES : (k + 1) * LANES, at] = one_hot(here - k * LANES)
        pick_ref[0:LANES, at] = one_hot(first[:, at])
        pick_ref[LANES : 2 * LANES, at] = one_hot(side[:, at])

    temps = temps_ref[...]
    day = jnp.broadcast_to(day_ref[...].astype(jnp.float32), (8, sites))
    lane1, wide_l = lanes_of(1), lanes_of(levels)
    unused = (lane1 & 3) == 3
    side_temps = jnp.full((levels, LANES), ref_temp, jnp.float32)
    side_day = jnp.zeros((8, LANES), jnp.float32)
    for k in range(count):
        t_here = jnp.where(unused, ref_temp, spread_lanes(temps[:, k * per_row : (k + 1) * per_row]))
        d_here = spread_lanes(day[:, k * per_row : (k + 1) * per_row])
        ntemps_ref[k * levels : (k + 1) * levels, :] = t_here
        nday_ref[8 * k : 8 * k + 8, :] = d_here
        if k:
            side_temps = jnp.where(wide_l == k, pltpu.roll(t_here, k, 1), side_temps)
            side_day = jnp.where(lanes_of(8) == k, pltpu.roll(d_here, k, 1), side_day)
    ntemps_ref[count * levels :, :] = side_temps
    nday_ref[8 * count :, :] = side_day


def inner_columns_kernel(iso_ref, sums_ref, den_ref, ntemps_ref, nday_ref, hot_ref, acc_ref, hiso_ref, left_ref, lhs_ref):
    size_x, size_y = den_ref.shape
    chans = acc_ref.shape[0]
    levels = chans // 3
    _, node_rows = row_maps(size_x)
    lane1 = lanes_of(1)
    own = ((lane1 & 3) == 3) | (lane1 == 0)
    wide = lanes_of(chans)
    hiso = jnp.full((chans, LANES), 3.0, jnp.float32)
    inv = 1.0 / den_ref[...]
    for k, n in enumerate(node_rows):
        if k == 0:
            continue
        iso = iso_ref[pl.ds(n, chans, stride=size_x), :]
        hiso = jnp.where(wide == k, pltpu.roll(iso, k, 1), hiso)
        gain = jnp.where(own, 0.0, time_step * inv[n : n + 1, :])
        tracers = iso + gain * sums_ref[pl.ds(k * chans, chans), :]
        hi, lo = split(physics(tracers, ntemps_ref[k * levels : (k + 1) * levels, :], nday_ref[8 * k : 8 * k + 1, :]))
        lhs_ref[0:chans, (k - 1) * LANES : k * LANES] = hi
        lhs_ref[chans : 2 * chans, (k - 1) * LANES : k * LANES] = lo
    hiso_ref[...] = hiso
    gather_column(0, sums_ref, den_ref[...], left_ref)
    both = dot(lhs_ref[...], hot_ref[...])
    acc_ref[...] = both[0:chans] + both[chans:]


def edge_columns_kernel(
    n_peers, paired, iso_ref, sums_ref, den_ref, left_ref, acc_ref, pick_ref, ntemps_ref, nday_ref, hiso_ref, corner_ref, before_ref, low_ref, high_ref, *send_refs
):
    chans, sites = acc_ref.shape
    levels = chans // 3
    size_x = den_ref.shape[0]
    _, node_rows = row_maps(size_x)
    count = len(node_rows)
    per_peer = sites // n_peers
    full, rest = per_peer // LANES, per_peer % LANES
    wide, lane1 = lanes_of(chans), lanes_of(1)
    unused = (lane1 & 3) == 3

    last = row_maps(size_x)[0][-1]
    extra = before_ref[...] + pltpu.roll(corner_ref[...], LANES - last, 1)
    total = sums_ref[0:chans, :] + low_ref[0:chans, :] + jnp.where(wide == 0, extra[0:chans, :], 0.0)
    den = den_ref[0:1, :] + low_ref[chans : chans + 1, :] + jnp.where(lane1 == 0, extra[chans : chans + 1, :], 0.0)
    iso = iso_ref[pl.ds(0, chans, stride=size_x), :]
    new_row = iso + jnp.where(unused, 0.0, time_step / den) * total
    phys_row = physics(new_row, ntemps_ref[0:levels, :], nday_ref[0:1, :])

    in_use = (lane1 > 0) & (lane1 < count)
    dcol = jnp.where(in_use, left_ref[chans : chans + 1, :] + before_ref[chans : chans + 1, :], 1.0)
    tcol = jnp.where(in_use, left_ref[0:chans, :] + before_ref[0:chans, :], 0.0)
    new_col = hiso_ref[...] + (time_step / dcol) * tcol
    phys_col = physics(new_col, ntemps_ref[count * levels :, :], nday_ref[8 * count : 8 * count + 1, :])

    rhi, rlo = split(phys_row)
    chi, clo = split(phys_col)
    lhs = jnp.concatenate([jnp.concatenate([rhi, chi], axis=1), jnp.concatenate([rlo, clo], axis=1)], axis=0)
    both = dot(lhs, pick_ref[...])
    out = acc_ref[...] + (both[0:chans] + both[chans:])
    for p in range(n_peers):
        for j in range(full):
            t = p * full + j
            send_refs[p][0, j * chans : (j + 1) * chans, :] = out[:, t * LANES : (t + 1) * LANES]
    if rest:
        begin = n_peers * full * LANES
        for t in range(n_peers * rest // LANES):
            block = out[:, begin + t * LANES : begin + (t + 1) * LANES]
            block = jnp.concatenate([block, jnp.zeros((LANES - chans, LANES), jnp.float32)], axis=0).T
            at = t * LANES
            while at < (t + 1) * LANES:
                p, i = at // rest, at % rest
                count = min(rest - i, (t + 1) * LANES - at)
                send_refs[p][0, full * chans + i : full * chans + i + count, :] = block[at - t * LANES : at - t * LANES + count, :]
                at += count


    lane, high = lanes_of(chans + 8), high_ref[...]
    edge = left_ref[...] + jnp.where(lane == 0, low_ref[...], 0.0) + jnp.where(lane == last, pltpu.roll(high, last, 1), 0.0)
    edge = jnp.where(lane == last + 1, pltpu.roll(high, last + 2, 1), edge)
    if not paired:
        send_refs[n_peers][...] = edge
    else:
        turned = jnp.concatenate([edge, jnp.zeros((LANES - edge.shape[0], LANES), jnp.float32)], axis=0).T
        for k in carriers(n_peers):
            rows = send_refs[k].shape[1] - send_refs[0].shape[1]
            send_refs[k][0, send_refs[0].shape[1] :, :] = turned[0:rows, :]


def advance_kernel(n_peers, paired, carried, iso_ref, sums_ref, den_ref, corner_ref, near_ref, low_ref, high_ref, *rest):
    *edge_refs, new_hbm, before_ref, after_ref, new_ref, sems = rest
    size_x = den_ref.shape[0]
    chans = low_ref.shape[0] - 8
    shared, _ = row_maps(size_x)
    last = shared[-1]
    lane1 = lanes_of(1)
    if paired:
        me = lax.axis_index("blk")
        turned = []
        for other in (lax.rem(me + 1, n_peers), lax.rem(me + n_peers - 1, n_peers)):
            mine = jnp.zeros((carried, LANES), jnp.float32)
            for k, ref in zip(carriers(n_peers), edge_refs):
                mine = jnp.where((me ^ other) == k, ref[0, ref.shape[1] - carried :, :], mine)
            turned.append(mine)
        pad = jnp.zeros((LANES - 2 * carried, LANES), jnp.float32)
        both = jnp.concatenate(turned + [pad], axis=0).T[0 : chans + 8, :]
        after_ref[...] = both
        beside = pltpu.roll(both, LANES - carried - 1, 1)
    else:
        after_ref[...] = edge_refs[0][...]
        beside = pltpu.roll(edge_refs[1][...], LANES - 1, 1)
    lane = lanes_of(chans + 8)
    near = near_ref[...] + jnp.where(lane == 0, pltpu.roll(corner_ref[...], LANES - last, 1), 0.0)
    before_ref[...] = near + jnp.where(lane == last, beside, 0.0)
    gains = []
    for n in range(size_x):
        den = den_ref[n : n + 1, :]
        for ref, at in ((low_ref, 0), (high_ref, size_x - 1)):
            if n == at:
                den = den + ref[chans : chans + 1, :]
        for ref, at in ((before_ref, 0), (after_ref, LANES - 1)):
            den = jnp.where(lane1 == at, den + ref[chans : chans + 1, shared[n] : shared[n] + 1], den)
        gains.append(time_step / den)
    levels = chans // 3
    part = levels * size_x
    wide = lanes_of(levels)
    copies = []
    for s in range(3):
        for n in range(size_x):
            r = shared[n]
            total = sums_ref[pl.ds(r * chans + s * levels, levels), :]
            at_s = pl.ds(s * levels, levels)
            for ref, at in ((low_ref, 0), (high_ref, size_x - 1)):
                if n == at:
                    total = total + ref[at_s, :]
            for ref, at in ((before_ref, 0), (after_ref, LANES - 1)):
                total = jnp.where(wide == at, total + ref[at_s, r : r + 1], total)
            here = pl.ds(s * part + n, levels, stride=size_x)
            new_ref[here, :] = iso_ref[here, :] + gains[n] * total
        done = pl.ds(s * part, part)
        copies.append(pltpu.make_async_copy(new_ref.at[done], new_hbm.at[done], sems.at[s]))
        copies[-1].start()
    for c in copies:
        c.wait()


def assemble_kernel(n_peers, paired, *refs):
    if paired:
        *slot_refs, out_hbm, got_ref, out_ref, sems = refs
        for k, ref in enumerate(slot_refs):
            got_ref[pl.ds(peer_of(k, paired), 1), :, :] = ref[:, 0 : got_ref.shape[1], :]
    else:
        got_ref, out_hbm, out_ref, sems = refs
    chans, sites = out_ref.shape
    per_peer = sites // n_peers
    full, rest = per_peer // LANES, per_peer % LANES
    lane = lanes_of(chans)
    blocks = [None] * (sites // LANES)

    def place(block, value, low, high):
        old = blocks[block]
        blocks[block] = value if old is None else jnp.where((lane >= low) & (lane < high), value, old)

    for p in range(n_peers):
        for j in range(full):
            begin = p * per_peer + j * LANES
            shift = begin % LANES
            value = got_ref[p, j * chans : (j + 1) * chans, :]
            if shift:
                value = pltpu.roll(value, shift, 1)
            place(begin // LANES, value, shift, LANES)
            if shift:
                place(begin // LANES + 1, value, 0, shift)
    if rest:
        tails = [got_ref[p, full * chans : full * chans + rest, :] for p in range(n_peers)]
        tails = jnp.concatenate(tails, axis=0)
        for t in range(n_peers * rest // LANES):
            block = tails[t * LANES : (t + 1) * LANES, :].T[0:chans, :]
            at = t * LANES
            while at < (t + 1) * LANES:
                p, i = at // rest, at % rest
                count = min(rest - i, (t + 1) * LANES - at)
                column = p * per_peer + full * LANES + i
                place(column // LANES, block, column % LANES, column % LANES + count)
                at += count
    copies = []
    for t, block in enumerate(blocks):
        at = pl.ds(t * LANES, LANES)
        out_ref[:, at] = block
        copies.append(pltpu.make_async_copy(out_ref.at[:, at], out_hbm.at[:, at], sems.at[t]))
        copies[-1].start()
    for c in copies:
        c.wait()


def exchange(slots, edge, paired):
    n_peers = lax.axis_size("blk")
    if not paired:
        got = lax.all_to_all(jnp.concatenate(slots, axis=0), "blk", split_axis=0, concat_axis=0, tiled=True)
        up = [(j, (j + 1) % n_peers) for j in range(n_peers)]
        return [got], [lax.ppermute(edge[0], "blk", [(j, i) for i, j in up]), lax.ppermute(edge[0], "blk", up)]
    got = {0: slots[0]}
    for k in SENT:
        block = slots[k]
        for w in AFTER.get(k, ()):
            block, got[w] = lax.optimization_barrier((block, got[w]))
        got[k] = lax.ppermute(block, "blk", [(j, j ^ k) for j in range(n_peers)])
    got = [got[k] for k in range(n_peers)]
    return got, [got[k] for k in carriers(n_peers)]


def call(kernel, outs, scratch, name, *args, **more):
    return pl.pallas_call(
        kernel,
        out_shape=outs,
        **more,
        scratch_shapes=scratch,
        name=name,
        compiler_params=pltpu.CompilerParams(vmem_limit_bytes=40 * 1024 * 1024),
    )(*args)


def on_device(
    isotope_ratios,
    advecting_velocity,
    metric_scaling,
    thermal_state,
    outgoing_site_order,
    daytime_indicator,
):
    size_x, size_y = metric_scaling.shape
    levels = isotope_ratios.shape[1]
    chans = 3 * levels
    sites = outgoing_site_order.shape[1]
    n_face, n_blk = lax.axis_size("face"), lax.axis_size("blk")
    shared, node_rows = row_maps(size_x)
    n_rows = shared[-1] + 1
    per_peer = sites // n_blk
    paired = n_blk == 8
    carried = -(-(n_rows + 1) // 8) * 8
    send_rows = chans * (per_peer // LANES) + per_peer % LANES

    def f32(*shape):
        return jax.ShapeDtypeStruct(shape, jnp.float32)

    iso = isotope_ratios.reshape(chans * size_x, size_y)
    wind = advecting_velocity.reshape(2 * levels * size_x, size_y)
    matrix = jnp.asarray(second_dim_matrix(size_y))
    edge = f32(chans + 8, LANES)
    integers = jax.ShapeDtypeStruct((1, sites), jnp.int32)
    bf16 = jnp.bfloat16
    args = (iso, wind, metric_scaling, matrix, thermal_state[0], daytime_indicator, outgoing_site_order)
    iso, temps, day, order, sums, den, low, high, right = call(
        transport_kernel,
        (
            f32(*iso.shape),
            f32(levels, sites),
            integers,
            integers,
            f32(n_rows * chans, size_y),
            f32(size_x, size_y),
            *[edge] * 3,
        ),
        [
            pltpu.VMEM(wind.shape, jnp.float32),
            pltpu.VMEM((size_x, size_y), jnp.float32),
            pltpu.VMEM(matrix.shape, bf16),
        ]
        + [pltpu.VMEM((n_rows * chans, 2 * size_y), bf16)] * 2 + [pltpu.SemaphoreType.DMA((10,))],
        "transport",
        *(pltpu.with_memory_space_constraint(x, pltpu.HBM) for x in args),
        in_specs=[pl.BlockSpec(memory_space=pltpu.HBM)] * len(args),
    )
    face_up = [(i, (i + 1) % n_face) for i in range(n_face)]
    blk_up = [(i, (i + 1) % n_blk) for i in range(n_blk)]
    corner = lax.ppermute(
        right, ("face", "blk"), [(i * n_blk + j, i_up * n_blk + j_up) for i, i_up in face_up for j, j_up in blk_up]
    )
    before = lax.ppermute(right, "blk", blk_up)
    from_low = lax.ppermute(high, "face", face_up)
    from_high = lax.ppermute(low, "face", [(j, i) for i, j in face_up])
    count = len(node_rows)
    hot, pick, ntemps, nday = call(
        lambda *refs: send_order_kernel(n_blk, paired, *refs),
        (
            jax.ShapeDtypeStruct(((count - 1) * LANES, sites), bf16),
            jax.ShapeDtypeStruct((2 * LANES, sites), bf16),
            f32((count + 1) * levels, LANES),
            f32((count + 1) * 8, LANES),
        ),
        [pltpu.VMEM((n_blk, -(-per_peer // LANES) * LANES), jnp.int32)],
        "send_order",
        den,
        temps,
        day,
        order,
    )
    acc, hiso, left = call(
        inner_columns_kernel,
        (f32(chans, sites), f32(chans, LANES), edge),
        [pltpu.VMEM((2 * chans, (count - 1) * LANES), bf16)],
        "inner_columns",
        iso,
        sums,
        den,
        ntemps,
        nday,
        hot,
    )
    slots = call(
        lambda *refs: edge_columns_kernel(n_blk, paired, *refs),
        [f32(1, send_rows + (carried if paired and k in carriers(n_blk) else 0), LANES) for k in range(n_blk)] + [edge] * (not paired),
        [],
        "edge_columns",
        iso,
        sums,
        den,
        left,
        acc,
        pick,
        ntemps,
        nday,
        hiso,
        corner,
        before,
        from_low,
        from_high,
    )
    got, edges = exchange(slots[0:n_blk], slots[n_blk:], paired)
    new = call(
        lambda *refs: advance_kernel(n_blk, paired, carried, *refs),
        f32(chans * size_x, size_y),
        [
            pltpu.VMEM((chans + 8, LANES), jnp.float32),
            pltpu.VMEM((chans + 8, LANES), jnp.float32),
            pltpu.VMEM((chans * size_x, size_y), jnp.float32),
            pltpu.SemaphoreType.DMA((3,)),
        ],
        "advance",
        iso,
        sums,
        den,
        corner,
        before,
        from_low,
        from_high,
        *edges,
        out_specs=pl.BlockSpec(memory_space=pltpu.HBM),
    )
    phys = call(
        lambda *refs: assemble_kernel(n_blk, paired, *refs),
        f32(chans, sites),
        ([pltpu.VMEM((n_blk, send_rows, LANES), jnp.float32)] if paired else [])
        + [pltpu.VMEM((chans, sites), jnp.float32), pltpu.SemaphoreType.DMA((sites // LANES,))],
        "assemble",
        *got,
        out_specs=pl.BlockSpec(memory_space=pltpu.HBM),
    )
    return (new.reshape(isotope_ratios.shape), phys.reshape(1, 3, levels, sites))


def solution(mesh):
    placed = (
        P(None, None, "face", "blk"),
        P(None, None, "face", "blk"),
        P("face", "blk"),
        P("face", None, "blk"),
        P("face", "blk"),
        P("face", "blk"),
    )
    return jax.shard_map(
        on_device,
        mesh=mesh,
        in_specs=placed,
        out_specs=(P(None, None, "face", "blk"), P("face", None, None, "blk")),
        check_vma=False,
    )
```

```python
import math

import jax
import jax.numpy as jnp
import numpy as np
from jax import lax
from jax.experimental import pallas as pl
from jax.experimental.pallas import tpu as pltpu
from jax.sharding import PartitionSpec as P

time_step = 0.006
absorb_coef = 0.02
heat_gain = 100.0
sat_base = 3.0
clausius = 0.07
ref_temp = 280.0
LANES = 128
PAD_ROWS = 8
SENT = (7, 4, 5, 1, 3, 6, 2)
AFTER = {6: (1,), 2: (7,)}


def gll_tables():
    inv_root = 1.0 / math.sqrt(5.0)
    gll_nodes = np.array([-1.0, -inv_root, inv_root, 1.0])
    legendre = (5.0 * gll_nodes**3 - 3.0 * gll_nodes) / 2.0
    deriv_matrix = np.zeros((4, 4))
    for row_index in range(4):
        for col_index in range(4):
            if row_index != col_index:
                deriv_matrix[row_index, col_index] = legendre[row_index] / (
                    legendre[col_index] * (gll_nodes[row_index] - gll_nodes[col_index])
                )
    deriv_matrix[0, 0] = -3.0
    deriv_matrix[3, 3] = 3.0
    weights = np.array([1.0, 5.0, 5.0, 1.0]) / 6.0
    return (deriv_matrix, weights)


def row_maps(size_x):
    shared, count = [], -1
    for n in range(size_x):
        if n == 0 or n % 4 != 0:
            count += 1
        shared.append(count)
    return shared, [n for n in range(size_x) if n % 4 != 3]


def second_dim_matrix(size_y):
    deriv, weight = gll_tables()
    w = np.diag(np.tile(weight, size_y // 4))
    d = np.kron(np.eye(size_y // 4), deriv)
    e = np.eye(size_y)
    for m in range(3, size_y - 1, 4):
        e[m, m + 1] = e[m + 1, m] = 1.0
    both = np.concatenate([-(e @ w @ d).T, -(e @ w).T], axis=0)
    hi = both.astype(jnp.bfloat16)
    lo = (both - hi.astype(np.float64)).astype(jnp.bfloat16)
    return np.concatenate([hi, lo], axis=1)


def split(x):
    hi = x.astype(jnp.bfloat16)
    return hi, (x - hi.astype(jnp.float32)).astype(jnp.bfloat16)


def dot(a, b):
    return jnp.dot(a, b, preferred_element_type=jnp.float32)


def lanes_of(rows):
    return lax.broadcasted_iota(jnp.int32, (rows, LANES), 1)


def put_split(hi_ref, lo_ref, at, a, b):
    size_y = a.shape[1]
    ahi, alo = split(a)
    bhi, blo = split(b)
    hi_ref[at, 0:size_y] = ahi
    hi_ref[at, size_y : 2 * size_y] = bhi
    lo_ref[at, 0:size_y] = alo
    lo_ref[at, size_y : 2 * size_y] = blo


def second_dim(hi, lo, mat):
    size_y = hi.shape[1] // 2
    first = dot(hi, mat)
    return first[:, 0:size_y] + (first[:, size_y:] + dot(lo, mat[:, 0:size_y]))


def fluxes(iso_ref, wind_ref, metric_ref, s, n, weight):
    pitch = metric_ref.shape[0] + PAD_ROWS
    part = wind_ref.shape[0] // 2
    levels = part // pitch
    jac = metric_ref[n : n + 1, :]
    q = iso_ref[pl.ds(s * part + n, levels, stride=pitch), :]
    fx = (jac * wind_ref[pl.ds(n, levels, stride=pitch), :]) * q
    if weight is None:
        return fx
    return fx, ((jac * weight) * wind_ref[pl.ds(part + n, levels, stride=pitch), :]) * q


def weighted_derivative(coefs, fx):
    total = None
    for coef, f in zip(coefs, fx):
        if coef != 0.0:
            total = float(coef) * f if total is None else total + float(coef) * f
    return total


def transport_kernel(
    iso_hbm,
    wind_hbm,
    metric_hbm,
    mat_hbm,
    temps_hbm,
    day_hbm,
    order_hbm,
    iso_ref,
    temps_ref,
    day_ref,
    order_ref,
    sums_ref,
    den_ref,
    low_ref,
    high_ref,
    right_ref,
    wind_ref,
    metric_ref,
    mat_ref,
    hi_ref,
    lo_ref,
    sems,
):
    size_x, size_y = metric_ref.shape
    part = wind_ref.shape[0] // 2
    pitch = size_x + PAD_ROWS
    levels = part // pitch
    chans = 3 * levels
    deriv, weight = gll_tables()
    shared, _ = row_maps(size_x)
    n_rows = shared[-1] + 1
    copies = [pltpu.make_async_copy(metric_hbm, metric_ref, sems.at[0])]
    wind_in, wind = (ref.reshape(2, levels, -1, size_y) for ref in (wind_hbm, wind_ref))
    iso_in, iso = (ref.reshape(3, levels, -1, size_y) for ref in (iso_hbm, iso_ref))
    rows = pl.ds(0, size_x)
    for k in range(2):
        copies.append(pltpu.make_async_copy(wind_in.at[k], wind.at[k, :, rows], sems.at[1 + k]))
    for s in range(3):
        copies.append(pltpu.make_async_copy(iso_in.at[s], iso.at[s, :, rows], sems.at[3 + s]))
    copies.append(pltpu.make_async_copy(mat_hbm, mat_ref, sems.at[6]))
    for k, (src, dst) in enumerate(((temps_hbm, temps_ref), (day_hbm, day_ref), (order_hbm, order_ref))):
        copies.append(pltpu.make_async_copy(src, dst, sems.at[7 + k]))
    for c in copies:
        c.start()

    copies[0].wait()
    lane = lanes_of(size_x)
    sub = lax.broadcasted_iota(jnp.int32, (size_x, LANES), 0)
    wl = jnp.where((lane % 4 == 0) | (lane % 4 == 3), float(weight[0]), float(weight[1]))
    ws = jnp.where((sub % 4 == 0) | (sub % 4 == 3), float(weight[0]), float(weight[1]))
    mass = (wl * ws) * metric_ref[...]
    after, before = pltpu.roll(mass, size_x - 1, 0), pltpu.roll(mass, 1, 0)
    mass = mass + jnp.where((sub % 4 == 3) & (sub != size_x - 1), after, 0.0) + jnp.where((sub % 4 == 0) & (sub != 0), before, 0.0)
    after, before = pltpu.roll(mass, size_y - 1, 1), pltpu.roll(mass, 1, 1)
    mass = mass + jnp.where((lane % 4 == 3) & (lane != size_y - 1), after, 0.0) + jnp.where((lane % 4 == 0) & (lane != 0), before, 0.0)
    den_ref[...] = mass

    for c in copies[1:3]:
        c.wait()
    for s in range(3):
        copies[3 + s].wait()
        held = None
        for e in range(size_x // 4):
            fx, fy = [], []
            for j in range(4):
                f, g = fluxes(iso_ref, wind_ref, metric_ref, s, 4 * e + j, float(weight[j]))
                fx.append(f)
                fy.append(g)
            for i in range(4):
                n = 4 * e + i
                a, b = fy[i], weighted_derivative(weight[i] * deriv[i], fx)
                if i == 0 and held is not None:
                    a, b = a + held[0], b + held[1]
                if i == 3 and n != size_x - 1:
                    held = (a, b)
                else:
                    put_split(hi_ref, lo_ref, pl.ds(shared[n] * chans + s * levels, levels), a, b)
    copies[6].wait()
    sums_ref[...] = second_dim(hi_ref[...], lo_ref[...], mat_ref[...])
    for ref, r, n in ((low_ref, 0, 0), (high_ref, n_rows - 1, size_x - 1)):
        ref[0:chans, :] = sums_ref[pl.ds(r * chans, chans), :]
        ref[chans : chans + 8, :] = jnp.broadcast_to(mass[n : n + 1, :], (8, LANES))
    gather_column(size_y - 1, sums_ref, mass, right_ref)
    for c in copies[7:]:
        c.wait()


def gather_column(lane, sums_ref, mass, out_ref):
    chans = out_ref.shape[0] - 8
    shared, _ = row_maps(mass.shape[0])
    wide, lane1 = lanes_of(chans), lanes_of(1)
    col = jnp.zeros((chans, LANES), jnp.float32)
    den = jnp.zeros((1, LANES), jnp.float32)
    for r in range(shared[-1] + 1):
        shift = (r - lane) % LANES
        here, n = sums_ref[pl.ds(r * chans, chans), :], shared.index(r)
        col = jnp.where(wide == r, pltpu.roll(here, shift, 1) if shift else here, col)
        den = jnp.where(lane1 == r, (pltpu.roll(mass, shift, 1) if shift else mass)[n : n + 1, :], den)
    out_ref[0:chans, :] = col
    out_ref[chans : chans + 8, :] = jnp.broadcast_to(den, (8, LANES))


def cumulative(x):
    rows = x.shape[0]
    sub = lax.broadcasted_iota(jnp.int32, x.shape, 0)
    step = 1
    while step < rows:
        x = x + jnp.where(sub >= step, pltpu.roll(x, step, 0), 0.0)
        step *= 2
    return x


def physics(tracers, temps, day):
    levels = temps.shape[0]
    vapour = tracers[0:levels]
    scaled = absorb_coef * vapour
    heating = heat_gain * scaled * jnp.exp(-cumulative(scaled))
    heated = temps + jnp.where(day == 1.0, heating, 0.0)
    saturation = sat_base * jnp.exp(clausius * (heated - ref_temp))
    remain = jnp.minimum(vapour, saturation)
    log_ratio = jnp.log(remain / vapour)
    inverse = 1.0 / heated
    alpha_heavy = jnp.exp(1137.0 * inverse * inverse - 0.4156 * inverse - 0.0020667)
    alpha_deut = jnp.exp(24844.0 * inverse * inverse - 76.248 * inverse + 0.052612)
    return jnp.concatenate(
        [
            remain,
            tracers[levels : 2 * levels] * jnp.exp(alpha_heavy * log_ratio),
            tracers[2 * levels :] * jnp.exp(alpha_deut * log_ratio),
        ],
        axis=0,
    )


def peer_of(slot, paired):
    return lax.axis_index("blk") ^ slot if paired else slot


def carriers(n_peers):
    return sorted({j ^ ((j - 1) % n_peers) for j in range(n_peers)})


def third(x):
    return lax.shift_right_logical(x * 43691, 17)


def spread_lanes(x):
    rows = x.shape[0]
    lane = lanes_of(rows)
    source = 3 * lax.shift_right_logical(lane, 2) + jnp.minimum(lane & 3, 2)
    padded = jnp.concatenate([x, jnp.zeros((rows, LANES - x.shape[1]), x.dtype)], axis=1)
    return jnp.take_along_axis(padded, source, axis=1)


def send_order_kernel(n_peers, paired, after_ref, order_ref, hot_ref, pick_ref, slots_ref):
    del after_ref
    sites = order_ref.shape[1]
    count = hot_ref.shape[0] // LANES + 1
    per_row = sites // count
    per_peer = sites // n_peers
    full, rest = per_peer // LANES, per_peer % LANES

    order = order_ref[...]
    for p in range(n_peers):
        mine = order[:, p * per_peer : (p + 1) * per_peer]
        pad = slots_ref.shape[1] - per_peer
        slots_ref[p : p + 1, :] = jnp.concatenate([mine, jnp.zeros((1, pad), jnp.int32)], axis=1) if pad else mine
    peers = [slots_ref[pl.ds(peer_of(k, paired), 1), :] for k in range(n_peers)]
    pieces = [mine[:, LANES * j : LANES * (j + 1)] for mine in peers for j in range(full)]
    if rest:
        pieces += [mine[:, LANES * full : per_peer] for mine in peers]
    order = jnp.concatenate(pieces, axis=1)
    row = third(lax.shift_right_logical(order, 5))
    within = order - per_row * row
    group = third(within)
    node = 4 * group + (within - 3 * group)
    main = jnp.where((row == 0) | (node == 0), -1, (row - 1) * LANES + node)
    first = jnp.where(row == 0, node, -1)
    side = jnp.where((row != 0) & (node == 0), row, -1)
    bf16 = jnp.bfloat16
    sub = lax.broadcasted_iota(jnp.int32, (LANES, LANES), 0).astype(bf16)

    def one_hot(index):
        index = jnp.broadcast_to(jnp.clip(index, -1, LANES).astype(jnp.float32), (16, LANES)).astype(bf16)
        index = jnp.concatenate([index] * (LANES // 16), axis=0)
        return jnp.where(sub == index, jnp.ones((), bf16), jnp.zeros((), bf16))

    for t in range(sites // LANES):
        at = slice(t * LANES, (t + 1) * LANES)
        here = main[:, at]
        for k in range(count - 1):
            hot_ref[k * LANES : (k + 1) * LANES, at] = one_hot(here - k * LANES)
        pick_ref[0:LANES, at] = one_hot(first[:, at])
        pick_ref[LANES : 2 * LANES, at] = one_hot(side[:, at])


def spread_columns(temps_ref, day_ref, ntemps_ref, nday_ref):
    levels, sites = temps_ref.shape
    count = ntemps_ref.shape[0] // levels - 1
    per_row = sites // count
    temps = temps_ref[...]
    day = jnp.broadcast_to(day_ref[...].astype(jnp.float32), (8, sites))
    lane1, wide_l = lanes_of(1), lanes_of(levels)
    unused = (lane1 & 3) == 3
    side_temps = jnp.full((levels, LANES), ref_temp, jnp.float32)
    side_day = jnp.zeros((8, LANES), jnp.float32)
    for k in range(count):
        t_here = jnp.where(unused, ref_temp, spread_lanes(temps[:, k * per_row : (k + 1) * per_row]))
        d_here = spread_lanes(day[:, k * per_row : (k + 1) * per_row])
        ntemps_ref[k * levels : (k + 1) * levels, :] = t_here
        nday_ref[8 * k : 8 * k + 8, :] = d_here
        if k:
            side_temps = jnp.where(wide_l == k, pltpu.roll(t_here, k, 1), side_temps)
            side_day = jnp.where(lanes_of(8) == k, pltpu.roll(d_here, k, 1), side_day)
    ntemps_ref[count * levels :, :] = side_temps
    nday_ref[8 * count :, :] = side_day


def inner_columns_kernel(iso_ref, sums_ref, den_ref, temps_ref, day_ref, hot_ref, acc_ref, hiso_ref, left_ref, ntemps_ref, nday_ref, lhs_ref):
    spread_columns(temps_ref, day_ref, ntemps_ref, nday_ref)
    size_x, size_y = den_ref.shape
    chans = acc_ref.shape[0]
    levels = chans // 3
    _, node_rows = row_maps(size_x)
    lane1 = lanes_of(1)
    own = ((lane1 & 3) == 3) | (lane1 == 0)
    wide = lanes_of(chans)
    hiso = jnp.full((chans, LANES), 3.0, jnp.float32)
    inv = 1.0 / den_ref[...]
    for k, n in enumerate(node_rows):
        if k == 0:
            continue
        iso = iso_ref[pl.ds(n, chans, stride=size_x + PAD_ROWS), :]
        hiso = jnp.where(wide == k, pltpu.roll(iso, k, 1), hiso)
        gain = jnp.where(own, 0.0, time_step * inv[n : n + 1, :])
        tracers = iso + gain * sums_ref[pl.ds(k * chans, chans), :]
        hi, lo = split(physics(tracers, ntemps_ref[k * levels : (k + 1) * levels, :], nday_ref[8 * k : 8 * k + 1, :]))
        lhs_ref[0:chans, (k - 1) * LANES : k * LANES] = hi
        lhs_ref[chans : 2 * chans, (k - 1) * LANES : k * LANES] = lo
    hiso_ref[...] = hiso
    gather_column(0, sums_ref, den_ref[...], left_ref)
    both = dot(lhs_ref[...], hot_ref[...])
    acc_ref[...] = both[0:chans] + both[chans:]


def edge_columns_kernel(
    n_peers, paired, iso_ref, sums_ref, den_ref, left_ref, acc_ref, pick_ref, ntemps_ref, nday_ref, hiso_ref, corner_ref, before_ref, low_ref, high_ref, *send_refs
):
    chans, sites = acc_ref.shape
    levels = chans // 3
    size_x = den_ref.shape[0]
    _, node_rows = row_maps(size_x)
    count = len(node_rows)
    per_peer = sites // n_peers
    full, rest = per_peer // LANES, per_peer % LANES
    wide, lane1 = lanes_of(chans), lanes_of(1)
    unused = (lane1 & 3) == 3

    last = row_maps(size_x)[0][-1]
    extra = before_ref[...] + pltpu.roll(corner_ref[...], LANES - last, 1)
    total = sums_ref[0:chans, :] + low_ref[0:chans, :] + jnp.where(wide == 0, extra[0:chans, :], 0.0)
    den = den_ref[0:1, :] + low_ref[chans : chans + 1, :] + jnp.where(lane1 == 0, extra[chans : chans + 1, :], 0.0)
    iso = iso_ref[pl.ds(0, chans, stride=size_x + PAD_ROWS), :]
    new_row = iso + jnp.where(unused, 0.0, time_step / den) * total
    phys_row = physics(new_row, ntemps_ref[0:levels, :], nday_ref[0:1, :])

    in_use = (lane1 > 0) & (lane1 < count)
    dcol = jnp.where(in_use, left_ref[chans : chans + 1, :] + before_ref[chans : chans + 1, :], 1.0)
    tcol = jnp.where(in_use, left_ref[0:chans, :] + before_ref[0:chans, :], 0.0)
    new_col = hiso_ref[...] + (time_step / dcol) * tcol
    phys_col = physics(new_col, ntemps_ref[count * levels :, :], nday_ref[8 * count : 8 * count + 1, :])

    rhi, rlo = split(phys_row)
    chi, clo = split(phys_col)
    lhs = jnp.concatenate([jnp.concatenate([rhi, chi], axis=1), jnp.concatenate([rlo, clo], axis=1)], axis=0)
    both = dot(lhs, pick_ref[...])
    out = acc_ref[...] + (both[0:chans] + both[chans:])
    for p in range(n_peers):
        for j in range(full):
            t = p * full + j
            send_refs[p][0, j * chans : (j + 1) * chans, :] = out[:, t * LANES : (t + 1) * LANES]
    if rest:
        begin = n_peers * full * LANES
        for t in range(n_peers * rest // LANES):
            block = out[:, begin + t * LANES : begin + (t + 1) * LANES]
            block = jnp.concatenate([block, jnp.zeros((LANES - chans, LANES), jnp.float32)], axis=0).T
            at = t * LANES
            while at < (t + 1) * LANES:
                p, i = at // rest, at % rest
                count = min(rest - i, (t + 1) * LANES - at)
                send_refs[p][0, full * chans + i : full * chans + i + count, :] = block[at - t * LANES : at - t * LANES + count, :]
                at += count


    lane, high = lanes_of(chans + 8), high_ref[...]
    edge = left_ref[...] + jnp.where(lane == 0, low_ref[...], 0.0) + jnp.where(lane == last, pltpu.roll(high, last, 1), 0.0)
    edge = jnp.where(lane == last + 1, pltpu.roll(high, last + 2, 1), edge)
    if not paired:
        send_refs[n_peers][...] = edge
    else:
        turned = jnp.concatenate([edge, jnp.zeros((LANES - edge.shape[0], LANES), jnp.float32)], axis=0).T
        for k in carriers(n_peers):
            rows = send_refs[k].shape[1] - send_refs[0].shape[1]
            send_refs[k][0, send_refs[0].shape[1] :, :] = turned[0:rows, :]


def advance_kernel(n_peers, paired, carried, iso_ref, sums_ref, den_ref, corner_ref, near_ref, low_ref, high_ref, *rest):
    *edge_refs, new_hbm, before_ref, after_ref, new_ref, sems = rest
    size_x = den_ref.shape[0]
    chans = low_ref.shape[0] - 8
    shared, _ = row_maps(size_x)
    last = shared[-1]
    lane1 = lanes_of(1)
    if paired:
        me = lax.axis_index("blk")
        turned = []
        for other in (lax.rem(me + 1, n_peers), lax.rem(me + n_peers - 1, n_peers)):
            mine = jnp.zeros((carried, LANES), jnp.float32)
            for k, ref in zip(carriers(n_peers), edge_refs):
                mine = jnp.where((me ^ other) == k, ref[0, ref.shape[1] - carried :, :], mine)
            turned.append(mine)
        pad = jnp.zeros((LANES - 2 * carried, LANES), jnp.float32)
        both = jnp.concatenate(turned + [pad], axis=0).T[0 : chans + 8, :]
        after_ref[...] = both
        beside = pltpu.roll(both, LANES - carried - 1, 1)
    else:
        after_ref[...] = edge_refs[0][...]
        beside = pltpu.roll(edge_refs[1][...], LANES - 1, 1)
    lane = lanes_of(chans + 8)
    near = near_ref[...] + jnp.where(lane == 0, pltpu.roll(corner_ref[...], LANES - last, 1), 0.0)
    before_ref[...] = near + jnp.where(lane == last, beside, 0.0)
    gains = []
    for n in range(size_x):
        den = den_ref[n : n + 1, :]
        for ref, at in ((low_ref, 0), (high_ref, size_x - 1)):
            if n == at:
                den = den + ref[chans : chans + 1, :]
        for ref, at in ((before_ref, 0), (after_ref, LANES - 1)):
            den = jnp.where(lane1 == at, den + ref[chans : chans + 1, shared[n] : shared[n] + 1], den)
        gains.append(time_step / den)
    levels = chans // 3
    wide = lanes_of(levels)
    copies = []
    for s in range(3):
        for n in range(size_x):
            r = shared[n]
            total = sums_ref[pl.ds(r * chans + s * levels, levels), :]
            at_s = pl.ds(s * levels, levels)
            for ref, at in ((low_ref, 0), (high_ref, size_x - 1)):
                if n == at:
                    total = total + ref[at_s, :]
            for ref, at in ((before_ref, 0), (after_ref, LANES - 1)):
                total = jnp.where(wide == at, total + ref[at_s, r : r + 1], total)
            here = pl.ds(s * levels * (size_x + PAD_ROWS) + n, levels, stride=size_x + PAD_ROWS)
            new_ref[here, :] = iso_ref[here, :] + gains[n] * total
        made, out = (ref.reshape(3, levels, -1, LANES) for ref in (new_ref, new_hbm))
        copies.append(pltpu.make_async_copy(made.at[s, :, pl.ds(0, size_x)], out.at[s], sems.at[s]))
        copies[-1].start()
    for c in copies:
        c.wait()


def assemble_kernel(n_peers, paired, *refs):
    if paired:
        *slot_refs, out_hbm, got_ref, out_ref, sems = refs
        for k, ref in enumerate(slot_refs):
            got_ref[pl.ds(peer_of(k, paired), 1), :, :] = ref[:, 0 : got_ref.shape[1], :]
    else:
        got_ref, out_hbm, out_ref, sems = refs
    chans, sites = out_ref.shape
    per_peer = sites // n_peers
    full, rest = per_peer // LANES, per_peer % LANES
    lane = lanes_of(chans)
    blocks = [None] * (sites // LANES)

    def place(block, value, low, high):
        old = blocks[block]
        blocks[block] = value if old is None else jnp.where((lane >= low) & (lane < high), value, old)

    for p in range(n_peers):
        for j in range(full):
            begin = p * per_peer + j * LANES
            shift = begin % LANES
            value = got_ref[p, j * chans : (j + 1) * chans, :]
            if shift:
                value = pltpu.roll(value, shift, 1)
            place(begin // LANES, value, shift, LANES)
            if shift:
                place(begin // LANES + 1, value, 0, shift)
    if rest:
        tails = [got_ref[p, full * chans : full * chans + rest, :] for p in range(n_peers)]
        tails = jnp.concatenate(tails, axis=0)
        for t in range(n_peers * rest // LANES):
            block = tails[t * LANES : (t + 1) * LANES, :].T[0:chans, :]
            at = t * LANES
            while at < (t + 1) * LANES:
                p, i = at // rest, at % rest
                count = min(rest - i, (t + 1) * LANES - at)
                column = p * per_peer + full * LANES + i
                place(column // LANES, block, column % LANES, column % LANES + count)
                at += count
    copies = []
    for t, block in enumerate(blocks):
        at = pl.ds(t * LANES, LANES)
        out_ref[:, at] = block
        copies.append(pltpu.make_async_copy(out_ref.at[:, at], out_hbm.at[:, at], sems.at[t]))
        copies[-1].start()
    for c in copies:
        c.wait()


def exchange(slots, edge, paired):
    n_peers = lax.axis_size("blk")
    if not paired:
        got = lax.all_to_all(jnp.concatenate(slots, axis=0), "blk", split_axis=0, concat_axis=0, tiled=True)
        up = [(j, (j + 1) % n_peers) for j in range(n_peers)]
        return [got], [lax.ppermute(edge[0], "blk", [(j, i) for i, j in up]), lax.ppermute(edge[0], "blk", up)]
    got = {0: slots[0]}
    for k in SENT:
        block = slots[k]
        for w in AFTER.get(k, ()):
            block, got[w] = lax.optimization_barrier((block, got[w]))
        got[k] = lax.ppermute(block, "blk", [(j, j ^ k) for j in range(n_peers)])
    got = [got[k] for k in range(n_peers)]
    return got, [got[k] for k in carriers(n_peers)]


def call(kernel, outs, scratch, name, *args, **more):
    return pl.pallas_call(
        kernel,
        out_shape=outs,
        **more,
        scratch_shapes=scratch,
        name=name,
        compiler_params=pltpu.CompilerParams(vmem_limit_bytes=40 * 1024 * 1024),
    )(*args)


def on_device(
    isotope_ratios,
    advecting_velocity,
    metric_scaling,
    thermal_state,
    outgoing_site_order,
    daytime_indicator,
):
    size_x, size_y = metric_scaling.shape
    levels = isotope_ratios.shape[1]
    chans = 3 * levels
    sites = outgoing_site_order.shape[1]
    n_face, n_blk = lax.axis_size("face"), lax.axis_size("blk")
    shared, node_rows = row_maps(size_x)
    n_rows = shared[-1] + 1
    per_peer = sites // n_blk
    paired = n_blk == 8
    carried = -(-(n_rows + 1) // 8) * 8
    send_rows = chans * (per_peer // LANES) + per_peer % LANES

    def f32(*shape):
        return jax.ShapeDtypeStruct(shape, jnp.float32)

    iso = isotope_ratios.reshape(chans * size_x, size_y)
    wind = advecting_velocity.reshape(2 * levels * size_x, size_y)
    matrix = jnp.asarray(second_dim_matrix(size_y))
    edge = f32(chans + 8, LANES)
    integers = jax.ShapeDtypeStruct((1, sites), jnp.int32)
    bf16 = jnp.bfloat16
    args = (iso, wind, metric_scaling, matrix, thermal_state[0], daytime_indicator, outgoing_site_order)
    iso, temps, day, order, sums, den, low, high, right = call(
        transport_kernel,
        (
            f32(chans * (size_x + PAD_ROWS), size_y),
            f32(levels, sites),
            integers,
            integers,
            f32(n_rows * chans, size_y),
            f32(size_x, size_y),
            *[edge] * 3,
        ),
        [
            pltpu.VMEM((2 * levels * (size_x + PAD_ROWS), size_y), jnp.float32),
            pltpu.VMEM((size_x, size_y), jnp.float32),
            pltpu.VMEM(matrix.shape, bf16),
        ]
        + [pltpu.VMEM((n_rows * chans, 2 * size_y), bf16)] * 2 + [pltpu.SemaphoreType.DMA((10,))],
        "transport",
        *(pltpu.with_memory_space_constraint(x, pltpu.HBM) for x in args),
        in_specs=[pl.BlockSpec(memory_space=pltpu.HBM)] * len(args),
    )
    face_up = [(i, (i + 1) % n_face) for i in range(n_face)]
    blk_up = [(i, (i + 1) % n_blk) for i in range(n_blk)]
    corner = lax.ppermute(
        right, ("face", "blk"), [(i * n_blk + j, i_up * n_blk + j_up) for i, i_up in face_up for j, j_up in blk_up]
    )
    before = lax.ppermute(right, "blk", blk_up)
    from_low = lax.ppermute(high, "face", face_up)
    from_high = lax.ppermute(low, "face", [(j, i) for i, j in face_up])
    count = len(node_rows)
    hot, pick = call(
        lambda *refs: send_order_kernel(n_blk, paired, *refs),
        (jax.ShapeDtypeStruct(((count - 1) * LANES, sites), bf16), jax.ShapeDtypeStruct((2 * LANES, sites), bf16)),
        [pltpu.VMEM((n_blk, -(-per_peer // LANES) * LANES), jnp.int32)],
        "send_order",
        den,
        order,
    )
    acc, hiso, left, ntemps, nday = call(
        inner_columns_kernel,
        (f32(chans, sites), f32(chans, LANES), edge, f32((count + 1) * levels, LANES), f32((count + 1) * 8, LANES)),
        [pltpu.VMEM((2 * chans, (count - 1) * LANES), bf16)],
        "inner_columns",
        iso,
        sums,
        den,
        temps,
        day,
        hot,
    )
    slots = call(
        lambda *refs: edge_columns_kernel(n_blk, paired, *refs),
        [f32(1, send_rows + (carried if paired and k in carriers(n_blk) else 0), LANES) for k in range(n_blk)] + [edge] * (not paired),
        [],
        "edge_columns",
        iso,
        sums,
        den,
        left,
        acc,
        pick,
        ntemps,
        nday,
        hiso,
        corner,
        before,
        from_low,
        from_high,
    )
    got, edges = exchange(slots[0:n_blk], slots[n_blk:], paired)
    new = call(
        lambda *refs: advance_kernel(n_blk, paired, carried, *refs),
        f32(chans * size_x, size_y),
        [
            pltpu.VMEM((chans + 8, LANES), jnp.float32),
            pltpu.VMEM((chans + 8, LANES), jnp.float32),
            pltpu.VMEM((chans * (size_x + PAD_ROWS), size_y), jnp.float32),
            pltpu.SemaphoreType.DMA((3,)),
        ],
        "advance",
        iso,
        sums,
        den,
        corner,
        before,
        from_low,
        from_high,
        *edges,
        out_specs=pl.BlockSpec(memory_space=pltpu.HBM),
    )
    phys = call(
        lambda *refs: assemble_kernel(n_blk, paired, *refs),
        f32(chans, sites),
        ([pltpu.VMEM((n_blk, send_rows, LANES), jnp.float32)] if paired else [])
        + [pltpu.VMEM((chans, sites), jnp.float32), pltpu.SemaphoreType.DMA((sites // LANES,))],
        "assemble",
        *got,
        out_specs=pl.BlockSpec(memory_space=pltpu.HBM),
    )
    return (new.reshape(isotope_ratios.shape), phys.reshape(1, 3, levels, sites))


def solution(mesh):
    placed = (
        P(None, None, "face", "blk"),
        P(None, None, "face", "blk"),
        P("face", "blk"),
        P("face", None, "blk"),
        P("face", "blk"),
        P("face", "blk"),
    )
    return jax.shard_map(
        on_device,
        mesh=mesh,
        in_specs=placed,
        out_specs=(P(None, None, "face", "blk"), P("face", None, None, "blk")),
        check_vma=False,
    )
```

```python
import math

import jax
import jax.numpy as jnp
import numpy as np
from jax import lax
from jax.experimental import pallas as pl
from jax.experimental.pallas import tpu as pltpu
from jax.sharding import PartitionSpec as P

time_step = 0.006
absorb_coef = 0.02
heat_gain = 100.0
sat_base = 3.0
clausius = 0.07
ref_temp = 280.0
LANES = 128
PAD_ROWS = 8
SENT = (7, 6, 5, 1, 3, 4, 2)
AFTER = {4: (1,), 2: (7,)}


def gll_tables():
    inv_root = 1.0 / math.sqrt(5.0)
    gll_nodes = np.array([-1.0, -inv_root, inv_root, 1.0])
    legendre = (5.0 * gll_nodes**3 - 3.0 * gll_nodes) / 2.0
    deriv_matrix = np.zeros((4, 4))
    for row_index in range(4):
        for col_index in range(4):
            if row_index != col_index:
                deriv_matrix[row_index, col_index] = legendre[row_index] / (
                    legendre[col_index] * (gll_nodes[row_index] - gll_nodes[col_index])
                )
    deriv_matrix[0, 0] = -3.0
    deriv_matrix[3, 3] = 3.0
    weights = np.array([1.0, 5.0, 5.0, 1.0]) / 6.0
    return (deriv_matrix, weights)


def row_maps(size_x):
    shared, count = [], -1
    for n in range(size_x):
        if n == 0 or n % 4 != 0:
            count += 1
        shared.append(count)
    return shared, [n for n in range(size_x) if n % 4 != 3]


def second_dim_matrix(size_y):
    deriv, weight = gll_tables()
    w = np.diag(np.tile(weight, size_y // 4))
    d = np.kron(np.eye(size_y // 4), deriv)
    e = np.eye(size_y)
    for m in range(3, size_y - 1, 4):
        e[m, m + 1] = e[m + 1, m] = 1.0
    both = np.concatenate([-(e @ w @ d).T, -(e @ w).T], axis=0)
    hi = both.astype(jnp.bfloat16)
    lo = (both - hi.astype(np.float64)).astype(jnp.bfloat16)
    return np.concatenate([hi, lo], axis=1)


def split(x):
    hi = x.astype(jnp.bfloat16)
    return hi, (x - hi.astype(jnp.float32)).astype(jnp.bfloat16)


def dot(a, b):
    return jnp.dot(a, b, preferred_element_type=jnp.float32)


def lanes_of(rows):
    return lax.broadcasted_iota(jnp.int32, (rows, LANES), 1)


def put_split(hi_ref, lo_ref, at, a, b):
    size_y = a.shape[1]
    ahi, alo = split(a)
    bhi, blo = split(b)
    hi_ref[at, 0:size_y] = ahi
    hi_ref[at, size_y : 2 * size_y] = bhi
    lo_ref[at, 0:size_y] = alo
    lo_ref[at, size_y : 2 * size_y] = blo


def second_dim(hi, lo, mat):
    size_y = hi.shape[1] // 2
    first = dot(hi, mat)
    return first[:, 0:size_y] + (first[:, size_y:] + dot(lo, mat[:, 0:size_y]))


def scale_winds(wind_ref, metric_ref, scaled_ref, weight):
    size_x = metric_ref.shape[0]
    pitch = size_x + PAD_ROWS
    part = wind_ref.shape[0] // 2
    levels = part // pitch
    for n in range(size_x):
        jac = metric_ref[n : n + 1, :]
        first, second = (pl.ds((2 * n + k) * levels, levels) for k in range(2))
        scaled_ref[first, :] = jac * wind_ref[pl.ds(n, levels, stride=pitch), :]
        scaled_ref[second, :] = (jac * float(weight[n % 4])) * wind_ref[pl.ds(part + n, levels, stride=pitch), :]


def fluxes(iso_ref, scaled_ref, size_x, s, n):
    levels = scaled_ref.shape[0] // (2 * size_x)
    pitch = size_x + PAD_ROWS
    q = iso_ref[pl.ds(s * levels * pitch + n, levels, stride=pitch), :]
    first, second = (scaled_ref[pl.ds((2 * n + k) * levels, levels), :] for k in range(2))
    return first * q, second * q


def weighted_derivative(coefs, fx):
    total = None
    for coef, f in zip(coefs, fx):
        if coef != 0.0:
            total = float(coef) * f if total is None else total + float(coef) * f
    return total


def transport_kernel(
    iso_hbm,
    wind_hbm,
    metric_hbm,
    mat_hbm,
    temps_hbm,
    day_hbm,
    order_hbm,
    iso_ref,
    temps_ref,
    day_ref,
    order_ref,
    sums_ref,
    den_ref,
    low_ref,
    high_ref,
    right_ref,
    wind_ref,
    metric_ref,
    mat_ref,
    scaled_ref,
    hi_ref,
    lo_ref,
    sems,
):
    size_x, size_y = metric_ref.shape
    part = wind_ref.shape[0] // 2
    pitch = size_x + PAD_ROWS
    levels = part // pitch
    chans = 3 * levels
    deriv, weight = gll_tables()
    shared, _ = row_maps(size_x)
    n_rows = shared[-1] + 1
    copies = [pltpu.make_async_copy(metric_hbm, metric_ref, sems.at[0])]
    wind_in, wind = (ref.reshape(2, levels, -1, size_y) for ref in (wind_hbm, wind_ref))
    iso_in, iso = (ref.reshape(3, levels, -1, size_y) for ref in (iso_hbm, iso_ref))
    rows = pl.ds(0, size_x)
    for k in range(2):
        copies.append(pltpu.make_async_copy(wind_in.at[k], wind.at[k, :, rows], sems.at[1 + k]))
    for s in range(3):
        copies.append(pltpu.make_async_copy(iso_in.at[s], iso.at[s, :, rows], sems.at[3 + s]))
    copies.append(pltpu.make_async_copy(mat_hbm, mat_ref, sems.at[6]))
    for k, (src, dst) in enumerate(((temps_hbm, temps_ref), (day_hbm, day_ref), (order_hbm, order_ref))):
        copies.append(pltpu.make_async_copy(src, dst, sems.at[7 + k]))
    for c in copies:
        c.start()

    copies[0].wait()
    lane = lanes_of(size_x)
    sub = lax.broadcasted_iota(jnp.int32, (size_x, LANES), 0)
    wl = jnp.where((lane % 4 == 0) | (lane % 4 == 3), float(weight[0]), float(weight[1]))
    ws = jnp.where((sub % 4 == 0) | (sub % 4 == 3), float(weight[0]), float(weight[1]))
    mass = (wl * ws) * metric_ref[...]
    after, before = pltpu.roll(mass, size_x - 1, 0), pltpu.roll(mass, 1, 0)
    mass = mass + jnp.where((sub % 4 == 3) & (sub != size_x - 1), after, 0.0) + jnp.where((sub % 4 == 0) & (sub != 0), before, 0.0)
    after, before = pltpu.roll(mass, size_y - 1, 1), pltpu.roll(mass, 1, 1)
    mass = mass + jnp.where((lane % 4 == 3) & (lane != size_y - 1), after, 0.0) + jnp.where((lane % 4 == 0) & (lane != 0), before, 0.0)
    den_ref[...] = mass

    for c in copies[1:3]:
        c.wait()
    scale_winds(wind_ref, metric_ref, scaled_ref, weight)
    for s in range(3):
        copies[3 + s].wait()
        held = None
        for e in range(size_x // 4):
            fx, fy = [], []
            for j in range(4):
                f, g = fluxes(iso_ref, scaled_ref, size_x, s, 4 * e + j)
                fx.append(f)
                fy.append(g)
            for i in range(4):
                n = 4 * e + i
                a, b = fy[i], weighted_derivative(weight[i] * deriv[i], fx)
                if i == 0 and held is not None:
                    a, b = a + held[0], b + held[1]
                if i == 3 and n != size_x - 1:
                    held = (a, b)
                else:
                    put_split(hi_ref, lo_ref, pl.ds(shared[n] * chans + s * levels, levels), a, b)
    copies[6].wait()
    sums_ref[...] = second_dim(hi_ref[...], lo_ref[...], mat_ref[...])
    for ref, r, n in ((low_ref, 0, 0), (high_ref, n_rows - 1, size_x - 1)):
        ref[0:chans, :] = sums_ref[pl.ds(r * chans, chans), :]
        ref[chans : chans + 8, :] = jnp.broadcast_to(mass[n : n + 1, :], (8, LANES))
    gather_column(size_y - 1, sums_ref, mass, right_ref)
    for c in copies[7:]:
        c.wait()


def gather_column(lane, sums_ref, mass, out_ref):
    chans = out_ref.shape[0] - 8
    shared, _ = row_maps(mass.shape[0])
    wide, lane1 = lanes_of(chans), lanes_of(1)
    col = jnp.zeros((chans, LANES), jnp.float32)
    den = jnp.zeros((1, LANES), jnp.float32)
    for r in range(shared[-1] + 1):
        shift = (r - lane) % LANES
        here, n = sums_ref[pl.ds(r * chans, chans), :], shared.index(r)
        col = jnp.where(wide == r, pltpu.roll(here, shift, 1) if shift else here, col)
        den = jnp.where(lane1 == r, (pltpu.roll(mass, shift, 1) if shift else mass)[n : n + 1, :], den)
    out_ref[0:chans, :] = col
    out_ref[chans : chans + 8, :] = jnp.broadcast_to(den, (8, LANES))


def cumulative(x):
    rows = x.shape[0]
    sub = lax.broadcasted_iota(jnp.int32, x.shape, 0)
    step = 1
    while step < rows:
        x = x + jnp.where(sub >= step, pltpu.roll(x, step, 0), 0.0)
        step *= 2
    return x


def physics(tracers, temps, day):
    levels = temps.shape[0]
    vapour = tracers[0:levels]
    scaled = absorb_coef * vapour
    heating = heat_gain * scaled * jnp.exp(-cumulative(scaled))
    heated = temps + jnp.where(day == 1.0, heating, 0.0)
    saturation = sat_base * jnp.exp(clausius * (heated - ref_temp))
    remain = jnp.minimum(vapour, saturation)
    log_ratio = jnp.log(remain / vapour)
    inverse = 1.0 / heated
    alpha_heavy = jnp.exp(1137.0 * inverse * inverse - 0.4156 * inverse - 0.0020667)
    alpha_deut = jnp.exp(24844.0 * inverse * inverse - 76.248 * inverse + 0.052612)
    return jnp.concatenate(
        [
            remain,
            tracers[levels : 2 * levels] * jnp.exp(alpha_heavy * log_ratio),
            tracers[2 * levels :] * jnp.exp(alpha_deut * log_ratio),
        ],
        axis=0,
    )


def peer_of(slot, paired):
    return lax.axis_index("blk") ^ slot if paired else slot


def carriers(n_peers):
    return sorted({j ^ ((j - 1) % n_peers) for j in range(n_peers)})


def third(x):
    return lax.shift_right_logical(x * 43691, 17)


def spread_lanes(x):
    rows = x.shape[0]
    lane = lanes_of(rows)
    source = 3 * lax.shift_right_logical(lane, 2) + jnp.minimum(lane & 3, 2)
    padded = jnp.concatenate([x, jnp.zeros((rows, LANES - x.shape[1]), x.dtype)], axis=1)
    return jnp.take_along_axis(padded, source, axis=1)


def send_order_kernel(n_peers, paired, after_ref, order_ref, hot_ref, pick_ref, slots_ref):
    del after_ref
    sites = order_ref.shape[1]
    count = hot_ref.shape[0] // LANES + 1
    per_row = sites // count
    per_peer = sites // n_peers
    full, rest = per_peer // LANES, per_peer % LANES

    order = order_ref[...]
    for p in range(n_peers):
        mine = order[:, p * per_peer : (p + 1) * per_peer]
        pad = slots_ref.shape[1] - per_peer
        slots_ref[p : p + 1, :] = jnp.concatenate([mine, jnp.zeros((1, pad), jnp.int32)], axis=1) if pad else mine
    peers = [slots_ref[pl.ds(peer_of(k, paired), 1), :] for k in range(n_peers)]
    pieces = [mine[:, LANES * j : LANES * (j + 1)] for mine in peers for j in range(full)]
    if rest:
        pieces += [mine[:, LANES * full : per_peer] for mine in peers]
    order = jnp.concatenate(pieces, axis=1)
    row = third(lax.shift_right_logical(order, 5))
    within = order - per_row * row
    group = third(within)
    node = 4 * group + (within - 3 * group)
    main = jnp.where((row == 0) | (node == 0), -1, (row - 1) * LANES + node)
    first = jnp.where(row == 0, node, -1)
    side = jnp.where((row != 0) & (node == 0), row, -1)
    bf16 = jnp.bfloat16
    sub = lax.broadcasted_iota(jnp.int32, (LANES, LANES), 0).astype(bf16)

    def one_hot(index):
        index = jnp.broadcast_to(jnp.clip(index, -1, LANES).astype(jnp.float32), (16, LANES)).astype(bf16)
        index = jnp.concatenate([index] * (LANES // 16), axis=0)
        return jnp.where(sub == index, jnp.ones((), bf16), jnp.zeros((), bf16))

    for t in range(sites // LANES):
        at = slice(t * LANES, (t + 1) * LANES)
        here = main[:, at]
        for k in range(count - 1):
            hot_ref[k * LANES : (k + 1) * LANES, at] = one_hot(here - k * LANES)
        pick_ref[0:LANES, at] = one_hot(first[:, at])
        pick_ref[LANES : 2 * LANES, at] = one_hot(side[:, at])


def spread_columns(temps_ref, day_ref, ntemps_ref, nday_ref):
    levels, sites = temps_ref.shape
    count = ntemps_ref.shape[0] // levels - 1
    per_row = sites // count
    temps = temps_ref[...]
    day = jnp.broadcast_to(day_ref[...].astype(jnp.float32), (8, sites))
    lane1, wide_l = lanes_of(1), lanes_of(levels)
    unused = (lane1 & 3) == 3
    side_temps = jnp.full((levels, LANES), ref_temp, jnp.float32)
    side_day = jnp.zeros((8, LANES), jnp.float32)
    for k in range(count):
        t_here = jnp.where(unused, ref_temp, spread_lanes(temps[:, k * per_row : (k + 1) * per_row]))
        d_here = spread_lanes(day[:, k * per_row : (k + 1) * per_row])
        ntemps_ref[k * levels : (k + 1) * levels, :] = t_here
        nday_ref[8 * k : 8 * k + 8, :] = d_here
        if k:
            side_temps = jnp.where(wide_l == k, pltpu.roll(t_here, k, 1), side_temps)
            side_day = jnp.where(lanes_of(8) == k, pltpu.roll(d_here, k, 1), side_day)
    ntemps_ref[count * levels :, :] = side_temps
    nday_ref[8 * count :, :] = side_day


def inner_columns_kernel(iso_ref, sums_ref, den_ref, temps_ref, day_ref, hot_ref, acc_ref, hiso_ref, left_ref, ntemps_ref, nday_ref, lhs_ref):
    spread_columns(temps_ref, day_ref, ntemps_ref, nday_ref)
    size_x, size_y = den_ref.shape
    chans = acc_ref.shape[0]
    levels = chans // 3
    _, node_rows = row_maps(size_x)
    lane1 = lanes_of(1)
    own = ((lane1 & 3) == 3) | (lane1 == 0)
    wide = lanes_of(chans)
    hiso = jnp.full((chans, LANES), 3.0, jnp.float32)
    inv = 1.0 / den_ref[...]
    for k, n in enumerate(node_rows):
        if k == 0:
            continue
        iso = iso_ref[pl.ds(n, chans, stride=size_x + PAD_ROWS), :]
        hiso = jnp.where(wide == k, pltpu.roll(iso, k, 1), hiso)
        gain = jnp.where(own, 0.0, time_step * inv[n : n + 1, :])
        tracers = iso + gain * sums_ref[pl.ds(k * chans, chans), :]
        hi, lo = split(physics(tracers, ntemps_ref[k * levels : (k + 1) * levels, :], nday_ref[8 * k : 8 * k + 1, :]))
        lhs_ref[0:chans, (k - 1) * LANES : k * LANES] = hi
        lhs_ref[chans : 2 * chans, (k - 1) * LANES : k * LANES] = lo
    hiso_ref[...] = hiso
    gather_column(0, sums_ref, den_ref[...], left_ref)
    both = dot(lhs_ref[...], hot_ref[...])
    acc_ref[...] = both[0:chans] + both[chans:]


def edge_columns_kernel(
    n_peers, paired, iso_ref, sums_ref, den_ref, left_ref, acc_ref, pick_ref, ntemps_ref, nday_ref, hiso_ref, corner_ref, before_ref, low_ref, high_ref, *send_refs
):
    chans, sites = acc_ref.shape
    levels = chans // 3
    size_x = den_ref.shape[0]
    _, node_rows = row_maps(size_x)
    count = len(node_rows)
    per_peer = sites // n_peers
    full, rest = per_peer // LANES, per_peer % LANES
    wide, lane1 = lanes_of(chans), lanes_of(1)
    unused = (lane1 & 3) == 3

    last = row_maps(size_x)[0][-1]
    extra = before_ref[...] + pltpu.roll(corner_ref[...], LANES - last, 1)
    total = sums_ref[0:chans, :] + low_ref[0:chans, :] + jnp.where(wide == 0, extra[0:chans, :], 0.0)
    den = den_ref[0:1, :] + low_ref[chans : chans + 1, :] + jnp.where(lane1 == 0, extra[chans : chans + 1, :], 0.0)
    iso = iso_ref[pl.ds(0, chans, stride=size_x + PAD_ROWS), :]
    new_row = iso + jnp.where(unused, 0.0, time_step / den) * total
    phys_row = physics(new_row, ntemps_ref[0:levels, :], nday_ref[0:1, :])

    in_use = (lane1 > 0) & (lane1 < count)
    dcol = jnp.where(in_use, left_ref[chans : chans + 1, :] + before_ref[chans : chans + 1, :], 1.0)
    tcol = jnp.where(in_use, left_ref[0:chans, :] + before_ref[0:chans, :], 0.0)
    new_col = hiso_ref[...] + (time_step / dcol) * tcol
    phys_col = physics(new_col, ntemps_ref[count * levels :, :], nday_ref[8 * count : 8 * count + 1, :])

    rhi, rlo = split(phys_row)
    chi, clo = split(phys_col)
    lhs = jnp.concatenate([jnp.concatenate([rhi, chi], axis=1), jnp.concatenate([rlo, clo], axis=1)], axis=0)
    both = dot(lhs, pick_ref[...])
    out = acc_ref[...] + (both[0:chans] + both[chans:])
    for p in range(n_peers):
        for j in range(full):
            t = p * full + j
            send_refs[p][0, j * chans : (j + 1) * chans, :] = out[:, t * LANES : (t + 1) * LANES]
    if rest:
        begin = n_peers * full * LANES
        for t in range(n_peers * rest // LANES):
            block = out[:, begin + t * LANES : begin + (t + 1) * LANES]
            block = jnp.concatenate([block, jnp.zeros((LANES - chans, LANES), jnp.float32)], axis=0).T
            at = t * LANES
            while at < (t + 1) * LANES:
                p, i = at // rest, at % rest
                count = min(rest - i, (t + 1) * LANES - at)
                send_refs[p][0, full * chans + i : full * chans + i + count, :] = block[at - t * LANES : at - t * LANES + count, :]
                at += count


    lane, high = lanes_of(chans + 8), high_ref[...]
    edge = left_ref[...] + jnp.where(lane == 0, low_ref[...], 0.0) + jnp.where(lane == last, pltpu.roll(high, last, 1), 0.0)
    edge = jnp.where(lane == last + 1, pltpu.roll(high, last + 2, 1), edge)
    if not paired:
        send_refs[n_peers][...] = edge
    else:
        turned = jnp.concatenate([edge, jnp.zeros((LANES - edge.shape[0], LANES), jnp.float32)], axis=0).T
        for k in carriers(n_peers):
            rows = send_refs[k].shape[1] - send_refs[0].shape[1]
            send_refs[k][0, send_refs[0].shape[1] :, :] = turned[0:rows, :]


def advance_kernel(n_peers, paired, carried, iso_ref, sums_ref, den_ref, corner_ref, near_ref, low_ref, high_ref, *rest):
    *edge_refs, new_hbm, before_ref, after_ref, new_ref, sems = rest
    size_x = den_ref.shape[0]
    chans = low_ref.shape[0] - 8
    shared, _ = row_maps(size_x)
    last = shared[-1]
    lane1 = lanes_of(1)
    if paired:
        me = lax.axis_index("blk")
        turned = []
        for other in (lax.rem(me + 1, n_peers), lax.rem(me + n_peers - 1, n_peers)):
            mine = jnp.zeros((carried, LANES), jnp.float32)
            for k, ref in zip(carriers(n_peers), edge_refs):
                mine = jnp.where((me ^ other) == k, ref[0, ref.shape[1] - carried :, :], mine)
            turned.append(mine)
        pad = jnp.zeros((LANES - 2 * carried, LANES), jnp.float32)
        both = jnp.concatenate(turned + [pad], axis=0).T[0 : chans + 8, :]
        after_ref[...] = both
        beside = pltpu.roll(both, LANES - carried - 1, 1)
    else:
        after_ref[...] = edge_refs[0][...]
        beside = pltpu.roll(edge_refs[1][...], LANES - 1, 1)
    lane = lanes_of(chans + 8)
    near = near_ref[...] + jnp.where(lane == 0, pltpu.roll(corner_ref[...], LANES - last, 1), 0.0)
    before_ref[...] = near + jnp.where(lane == last, beside, 0.0)
    gains = []
    for n in range(size_x):
        den = den_ref[n : n + 1, :]
        for ref, at in ((low_ref, 0), (high_ref, size_x - 1)):
            if n == at:
                den = den + ref[chans : chans + 1, :]
        for ref, at in ((before_ref, 0), (after_ref, LANES - 1)):
            den = jnp.where(lane1 == at, den + ref[chans : chans + 1, shared[n] : shared[n] + 1], den)
        gains.append(time_step / den)
    levels = chans // 3
    wide = lanes_of(levels)
    copies = []
    for s in range(3):
        for n in range(size_x):
            r = shared[n]
            total = sums_ref[pl.ds(r * chans + s * levels, levels), :]
            at_s = pl.ds(s * levels, levels)
            for ref, at in ((low_ref, 0), (high_ref, size_x - 1)):
                if n == at:
                    total = total + ref[at_s, :]
            for ref, at in ((before_ref, 0), (after_ref, LANES - 1)):
                total = jnp.where(wide == at, total + ref[at_s, r : r + 1], total)
            here = pl.ds(s * levels * (size_x + PAD_ROWS) + n, levels, stride=size_x + PAD_ROWS)
            new_ref[here, :] = iso_ref[here, :] + gains[n] * total
        made, out = (ref.reshape(3, levels, -1, LANES) for ref in (new_ref, new_hbm))
        copies.append(pltpu.make_async_copy(made.at[s, :, pl.ds(0, size_x)], out.at[s], sems.at[s]))
        copies[-1].start()
    for c in copies:
        c.wait()


def assemble_kernel(n_peers, paired, *refs):
    if paired:
        *slot_refs, out_hbm, got_ref, out_ref, sems = refs
        for k, ref in enumerate(slot_refs):
            got_ref[pl.ds(peer_of(k, paired), 1), :, :] = ref[:, 0 : got_ref.shape[1], :]
    else:
        got_ref, out_hbm, out_ref, sems = refs
    chans, sites = out_ref.shape
    per_peer = sites // n_peers
    full, rest = per_peer // LANES, per_peer % LANES
    lane = lanes_of(chans)
    blocks = [None] * (sites // LANES)

    def place(block, value, low, high):
        old = blocks[block]
        blocks[block] = value if old is None else jnp.where((lane >= low) & (lane < high), value, old)

    for p in range(n_peers):
        for j in range(full):
            begin = p * per_peer + j * LANES
            shift = begin % LANES
            value = got_ref[p, j * chans : (j + 1) * chans, :]
            if shift:
                value = pltpu.roll(value, shift, 1)
            place(begin // LANES, value, shift, LANES)
            if shift:
                place(begin // LANES + 1, value, 0, shift)
    if rest:
        tails = [got_ref[p, full * chans : full * chans + rest, :] for p in range(n_peers)]
        tails = jnp.concatenate(tails, axis=0)
        for t in range(n_peers * rest // LANES):
            block = tails[t * LANES : (t + 1) * LANES, :].T[0:chans, :]
            at = t * LANES
            while at < (t + 1) * LANES:
                p, i = at // rest, at % rest
                count = min(rest - i, (t + 1) * LANES - at)
                column = p * per_peer + full * LANES + i
                place(column // LANES, block, column % LANES, column % LANES + count)
                at += count
    copies = []
    for t, block in enumerate(blocks):
        at = pl.ds(t * LANES, LANES)
        out_ref[:, at] = block
        copies.append(pltpu.make_async_copy(out_ref.at[:, at], out_hbm.at[:, at], sems.at[t]))
        copies[-1].start()
    for c in copies:
        c.wait()


def exchange(slots, edge, paired):
    n_peers = lax.axis_size("blk")
    if not paired:
        got = lax.all_to_all(jnp.concatenate(slots, axis=0), "blk", split_axis=0, concat_axis=0, tiled=True)
        up = [(j, (j + 1) % n_peers) for j in range(n_peers)]
        return [got], [lax.ppermute(edge[0], "blk", [(j, i) for i, j in up]), lax.ppermute(edge[0], "blk", up)]
    got = {0: slots[0]}
    for k in SENT:
        block = slots[k]
        for w in AFTER.get(k, ()):
            block, got[w] = lax.optimization_barrier((block, got[w]))
        got[k] = lax.ppermute(block, "blk", [(j, j ^ k) for j in range(n_peers)])
    got = [got[k] for k in range(n_peers)]
    return got, [got[k] for k in carriers(n_peers)]


def call(kernel, outs, scratch, name, *args, **more):
    return pl.pallas_call(
        kernel,
        out_shape=outs,
        **more,
        scratch_shapes=scratch,
        name=name,
        compiler_params=pltpu.CompilerParams(vmem_limit_bytes=40 * 1024 * 1024),
    )(*args)


def on_device(
    isotope_ratios,
    advecting_velocity,
    metric_scaling,
    thermal_state,
    outgoing_site_order,
    daytime_indicator,
):
    size_x, size_y = metric_scaling.shape
    levels = isotope_ratios.shape[1]
    chans = 3 * levels
    sites = outgoing_site_order.shape[1]
    n_face, n_blk = lax.axis_size("face"), lax.axis_size("blk")
    shared, node_rows = row_maps(size_x)
    n_rows = shared[-1] + 1
    per_peer = sites // n_blk
    paired = n_blk == 8
    carried = -(-(n_rows + 1) // 8) * 8
    send_rows = chans * (per_peer // LANES) + per_peer % LANES

    def f32(*shape):
        return jax.ShapeDtypeStruct(shape, jnp.float32)

    iso = isotope_ratios.reshape(chans * size_x, size_y)
    wind = advecting_velocity.reshape(2 * levels * size_x, size_y)
    matrix = jnp.asarray(second_dim_matrix(size_y))
    edge = f32(chans + 8, LANES)
    integers = jax.ShapeDtypeStruct((1, sites), jnp.int32)
    bf16 = jnp.bfloat16
    args = (iso, wind, metric_scaling, matrix, thermal_state[0], daytime_indicator, outgoing_site_order)
    iso, temps, day, order, sums, den, low, high, right = call(
        transport_kernel,
        (
            f32(chans * (size_x + PAD_ROWS), size_y),
            f32(levels, sites),
            integers,
            integers,
            f32(n_rows * chans, size_y),
            f32(size_x, size_y),
            *[edge] * 3,
        ),
        [
            pltpu.VMEM((2 * levels * (size_x + PAD_ROWS), size_y), jnp.float32),
            pltpu.VMEM((size_x, size_y), jnp.float32),
            pltpu.VMEM(matrix.shape, bf16),
            pltpu.VMEM((2 * levels * size_x, size_y), jnp.float32),
        ]
        + [pltpu.VMEM((n_rows * chans, 2 * size_y), bf16)] * 2 + [pltpu.SemaphoreType.DMA((10,))],
        "transport",
        *(pltpu.with_memory_space_constraint(x, pltpu.HBM) for x in args),
        in_specs=[pl.BlockSpec(memory_space=pltpu.HBM)] * len(args),
    )
    face_up = [(i, (i + 1) % n_face) for i in range(n_face)]
    blk_up = [(i, (i + 1) % n_blk) for i in range(n_blk)]
    corner = lax.ppermute(
        right, ("face", "blk"), [(i * n_blk + j, i_up * n_blk + j_up) for i, i_up in face_up for j, j_up in blk_up]
    )
    before = lax.ppermute(right, "blk", blk_up)
    from_low = lax.ppermute(high, "face", face_up)
    from_high = lax.ppermute(low, "face", [(j, i) for i, j in face_up])
    count = len(node_rows)
    hot, pick = call(
        lambda *refs: send_order_kernel(n_blk, paired, *refs),
        (jax.ShapeDtypeStruct(((count - 1) * LANES, sites), bf16), jax.ShapeDtypeStruct((2 * LANES, sites), bf16)),
        [pltpu.VMEM((n_blk, -(-per_peer // LANES) * LANES), jnp.int32)],
        "send_order",
        den,
        order,
    )
    acc, hiso, left, ntemps, nday = call(
        inner_columns_kernel,
        (f32(chans, sites), f32(chans, LANES), edge, f32((count + 1) * levels, LANES), f32((count + 1) * 8, LANES)),
        [pltpu.VMEM((2 * chans, (count - 1) * LANES), bf16)],
        "inner_columns",
        iso,
        sums,
        den,
        temps,
        day,
        hot,
    )
    slots = call(
        lambda *refs: edge_columns_kernel(n_blk, paired, *refs),
        [f32(1, send_rows + (carried if paired and k in carriers(n_blk) else 0), LANES) for k in range(n_blk)] + [edge] * (not paired),
        [],
        "edge_columns",
        iso,
        sums,
        den,
        left,
        acc,
        pick,
        ntemps,
        nday,
        hiso,
        corner,
        before,
        from_low,
        from_high,
    )
    got, edges = exchange(slots[0:n_blk], slots[n_blk:], paired)
    new = call(
        lambda *refs: advance_kernel(n_blk, paired, carried, *refs),
        f32(chans * size_x, size_y),
        [
            pltpu.VMEM((chans + 8, LANES), jnp.float32),
            pltpu.VMEM((chans + 8, LANES), jnp.float32),
            pltpu.VMEM((chans * (size_x + PAD_ROWS), size_y), jnp.float32),
            pltpu.SemaphoreType.DMA((3,)),
        ],
        "advance",
        iso,
        sums,
        den,
        corner,
        before,
        from_low,
        from_high,
        *edges,
        out_specs=pl.BlockSpec(memory_space=pltpu.HBM),
    )
    phys = call(
        lambda *refs: assemble_kernel(n_blk, paired, *refs),
        f32(chans, sites),
        ([pltpu.VMEM((n_blk, send_rows, LANES), jnp.float32)] if paired else [])
        + [pltpu.VMEM((chans, sites), jnp.float32), pltpu.SemaphoreType.DMA((sites // LANES,))],
        "assemble",
        *got,
        out_specs=pl.BlockSpec(memory_space=pltpu.HBM),
    )
    return (new.reshape(isotope_ratios.shape), phys.reshape(1, 3, levels, sites))


def solution(mesh):
    placed = (
        P(None, None, "face", "blk"),
        P(None, None, "face", "blk"),
        P("face", "blk"),
        P("face", None, "blk"),
        P("face", "blk"),
        P("face", "blk"),
    )
    return jax.shard_map(
        on_device,
        mesh=mesh,
        in_specs=placed,
        out_specs=(P(None, None, "face", "blk"), P("face", None, None, "blk")),
        check_vma=False,
    )
```

```python
import math

import jax
import jax.numpy as jnp
import numpy as np
from jax import lax
from jax.experimental import pallas as pl
from jax.experimental.pallas import tpu as pltpu
from jax.sharding import PartitionSpec as P

time_step = 0.006
absorb_coef = 0.02
heat_gain = 100.0
sat_base = 3.0
clausius = 0.07
ref_temp = 280.0
LANES = 128
PAD_ROWS = 8
SENT = (7, 6, 5, 1, 3, 4, 2)
AFTER = {4: (1,), 2: (5,)}


def gll_tables():
    inv_root = 1.0 / math.sqrt(5.0)
    gll_nodes = np.array([-1.0, -inv_root, inv_root, 1.0])
    legendre = (5.0 * gll_nodes**3 - 3.0 * gll_nodes) / 2.0
    deriv_matrix = np.zeros((4, 4))
    for row_index in range(4):
        for col_index in range(4):
            if row_index != col_index:
                deriv_matrix[row_index, col_index] = legendre[row_index] / (
                    legendre[col_index] * (gll_nodes[row_index] - gll_nodes[col_index])
                )
    deriv_matrix[0, 0] = -3.0
    deriv_matrix[3, 3] = 3.0
    weights = np.array([1.0, 5.0, 5.0, 1.0]) / 6.0
    return (deriv_matrix, weights)


def row_maps(size_x):
    shared, count = [], -1
    for n in range(size_x):
        if n == 0 or n % 4 != 0:
            count += 1
        shared.append(count)
    return shared, [n for n in range(size_x) if n % 4 != 3]


def second_dim_matrix(size_y):
    deriv, weight = gll_tables()
    w = np.diag(np.tile(weight, size_y // 4))
    d = np.kron(np.eye(size_y // 4), deriv)
    e = np.eye(size_y)
    for m in range(3, size_y - 1, 4):
        e[m, m + 1] = e[m + 1, m] = 1.0
    both = np.concatenate([-(e @ w @ d).T, -(e @ w).T], axis=0)
    hi = both.astype(jnp.bfloat16)
    lo = (both - hi.astype(np.float64)).astype(jnp.bfloat16)
    return np.concatenate([hi, lo], axis=1)


def split(x):
    hi = x.astype(jnp.bfloat16)
    return hi, (x - hi.astype(jnp.float32)).astype(jnp.bfloat16)


def dot(a, b):
    return jnp.dot(a, b, preferred_element_type=jnp.float32)


def lanes_of(rows):
    return lax.broadcasted_iota(jnp.int32, (rows, LANES), 1)


def put_split(hi_ref, lo_ref, at, a, b):
    size_y = a.shape[1]
    ahi, alo = split(a)
    bhi, blo = split(b)
    hi_ref[at, 0:size_y] = ahi
    hi_ref[at, size_y : 2 * size_y] = bhi
    lo_ref[at, 0:size_y] = alo
    lo_ref[at, size_y : 2 * size_y] = blo


def second_dim(hi, lo, mat):
    size_y = hi.shape[1] // 2
    first = dot(hi, mat)
    return first[:, 0:size_y] + (first[:, size_y:] + dot(lo, mat[:, 0:size_y]))


def scale_winds(wind_ref, metric_ref, scaled_ref, weight):
    size_x = metric_ref.shape[0]
    pitch = size_x + PAD_ROWS
    part = wind_ref.shape[0] // 2
    levels = part // pitch
    for n in range(size_x):
        jac = metric_ref[n : n + 1, :]
        first, second = (pl.ds((2 * n + k) * levels, levels) for k in range(2))
        scaled_ref[first, :] = jac * wind_ref[pl.ds(n, levels, stride=pitch), :]
        scaled_ref[second, :] = (jac * float(weight[n % 4])) * wind_ref[pl.ds(part + n, levels, stride=pitch), :]


def fluxes(iso_ref, scaled_ref, size_x, s, n):
    levels = scaled_ref.shape[0] // (2 * size_x)
    pitch = size_x + PAD_ROWS
    q = iso_ref[pl.ds(s * levels * pitch + n, levels, stride=pitch), :]
    first, second = (scaled_ref[pl.ds((2 * n + k) * levels, levels), :] for k in range(2))
    return first * q, second * q


def weighted_derivative(coefs, fx):
    total = None
    for coef, f in zip(coefs, fx):
        if coef != 0.0:
            total = float(coef) * f if total is None else total + float(coef) * f
    return total


def transport_kernel(
    iso_hbm,
    wind_hbm,
    metric_hbm,
    mat_hbm,
    temps_hbm,
    day_hbm,
    order_hbm,
    iso_ref,
    temps_ref,
    day_ref,
    order_ref,
    sums_ref,
    den_ref,
    low_ref,
    high_ref,
    right_ref,
    wind_ref,
    metric_ref,
    mat_ref,
    scaled_ref,
    hi_ref,
    lo_ref,
    sems,
):
    size_x, size_y = metric_ref.shape
    part = wind_ref.shape[0] // 2
    pitch = size_x + PAD_ROWS
    levels = part // pitch
    chans = 3 * levels
    deriv, weight = gll_tables()
    shared, _ = row_maps(size_x)
    n_rows = shared[-1] + 1
    copies = [pltpu.make_async_copy(metric_hbm, metric_ref, sems.at[0])]
    wind_in, wind = (ref.reshape(2, levels, -1, size_y) for ref in (wind_hbm, wind_ref))
    iso_in, iso = (ref.reshape(3, levels, -1, size_y) for ref in (iso_hbm, iso_ref))
    rows = pl.ds(0, size_x)
    for k in range(2):
        copies.append(pltpu.make_async_copy(wind_in.at[k], wind.at[k, :, rows], sems.at[1 + k]))
    for s in range(3):
        copies.append(pltpu.make_async_copy(iso_in.at[s], iso.at[s, :, rows], sems.at[3 + s]))
    copies.append(pltpu.make_async_copy(mat_hbm, mat_ref, sems.at[6]))
    for k, (src, dst) in enumerate(((temps_hbm, temps_ref), (day_hbm, day_ref), (order_hbm, order_ref))):
        copies.append(pltpu.make_async_copy(src, dst, sems.at[7 + k]))
    for c in copies:
        c.start()

    copies[0].wait()
    lane = lanes_of(size_x)
    sub = lax.broadcasted_iota(jnp.int32, (size_x, LANES), 0)
    wl = jnp.where((lane % 4 == 0) | (lane % 4 == 3), float(weight[0]), float(weight[1]))
    ws = jnp.where((sub % 4 == 0) | (sub % 4 == 3), float(weight[0]), float(weight[1]))
    mass = (wl * ws) * metric_ref[...]
    after, before = pltpu.roll(mass, size_x - 1, 0), pltpu.roll(mass, 1, 0)
    mass = mass + jnp.where((sub % 4 == 3) & (sub != size_x - 1), after, 0.0) + jnp.where((sub % 4 == 0) & (sub != 0), before, 0.0)
    after, before = pltpu.roll(mass, size_y - 1, 1), pltpu.roll(mass, 1, 1)
    mass = mass + jnp.where((lane % 4 == 3) & (lane != size_y - 1), after, 0.0) + jnp.where((lane % 4 == 0) & (lane != 0), before, 0.0)
    den_ref[...] = mass

    for c in copies[1:3]:
        c.wait()
    scale_winds(wind_ref, metric_ref, scaled_ref, weight)
    for s in range(3):
        copies[3 + s].wait()
        held = None
        for e in range(size_x // 4):
            fx, fy = [], []
            for j in range(4):
                f, g = fluxes(iso_ref, scaled_ref, size_x, s, 4 * e + j)
                fx.append(f)
                fy.append(g)
            for i in range(4):
                n = 4 * e + i
                a, b = fy[i], weighted_derivative(weight[i] * deriv[i], fx)
                if i == 0 and held is not None:
                    a, b = a + held[0], b + held[1]
                if i == 3 and n != size_x - 1:
                    held = (a, b)
                else:
                    put_split(hi_ref, lo_ref, pl.ds(shared[n] * chans + s * levels, levels), a, b)
    copies[6].wait()
    sums_ref[...] = second_dim(hi_ref[...], lo_ref[...], mat_ref[...])
    for ref, r, n in ((low_ref, 0, 0), (high_ref, n_rows - 1, size_x - 1)):
        ref[0:chans, :] = sums_ref[pl.ds(r * chans, chans), :]
        ref[chans : chans + 8, :] = jnp.broadcast_to(mass[n : n + 1, :], (8, LANES))
    gather_column(size_y - 1, sums_ref, mass, right_ref)
    for c in copies[7:]:
        c.wait()


def gather_column(lane, sums_ref, mass, out_ref):
    chans = out_ref.shape[0] - 8
    shared, _ = row_maps(mass.shape[0])
    wide, lane1 = lanes_of(chans), lanes_of(1)
    col = jnp.zeros((chans, LANES), jnp.float32)
    den = jnp.zeros((1, LANES), jnp.float32)
    for r in range(shared[-1] + 1):
        shift = (r - lane) % LANES
        here, n = sums_ref[pl.ds(r * chans, chans), :], shared.index(r)
        col = jnp.where(wide == r, pltpu.roll(here, shift, 1) if shift else here, col)
        den = jnp.where(lane1 == r, (pltpu.roll(mass, shift, 1) if shift else mass)[n : n + 1, :], den)
    out_ref[0:chans, :] = col
    out_ref[chans : chans + 8, :] = jnp.broadcast_to(den, (8, LANES))


def cumulative(x):
    rows = x.shape[0]
    sub = lax.broadcasted_iota(jnp.int32, x.shape, 0)
    step = 1
    while step < rows:
        x = x + jnp.where(sub >= step, pltpu.roll(x, step, 0), 0.0)
        step *= 2
    return x


def physics(tracers, temps, day):
    levels = temps.shape[0]
    vapour = tracers[0:levels]
    scaled = absorb_coef * vapour
    heating = heat_gain * scaled * jnp.exp(-cumulative(scaled))
    heated = temps + jnp.where(day == 1.0, heating, 0.0)
    saturation = sat_base * jnp.exp(clausius * (heated - ref_temp))
    remain = jnp.minimum(vapour, saturation)
    log_ratio = jnp.log(remain / vapour)
    inverse = 1.0 / heated
    alpha_heavy = jnp.exp(1137.0 * inverse * inverse - 0.4156 * inverse - 0.0020667)
    alpha_deut = jnp.exp(24844.0 * inverse * inverse - 76.248 * inverse + 0.052612)
    return jnp.concatenate(
        [
            remain,
            tracers[levels : 2 * levels] * jnp.exp(alpha_heavy * log_ratio),
            tracers[2 * levels :] * jnp.exp(alpha_deut * log_ratio),
        ],
        axis=0,
    )


def peer_of(slot, paired):
    return lax.axis_index("blk") ^ slot if paired else slot


def carriers(n_peers):
    return sorted({j ^ ((j - 1) % n_peers) for j in range(n_peers)})


def third(x):
    return lax.shift_right_logical(x * 43691, 17)


def spread_lanes(x):
    rows = x.shape[0]
    lane = lanes_of(rows)
    source = 3 * lax.shift_right_logical(lane, 2) + jnp.minimum(lane & 3, 2)
    padded = jnp.concatenate([x, jnp.zeros((rows, LANES - x.shape[1]), x.dtype)], axis=1)
    return jnp.take_along_axis(padded, source, axis=1)


def send_order_kernel(n_peers, paired, after_ref, order_ref, hot_ref, pick_ref, slots_ref):
    del after_ref
    sites = order_ref.shape[1]
    count = hot_ref.shape[0] // LANES + 1
    per_row = sites // count
    per_peer = sites // n_peers
    full, rest = per_peer // LANES, per_peer % LANES

    order = order_ref[...]
    for p in range(n_peers):
        mine = order[:, p * per_peer : (p + 1) * per_peer]
        pad = slots_ref.shape[1] - per_peer
        slots_ref[p : p + 1, :] = jnp.concatenate([mine, jnp.zeros((1, pad), jnp.int32)], axis=1) if pad else mine
    peers = [slots_ref[pl.ds(peer_of(k, paired), 1), :] for k in range(n_peers)]
    pieces = [mine[:, LANES * j : LANES * (j + 1)] for mine in peers for j in range(full)]
    if rest:
        pieces += [mine[:, LANES * full : per_peer] for mine in peers]
    order = jnp.concatenate(pieces, axis=1)
    row = third(lax.shift_right_logical(order, 5))
    within = order - per_row * row
    group = third(within)
    node = 4 * group + (within - 3 * group)
    main = jnp.where((row == 0) | (node == 0), -1, (row - 1) * LANES + node)
    first = jnp.where(row == 0, node, -1)
    side = jnp.where((row != 0) & (node == 0), row, -1)
    bf16 = jnp.bfloat16
    sub = lax.broadcasted_iota(jnp.int32, (LANES, LANES), 0).astype(bf16)

    def one_hot(index):
        index = jnp.broadcast_to(jnp.clip(index, -1, LANES).astype(jnp.float32), (16, LANES)).astype(bf16)
        index = jnp.concatenate([index] * (LANES // 16), axis=0)
        return jnp.where(sub == index, jnp.ones((), bf16), jnp.zeros((), bf16))

    for t in range(sites // LANES):
        at = slice(t * LANES, (t + 1) * LANES)
        here = main[:, at]
        for k in range(count - 1):
            hot_ref[k * LANES : (k + 1) * LANES, at] = one_hot(here - k * LANES)
        pick_ref[0:LANES, at] = one_hot(first[:, at])
        pick_ref[LANES : 2 * LANES, at] = one_hot(side[:, at])


def spread_columns(temps_ref, day_ref, ntemps_ref, nday_ref):
    levels, sites = temps_ref.shape
    count = ntemps_ref.shape[0] // levels - 1
    per_row = sites // count
    temps = temps_ref[...]
    day = jnp.broadcast_to(day_ref[...].astype(jnp.float32), (8, sites))
    lane1, wide_l = lanes_of(1), lanes_of(levels)
    unused = (lane1 & 3) == 3
    side_temps = jnp.full((levels, LANES), ref_temp, jnp.float32)
    side_day = jnp.zeros((8, LANES), jnp.float32)
    for k in range(count):
        t_here = jnp.where(unused, ref_temp, spread_lanes(temps[:, k * per_row : (k + 1) * per_row]))
        d_here = spread_lanes(day[:, k * per_row : (k + 1) * per_row])
        ntemps_ref[k * levels : (k + 1) * levels, :] = t_here
        nday_ref[8 * k : 8 * k + 8, :] = d_here
        if k:
            side_temps = jnp.where(wide_l == k, pltpu.roll(t_here, k, 1), side_temps)
            side_day = jnp.where(lanes_of(8) == k, pltpu.roll(d_here, k, 1), side_day)
    ntemps_ref[count * levels :, :] = side_temps
    nday_ref[8 * count :, :] = side_day


def inner_columns_kernel(iso_ref, sums_ref, den_ref, temps_ref, day_ref, hot_ref, acc_ref, hiso_ref, left_ref, ntemps_ref, nday_ref, lhs_ref):
    spread_columns(temps_ref, day_ref, ntemps_ref, nday_ref)
    size_x, size_y = den_ref.shape
    chans = acc_ref.shape[0]
    levels = chans // 3
    _, node_rows = row_maps(size_x)
    lane1 = lanes_of(1)
    own = ((lane1 & 3) == 3) | (lane1 == 0)
    wide = lanes_of(chans)
    hiso = jnp.full((chans, LANES), 3.0, jnp.float32)
    inv = 1.0 / den_ref[...]
    for k, n in enumerate(node_rows):
        if k == 0:
            continue
        iso = iso_ref[pl.ds(n, chans, stride=size_x + PAD_ROWS), :]
        hiso = jnp.where(wide == k, pltpu.roll(iso, k, 1), hiso)
        gain = jnp.where(own, 0.0, time_step * inv[n : n + 1, :])
        tracers = iso + gain * sums_ref[pl.ds(k * chans, chans), :]
        hi, lo = split(physics(tracers, ntemps_ref[k * levels : (k + 1) * levels, :], nday_ref[8 * k : 8 * k + 1, :]))
        lhs_ref[0:chans, (k - 1) * LANES : k * LANES] = hi
        lhs_ref[chans : 2 * chans, (k - 1) * LANES : k * LANES] = lo
    hiso_ref[...] = hiso
    gather_column(0, sums_ref, den_ref[...], left_ref)
    both = dot(lhs_ref[...], hot_ref[...])
    acc_ref[...] = both[0:chans] + both[chans:]


def edge_columns_kernel(
    n_peers, paired, iso_ref, sums_ref, den_ref, left_ref, acc_ref, pick_ref, ntemps_ref, nday_ref, hiso_ref, corner_ref, before_ref, low_ref, high_ref, *send_refs
):
    chans, sites = acc_ref.shape
    levels = chans // 3
    size_x = den_ref.shape[0]
    _, node_rows = row_maps(size_x)
    count = len(node_rows)
    per_peer = sites // n_peers
    full, rest = per_peer // LANES, per_peer % LANES
    wide, lane1 = lanes_of(chans), lanes_of(1)
    unused = (lane1 & 3) == 3

    last = row_maps(size_x)[0][-1]
    extra = before_ref[...] + pltpu.roll(corner_ref[...], LANES - last, 1)
    total = sums_ref[0:chans, :] + low_ref[0:chans, :] + jnp.where(wide == 0, extra[0:chans, :], 0.0)
    den = den_ref[0:1, :] + low_ref[chans : chans + 1, :] + jnp.where(lane1 == 0, extra[chans : chans + 1, :], 0.0)
    iso = iso_ref[pl.ds(0, chans, stride=size_x + PAD_ROWS), :]
    new_row = iso + jnp.where(unused, 0.0, time_step / den) * total
    phys_row = physics(new_row, ntemps_ref[0:levels, :], nday_ref[0:1, :])

    in_use = (lane1 > 0) & (lane1 < count)
    dcol = jnp.where(in_use, left_ref[chans : chans + 1, :] + before_ref[chans : chans + 1, :], 1.0)
    tcol = jnp.where(in_use, left_ref[0:chans, :] + before_ref[0:chans, :], 0.0)
    new_col = hiso_ref[...] + (time_step / dcol) * tcol
    phys_col = physics(new_col, ntemps_ref[count * levels :, :], nday_ref[8 * count : 8 * count + 1, :])

    rhi, rlo = split(phys_row)
    chi, clo = split(phys_col)
    lhs = jnp.concatenate([jnp.concatenate([rhi, chi], axis=1), jnp.concatenate([rlo, clo], axis=1)], axis=0)
    both = dot(lhs, pick_ref[...])
    out = acc_ref[...] + (both[0:chans] + both[chans:])
    for p in range(n_peers):
        for j in range(full):
            t = p * full + j
            send_refs[p][0, j * chans : (j + 1) * chans, :] = out[:, t * LANES : (t + 1) * LANES]
    if rest:
        begin = n_peers * full * LANES
        for t in range(n_peers * rest // LANES):
            block = out[:, begin + t * LANES : begin + (t + 1) * LANES]
            block = jnp.concatenate([block, jnp.zeros((LANES - chans, LANES), jnp.float32)], axis=0).T
            at = t * LANES
            while at < (t + 1) * LANES:
                p, i = at // rest, at % rest
                count = min(rest - i, (t + 1) * LANES - at)
                send_refs[p][0, full * chans + i : full * chans + i + count, :] = block[at - t * LANES : at - t * LANES + count, :]
                at += count


    lane, high = lanes_of(chans + 8), high_ref[...]
    edge = left_ref[...] + jnp.where(lane == 0, low_ref[...], 0.0) + jnp.where(lane == last, pltpu.roll(high, last, 1), 0.0)
    edge = jnp.where(lane == last + 1, pltpu.roll(high, last + 2, 1), edge)
    if not paired:
        send_refs[n_peers][...] = edge
    else:
        turned = jnp.concatenate([edge, jnp.zeros((LANES - edge.shape[0], LANES), jnp.float32)], axis=0).T
        for k in carriers(n_peers):
            rows = send_refs[k].shape[1] - send_refs[0].shape[1]
            send_refs[k][0, send_refs[0].shape[1] :, :] = turned[0:rows, :]


def advance_kernel(n_peers, paired, carried, iso_ref, sums_ref, den_ref, corner_ref, near_ref, low_ref, high_ref, *rest):
    *edge_refs, new_hbm, before_ref, after_ref, new_ref, sems = rest
    size_x = den_ref.shape[0]
    chans = low_ref.shape[0] - 8
    shared, _ = row_maps(size_x)
    last = shared[-1]
    lane1 = lanes_of(1)
    if paired:
        me = lax.axis_index("blk")
        turned = []
        for other in (lax.rem(me + 1, n_peers), lax.rem(me + n_peers - 1, n_peers)):
            mine = jnp.zeros((carried, LANES), jnp.float32)
            for k, ref in zip(carriers(n_peers), edge_refs):
                mine = jnp.where((me ^ other) == k, ref[0, ref.shape[1] - carried :, :], mine)
            turned.append(mine)
        pad = jnp.zeros((LANES - 2 * carried, LANES), jnp.float32)
        both = jnp.concatenate(turned + [pad], axis=0).T[0 : chans + 8, :]
        after_ref[...] = both
        beside = pltpu.roll(both, LANES - carried - 1, 1)
    else:
        after_ref[...] = edge_refs[0][...]
        beside = pltpu.roll(edge_refs[1][...], LANES - 1, 1)
    lane = lanes_of(chans + 8)
    near = near_ref[...] + jnp.where(lane == 0, pltpu.roll(corner_ref[...], LANES - last, 1), 0.0)
    before_ref[...] = near + jnp.where(lane == last, beside, 0.0)
    gains = []
    for n in range(size_x):
        den = den_ref[n : n + 1, :]
        for ref, at in ((low_ref, 0), (high_ref, size_x - 1)):
            if n == at:
                den = den + ref[chans : chans + 1, :]
        for ref, at in ((before_ref, 0), (after_ref, LANES - 1)):
            den = jnp.where(lane1 == at, den + ref[chans : chans + 1, shared[n] : shared[n] + 1], den)
        gains.append(time_step / den)
    levels = chans // 3
    wide = lanes_of(levels)
    copies = []
    for s in range(3):
        for n in range(size_x):
            r = shared[n]
            total = sums_ref[pl.ds(r * chans + s * levels, levels), :]
            at_s = pl.ds(s * levels, levels)
            for ref, at in ((low_ref, 0), (high_ref, size_x - 1)):
                if n == at:
                    total = total + ref[at_s, :]
            for ref, at in ((before_ref, 0), (after_ref, LANES - 1)):
                total = jnp.where(wide == at, total + ref[at_s, r : r + 1], total)
            here = pl.ds(s * levels * (size_x + PAD_ROWS) + n, levels, stride=size_x + PAD_ROWS)
            new_ref[here, :] = iso_ref[here, :] + gains[n] * total
        made, out = (ref.reshape(3, levels, -1, LANES) for ref in (new_ref, new_hbm))
        copies.append(pltpu.make_async_copy(made.at[s, :, pl.ds(0, size_x)], out.at[s], sems.at[s]))
        copies[-1].start()
    for c in copies:
        c.wait()


def assemble_kernel(n_peers, paired, *refs):
    if paired:
        *slot_refs, out_hbm, got_ref, out_ref, sems = refs
        for k, ref in enumerate(slot_refs):
            got_ref[pl.ds(peer_of(k, paired), 1), :, :] = ref[:, 0 : got_ref.shape[1], :]
    else:
        got_ref, out_hbm, out_ref, sems = refs
    chans, sites = out_ref.shape
    per_peer = sites // n_peers
    full, rest = per_peer // LANES, per_peer % LANES
    lane = lanes_of(chans)
    blocks = [None] * (sites // LANES)

    def place(block, value, low, high):
        old = blocks[block]
        blocks[block] = value if old is None else jnp.where((lane >= low) & (lane < high), value, old)

    for p in range(n_peers):
        for j in range(full):
            begin = p * per_peer + j * LANES
            shift = begin % LANES
            value = got_ref[p, j * chans : (j + 1) * chans, :]
            if shift:
                value = pltpu.roll(value, shift, 1)
            place(begin // LANES, value, shift, LANES)
            if shift:
                place(begin // LANES + 1, value, 0, shift)
    if rest:
        tails = [got_ref[p, full * chans : full * chans + rest, :] for p in range(n_peers)]
        tails = jnp.concatenate(tails, axis=0)
        for t in range(n_peers * rest // LANES):
            block = tails[t * LANES : (t + 1) * LANES, :].T[0:chans, :]
            at = t * LANES
            while at < (t + 1) * LANES:
                p, i = at // rest, at % rest
                count = min(rest - i, (t + 1) * LANES - at)
                column = p * per_peer + full * LANES + i
                place(column // LANES, block, column % LANES, column % LANES + count)
                at += count
    copies = []
    for t, block in enumerate(blocks):
        at = pl.ds(t * LANES, LANES)
        out_ref[:, at] = block
        copies.append(pltpu.make_async_copy(out_ref.at[:, at], out_hbm.at[:, at], sems.at[t]))
        copies[-1].start()
    for c in copies:
        c.wait()


def exchange(slots, edge, paired):
    n_peers = lax.axis_size("blk")
    if not paired:
        got = lax.all_to_all(jnp.concatenate(slots, axis=0), "blk", split_axis=0, concat_axis=0, tiled=True)
        up = [(j, (j + 1) % n_peers) for j in range(n_peers)]
        return [got], [lax.ppermute(edge[0], "blk", [(j, i) for i, j in up]), lax.ppermute(edge[0], "blk", up)]
    got = {0: slots[0]}
    for k in SENT:
        block = slots[k]
        for w in AFTER.get(k, ()):
            block, got[w] = lax.optimization_barrier((block, got[w]))
        got[k] = lax.ppermute(block, "blk", [(j, j ^ k) for j in range(n_peers)])
    got = [got[k] for k in range(n_peers)]
    return got, [got[k] for k in carriers(n_peers)]


def call(kernel, outs, scratch, name, *args, **more):
    return pl.pallas_call(
        kernel,
        out_shape=outs,
        **more,
        scratch_shapes=scratch,
        name=name,
        compiler_params=pltpu.CompilerParams(vmem_limit_bytes=40 * 1024 * 1024),
    )(*args)


def on_device(
    isotope_ratios,
    advecting_velocity,
    metric_scaling,
    thermal_state,
    outgoing_site_order,
    daytime_indicator,
):
    size_x, size_y = metric_scaling.shape
    levels = isotope_ratios.shape[1]
    chans = 3 * levels
    sites = outgoing_site_order.shape[1]
    n_face, n_blk = lax.axis_size("face"), lax.axis_size("blk")
    shared, node_rows = row_maps(size_x)
    n_rows = shared[-1] + 1
    per_peer = sites // n_blk
    paired = n_blk == 8
    carried = -(-(n_rows + 1) // 8) * 8
    send_rows = chans * (per_peer // LANES) + per_peer % LANES

    def f32(*shape):
        return jax.ShapeDtypeStruct(shape, jnp.float32)

    iso = isotope_ratios.reshape(chans * size_x, size_y)
    wind = advecting_velocity.reshape(2 * levels * size_x, size_y)
    matrix = jnp.asarray(second_dim_matrix(size_y))
    edge = f32(chans + 8, LANES)
    integers = jax.ShapeDtypeStruct((1, sites), jnp.int32)
    bf16 = jnp.bfloat16
    args = (iso, wind, metric_scaling, matrix, thermal_state[0], daytime_indicator, outgoing_site_order)
    iso, temps, day, order, sums, den, low, high, right = call(
        transport_kernel,
        (
            f32(chans * (size_x + PAD_ROWS), size_y),
            f32(levels, sites),
            integers,
            integers,
            f32(n_rows * chans, size_y),
            f32(size_x, size_y),
            *[edge] * 3,
        ),
        [
            pltpu.VMEM((2 * levels * (size_x + PAD_ROWS), size_y), jnp.float32),
            pltpu.VMEM((size_x, size_y), jnp.float32),
            pltpu.VMEM(matrix.shape, bf16),
            pltpu.VMEM((2 * levels * size_x, size_y), jnp.float32),
        ]
        + [pltpu.VMEM((n_rows * chans, 2 * size_y), bf16)] * 2 + [pltpu.SemaphoreType.DMA((10,))],
        "transport",
        *(pltpu.with_memory_space_constraint(x, pltpu.HBM) for x in args),
        in_specs=[pl.BlockSpec(memory_space=pltpu.HBM)] * len(args),
    )
    face_up = [(i, (i + 1) % n_face) for i in range(n_face)]
    blk_up = [(i, (i + 1) % n_blk) for i in range(n_blk)]
    corner = lax.ppermute(
        right, ("face", "blk"), [(i * n_blk + j, i_up * n_blk + j_up) for i, i_up in face_up for j, j_up in blk_up]
    )
    before = lax.ppermute(right, "blk", blk_up)
    from_low = lax.ppermute(high, "face", face_up)
    from_high = lax.ppermute(low, "face", [(j, i) for i, j in face_up])
    count = len(node_rows)
    hot, pick = call(
        lambda *refs: send_order_kernel(n_blk, paired, *refs),
        (jax.ShapeDtypeStruct(((count - 1) * LANES, sites), bf16), jax.ShapeDtypeStruct((2 * LANES, sites), bf16)),
        [pltpu.VMEM((n_blk, -(-per_peer // LANES) * LANES), jnp.int32)],
        "send_order",
        den,
        order,
    )
    acc, hiso, left, ntemps, nday = call(
        inner_columns_kernel,
        (f32(chans, sites), f32(chans, LANES), edge, f32((count + 1) * levels, LANES), f32((count + 1) * 8, LANES)),
        [pltpu.VMEM((2 * chans, (count - 1) * LANES), bf16)],
        "inner_columns",
        iso,
        sums,
        den,
        temps,
        day,
        hot,
    )
    slots = call(
        lambda *refs: edge_columns_kernel(n_blk, paired, *refs),
        [f32(1, send_rows + (carried if paired and k in carriers(n_blk) else 0), LANES) for k in range(n_blk)] + [edge] * (not paired),
        [],
        "edge_columns",
        iso,
        sums,
        den,
        left,
        acc,
        pick,
        ntemps,
        nday,
        hiso,
        corner,
        before,
        from_low,
        from_high,
    )
    got, edges = exchange(slots[0:n_blk], slots[n_blk:], paired)
    new = call(
        lambda *refs: advance_kernel(n_blk, paired, carried, *refs),
        f32(chans * size_x, size_y),
        [
            pltpu.VMEM((chans + 8, LANES), jnp.float32),
            pltpu.VMEM((chans + 8, LANES), jnp.float32),
            pltpu.VMEM((chans * (size_x + PAD_ROWS), size_y), jnp.float32),
            pltpu.SemaphoreType.DMA((3,)),
        ],
        "advance",
        iso,
        sums,
        den,
        corner,
        before,
        from_low,
        from_high,
        *edges,
        out_specs=pl.BlockSpec(memory_space=pltpu.HBM),
    )
    phys = call(
        lambda *refs: assemble_kernel(n_blk, paired, *refs),
        f32(chans, sites),
        ([pltpu.VMEM((n_blk, send_rows, LANES), jnp.float32)] if paired else [])
        + [pltpu.VMEM((chans, sites), jnp.float32), pltpu.SemaphoreType.DMA((sites // LANES,))],
        "assemble",
        *got,
        out_specs=pl.BlockSpec(memory_space=pltpu.HBM),
    )
    return (new.reshape(isotope_ratios.shape), phys.reshape(1, 3, levels, sites))


def solution(mesh):
    placed = (
        P(None, None, "face", "blk"),
        P(None, None, "face", "blk"),
        P("face", "blk"),
        P("face", None, "blk"),
        P("face", "blk"),
        P("face", "blk"),
    )
    return jax.shard_map(
        on_device,
        mesh=mesh,
        in_specs=placed,
        out_specs=(P(None, None, "face", "blk"), P("face", None, None, "blk")),
        check_vma=False,
    )
```
